256 devices in a mesh: gz: 16 (over z_hi, x), gy: 16 (over z_lo, y, core).
Axes of the slice: x: 4, y: 4, z: 8 (z_hi: 4, z_lo: 2; z = z_hi * 2 + z_lo), core: 2. Of those that a mesh axis runs over, the one named last changes fastest.
Arguments:
- queries: bfloat16 [32, 64, 16, 256], P('gz', 'gy'), may hold values from -2 to 2
- keys: bfloat16 [32, 64, 16, 256], P('gz', 'gy'), may hold values from -2 to 2
- values: bfloat16 [32, 64, 16, 256], P('gz', 'gy'), may hold values from -6 to 6
- cotangent: bfloat16 [32, 64, 16, 256], P('gz', 'gy'), may hold values from -6 to 6
- conv_weight: bfloat16 [27, 256], replicated, may hold values from -0.625 to 0.625
- block_keep: int32 [16, 16, 2], P('gz', 'gy'), may hold values 0 or 1
Outputs:
- grad_query: bfloat16 [32, 64, 16, 256], P('gz', 'gy')
- grad_key: bfloat16 [32, 64, 16, 256], P('gz', 'gy')
- grad_value: bfloat16 [32, 64, 16, 256], P('gz', 'gy')
- conv_grad: float32 [27, 256], replicated
The draws below stay inside these ranges and needn't reach their ends.
Inputs may be any that keep to these rules, and one draw needn't show every extreme that they name: `block_keep`: 1 keeps a block, 0 leaves its tokens out as queries and keys.
All inputs are finite; a program needn't handle non-finite values.
Results may differ from the reference program's by a relative error of at most 0.0051.
Values may be sent and summed in bfloat16 or wider, within the bound.
A program may use at most 64 MiB of HBM per device.

```python
import jax
import jax.numpy as jnp
from jax import lax

HEADS = 8
HEAD = 32
C = 256
BZ = 2
BY = 4
BX = 8
X = 16
NZ = 32
NY = 64
TOKENS = 32768


def touch_ends(result, own_key, least, top_value):
    shape = result.shape
    place = [jax.random.randint(jax.random.fold_in(own_key, axis), (), 0, shape[axis]) for axis in range(len(shape))]
    result = result.at[tuple(place)].set(least)
    longest = shape.index(max(shape))
    place[longest] = (place[longest] + 1) % shape[longest]
    return result.at[tuple(place)].set(top_value)


def block_scale(rng, extent, split, low, high):
    def one(position, parts):
        heights = jax.random.uniform(jax.random.fold_in(jax.random.fold_in(rng, 6), position), (parts,), jnp.float32, low / len(split), high / len(split))
        return jnp.repeat(jnp.exp(heights), extent[position] // parts).reshape((-1,) + (1,) * (len(extent) - position - 1))

    factor_of = one(*split[0])
    for cut in split[1:]:
        factor_of = factor_of * one(*cut)
    return factor_of


def scatter_about(rng, dims, spread, most, cuts=(), kind=jnp.bfloat16):
    drawn = jax.random.normal(rng, dims, jnp.float32) * spread
    if len(cuts) > 0:
        drawn = block_scale(rng, dims, cuts, -0.22, 0.18) * drawn
    return jnp.clip(drawn, min=-most, max=most).astype(kind)


def setup_inputs(seed: int = 0) -> dict:
    splits = jax.random.split(jax.random.key(seed), 7)
    return {
        "queries": jnp.clip(jax.random.uniform(splits[0], (NZ, NY, X, C), jnp.float32, -2.0, 2.0) * block_scale(splits[0], (NZ, NY, X, C), ((0, 16), (1, 16)), -0.4, 0.0), -2.0, 2.0).astype(jnp.bfloat16),
        "keys": jnp.clip(jax.random.uniform(splits[1], (NZ, NY, X, C), jnp.float32, -2.0, 2.0) * block_scale(splits[1], (NZ, NY, X, C), ((0, 16), (1, 16)), -0.4, 0.0), -2.0, 2.0).astype(jnp.bfloat16),
        "values": scatter_about(splits[2], (NZ, NY, X, C), 1.0, 6.0, ((0, 16), (1, 16))),
        "cotangent": scatter_about(splits[3], (NZ, NY, X, C), 1.0, 6.0, ((0, 16), (1, 16))),
        "conv_weight": scatter_about(splits[4], (27, C), 108 ** -0.5, 0.625),
        "block_keep": touch_ends((jax.random.randint(splits[5], (NZ // BZ, NY // BY, X // BX), 0, 4) < 3).astype(jnp.int32), jax.random.fold_in(splits[5], 1), 0, 1),
    }


def token_mask(block_keep):
    expanded = jnp.repeat(block_keep, BZ, axis=0)
    expanded = jnp.repeat(expanded, BY, axis=1)
    return jnp.repeat(expanded, BX, axis=2)


def reference(queries, keys, values, cotangent, conv_weight, block_keep):
    grid_shape = (NZ, NY, X, C)
    keep_mask = token_mask(block_keep).astype(jnp.float32)
    scaling = HEAD ** -0.5
    pad_spec = ((2, 2), (2, 2), (2, 2), (0, 0))
    key_pad = jnp.pad(keys.astype(jnp.float32), pad_spec)
    value_pad = jnp.pad(values.astype(jnp.float32), pad_spec)
    mask_pad = jnp.pad(keep_mask, 2)
    query_full = queries.astype(jnp.float32)
    grad_full = cotangent.astype(jnp.float32)
    offsets = jnp.array([[step_z, step_y, step_x] for step_z in range(5) for step_y in range(5) for step_x in range(5)], dtype=jnp.int32)
    zero_index = jnp.int32(0)

    def window(source, offset):
        return lax.dynamic_slice(source, (offset[0], offset[1], offset[2], zero_index), grid_shape)

    def window_mask(offset):
        return lax.dynamic_slice(mask_pad, (offset[0], offset[1], offset[2]), (NZ, NY, X))[..., None]

    def per_head(left, right):
        return jnp.sum((left * right).reshape(NZ, NY, X, HEADS, HEAD), axis=-1)

    def expand(weights, source):
        return (weights[..., None] * source.reshape(NZ, NY, X, HEADS, HEAD)).reshape(grid_shape)

    def add_total(totals, offset):
        scores = per_head(query_full, window(key_pad, offset)) * scaling
        return totals + window_mask(offset) * jnp.exp(scores), None

    totals, _ = lax.scan(add_total, jnp.zeros((NZ, NY, X, HEADS), jnp.float32), offsets)
    totals = totals + (1.0 - keep_mask)[..., None]
    factor = keep_mask[..., None] / totals

    def probabilities(offset):
        key_window = window(key_pad, offset)
        scores = per_head(query_full, key_window) * scaling
        probs = window_mask(offset) * jnp.exp(scores) * factor
        rounded = lax.optimization_barrier(probs.astype(jnp.bfloat16)).astype(jnp.float32)
        return key_window, probs, rounded

    def add_output(attended, offset):
        key_window, probs, rounded = probabilities(offset)
        return attended + expand(rounded, window(value_pad, offset)), None

    attended, _ = lax.scan(add_output, jnp.zeros(grid_shape, jnp.float32), offsets)
    deltas = per_head(grad_full, attended)

    def add_grads(carry, offset):
        grad_q, grad_k, grad_v = carry
        key_window, probs, rounded = probabilities(offset)
        dprobs = per_head(grad_full, window(value_pad, offset))
        logit_derivatives = lax.optimization_barrier((scaling * probs * (dprobs - deltas)).astype(jnp.bfloat16)).astype(jnp.float32)
        grad_q = grad_q + expand(logit_derivatives, key_window)
        start = (offset[0], offset[1], offset[2], zero_index)
        grad_k = lax.dynamic_update_slice(grad_k, window(grad_k, offset) + expand(logit_derivatives, query_full), start)
        grad_v = lax.dynamic_update_slice(grad_v, window(grad_v, offset) + expand(rounded, grad_full), start)
        return (grad_q, grad_k, grad_v), None

    padded_shape = (NZ + 4, NY + 4, X + 4, C)
    initial = (jnp.zeros(grid_shape, jnp.float32), jnp.zeros(padded_shape, jnp.float32), jnp.zeros(padded_shape, jnp.float32))
    (grad_q, grad_k, grad_v), _ = lax.scan(add_grads, initial, offsets)
    grad_k = grad_k[2:NZ + 2, 2:NY + 2, 2:X + 2]
    grad_v = grad_v[2:NZ + 2, 2:NY + 2, 2:X + 2]

    neighbour_layout = ((1, 1), (1, 1), (1, 1), (0, 0))
    grad_near = jnp.pad(grad_full, neighbour_layout)
    value_near = jnp.pad(values.astype(jnp.float32), neighbour_layout)
    filter_full = conv_weight.astype(jnp.float32)
    conv_values = jnp.zeros(grid_shape, jnp.float32)
    filter_terms = []
    for shift_z in range(3):
        for shift_y in range(3):
            for shift_x in range(3):
                row_index = shift_z * 9 + shift_y * 3 + shift_x
                conv_values = conv_values + filter_full[row_index] * grad_near[2 - shift_z:2 - shift_z + NZ, 2 - shift_y:2 - shift_y + NY, 2 - shift_x:2 - shift_x + X]
                filter_terms.append(jnp.sum(grad_full * value_near[shift_z:shift_z + NZ, shift_y:shift_y + NY, shift_x:shift_x + X], axis=(0, 1, 2)))
    conv_grad = jnp.stack(filter_terms) * (TOKENS ** -0.5)
    grad_value = (grad_v + conv_values).astype(jnp.bfloat16)
    return grad_q.astype(jnp.bfloat16), grad_k.astype(jnp.bfloat16), grad_value, conv_grad
```

```python
from functools import partial

import jax
import jax.numpy as jnp
from jax import lax
from jax.experimental import pallas as pl
from jax.experimental.pallas import tpu as pltpu
from jax.sharding import PartitionSpec as P

HEAD = 32
BX = 8
LANES = 128
GROUP_HEADS = LANES // HEAD
DEAD = 4.0
LOG2E = 1.4426950408889634
MESH = pl.DeviceIdType.MESH
F32 = jnp.float32
BF16 = jnp.bfloat16


def rounds_of(sections, rows):
    first = [("gy", rows // 2, 2), ("gy", 1, 2)]
    between = [[("gy", 2, rows // 4)]] if rows > 4 else []
    along = []
    stride = 1
    while stride < sections:
        along.append([("gz", stride, min(4, sections // stride))])
        stride *= 4
    return [first] + between + along


def kernel(
    sections,
    rows_n,
    depth,
    rows,
    cols,
    q_ref,
    k_ref,
    v_ref,
    g_ref,
    w_ref,
    keep_ref,
    gq_ref,
    gk_ref,
    gv_ref,
    cg_ref,
    ext,
    acc,
    qm,
    gm,
    shifted,
    filt,
    eights,
    mask,
    part_y,
    got_y,
    part_z,
    got_z,
    terms,
    halo_send,
    halo_recv,
    py_send,
    py_recv,
    pz_send,
    pz_recv,
    sum_send,
    sum_recv,
):
    groups = ext.shape[0]
    tokens = depth * rows * cols
    place = {"gz": lax.axis_index("gz"), "gy": lax.axis_index("gy")}
    gz, gy = place["gz"], place["gy"]
    has = {
        "zm": gz > 0,
        "zp": gz < sections - 1,
        "ym": gy > 0,
        "yp": gy < rows_n - 1,
    }
    device = {"zm": (gz - 1, gy), "zp": (gz + 1, gy), "ym": (gz, gy - 1), "yp": (gz, gy + 1)}
    sum_rounds = rounds_of(sections, rows_n)

    def digit(spec):
        axis, stride, count = spec
        return (place[axis] // stride) % count

    def member_of(digits):
        m = 0
        for spec in digits:
            m = m * spec[2] + digit(spec)
        return m

    def peer(digits, m):
        out = dict(place)
        for spec in reversed(digits):
            axis, stride, count = spec
            want = m % count
            m = m // count
            out[axis] = out[axis] + (want - digit(spec)) * stride
        return (out["gz"], out["gy"])

    def size_of(digits):
        n = 1
        for spec in digits:
            n *= spec[2]
        return n

    barrier = pltpu.get_barrier_semaphore()
    expected = 0
    for side in ("zm", "zp", "ym", "yp"):

        @pl.when(has[side])
        def _(side=side):
            pl.semaphore_signal(barrier, inc=1, device_id=device[side], device_id_type=MESH)

        expected = expected + has[side].astype(jnp.int32)
    for digits in sum_rounds:
        n = size_of(digits)
        me = member_of(digits)
        for step in range(1, n):
            pl.semaphore_signal(
                barrier, inc=1, device_id=peer(digits, (me + step) % n), device_id_type=MESH
            )
        expected = expected + (n - 1)

    keep_low = keep_ref[0, 0, 0].astype(F32)
    keep_high = keep_ref[0, 0, 1].astype(F32)
    row_x = lax.broadcasted_iota(jnp.int32, (cols, LANES), 0)
    row_keep = jnp.where(row_x < BX, keep_low, keep_high)
    lane = lax.broadcasted_iota(jnp.int32, (1, LANES), 1)
    lane_x = lane % cols
    lane_keep = jnp.where(lane_x < BX, keep_low, keep_high)
    lane_head = lane // HEAD

    for g in range(groups):
        part = slice(g * LANES, (g + 1) * LANES)
        own = k_ref[:, :, :, part].astype(F32)
        ext[g, 0, 2 : 2 + depth, 2 : 2 + rows] = jnp.where(row_keep > 0.5, own, DEAD).astype(BF16)
        ext[g, 1, 2 : 2 + depth, 2 : 2 + rows] = v_ref[:, :, :, part]

    pl.semaphore_wait(barrier, expected)

    inner = pl.ds(2, rows)
    low = pl.ds(2, 2)
    high = pl.ds(rows, 2)
    z_own, z_first, z_last = pl.ds(2, depth), pl.ds(0, 2), pl.ds(2 + depth, 2)
    y_first, y_last = pl.ds(0, 2), pl.ds(2 + rows, 2)

    halo = [
        (("zp",), (z_own, inner), (z_first, inner), ("zm",)),
        (("zm",), (z_own, inner), (z_last, inner), ("zp",)),
        (("yp",), (z_own, high), (z_own, y_first), ("ym",)),
        (("ym",), (z_own, low), (z_own, y_last), ("yp",)),
        (("yp", "zm"), (z_first, high), (z_first, y_first), ("ym", "zm")),
        (("ym", "zm"), (z_first, low), (z_first, y_last), ("yp", "zm")),
        (("yp", "zp"), (z_last, high), (z_last, y_first), ("ym", "zp")),
        (("ym", "zp"), (z_last, low), (z_last, y_last), ("yp", "zp")),
    ]

    def both(names):
        found = has[names[0]]
        for name in names[1:]:
            found = jnp.logical_and(found, has[name])
        return found

    def halo_copy(g, slot):
        to, (sz, sy), (dz, dy), _ = halo[slot]
        return pltpu.make_async_remote_copy(
            src_ref=ext.at[g, :, sz, sy],
            dst_ref=ext.at[g, :, dz, dy],
            send_sem=halo_send.at[g, slot],
            recv_sem=halo_recv.at[g, slot],
            device_id=device[to[0]],
            device_id_type=MESH,
        )

    def halo_start(g, slot):
        @pl.when(both(halo[slot][0]))
        def _():
            halo_copy(g, slot).start()

    def halo_sent(g, slot):
        @pl.when(both(halo[slot][0]))
        def _():
            halo_copy(g, slot).wait_send()

    def halo_got(g, slot):
        @pl.when(both(halo[slot][3]))
        def _():
            halo_copy(g, slot).wait_recv()

    for g in range(groups):
        for slot in range(4):
            halo_start(g, slot)

    for side, where in (
        ("zm", (z_first, slice(None))),
        ("zp", (z_last, slice(None))),
        ("ym", (slice(None), y_first)),
        ("yp", (slice(None), y_last)),
    ):

        @pl.when(jnp.logical_not(has[side]))
        def _(side=side, where=where):
            shape = ext[(slice(None), 0) + where].shape
            ext[(slice(None), 0) + where] = jnp.full(shape, DEAD, BF16)
            ext[(slice(None), 1) + where] = jnp.zeros(shape, BF16)
            got = got_z if side[0] == "z" else got_y
            slot = 0 if side[1] == "m" else 1
            got[:, slot] = jnp.zeros(got[:, slot].shape, BF16)

    for o in range(27):
        filt[o] = jnp.broadcast_to(w_ref[o : o + 1].astype(F32), filt.shape[1:])

    def own_row(y, carry):
        for g in range(groups):
            part = slice(g * LANES, (g + 1) * LANES)
            for z in range(depth):
                q_row = q_ref[z, y, :, part].astype(F32)
                g_row = g_ref[z, y, :, part].astype(F32)
                for h in range(GROUP_HEADS):
                    at = pl.ds((z * GROUP_HEADS + h) * cols, cols)
                    mine = lane_head == h
                    qm[g, y, at] = jnp.where(mine, q_row, 0.0).astype(BF16)
                    gm[g, y, at] = jnp.where(mine, g_row, 0.0).astype(BF16)
                none = jnp.zeros((1, LANES), F32)
                shifted[g, 0, z, y] = jnp.concatenate([g_row[1:], none], axis=0)
                shifted[g, 1, z, y] = g_row
                shifted[g, 2, z, y] = jnp.concatenate([none, g_row[:-1]], axis=0)
        return carry

    lax.fori_loop(0, rows, own_row, 0)
    acc[...] = jnp.zeros(acc.shape, F32)
    eights[27:] = jnp.zeros((5, 8, eights.shape[2]), F32)

    octets = (depth * rows * cols // 8, 8, LANES)
    whole = (depth, rows, cols, LANES)

    def filter_values(i, carry):
        oz, oy = i // 3, i % 3
        for g in range(groups):
            part = slice(g * LANES, (g + 1) * LANES)
            total = acc[g, 1, pl.ds(1 + oz, depth), pl.ds(1 + oy, rows)].reshape(octets)
            for ox in range(3):
                total = total + filt[3 * i + ox, :, part] * shifted[g, ox].reshape(octets)
            acc[g, 1, pl.ds(1 + oz, depth), pl.ds(1 + oy, rows)] = total.reshape(whole)
        return carry

    lax.fori_loop(0, 9, filter_values, 0)

    band = jnp.abs(row_x - lane_x) <= 2
    half = lax.broadcasted_iota(jnp.int32, (cols, LANES), 1) // (GROUP_HEADS * cols)

    def make_mask():
        for z in range(depth + 4):
            reach = band
            for own in range(depth):
                if not own <= z <= own + 4:
                    reach = jnp.logical_and(reach, half != own)
            live = jnp.where(reach, 1.0, 0.0)
            mask[z] = jnp.where(ext[0, 0, z].astype(F32) < 3.0, live, 0.0)

    scaling = HEAD**-0.5
    keys_n = (depth + 4) * 5 * cols
    head_row = lax.broadcasted_iota(jnp.int32, (depth * GROUP_HEADS * cols, LANES), 0)
    head_row = (head_row // cols) % GROUP_HEADS
    own_head = head_row == lax.broadcasted_iota(jnp.int32, head_row.shape, 1) // HEAD

    def attend(g):
        part = slice(g * LANES, (g + 1) * LANES)

        def row(y, carry):
            near = pl.ds(y, 5)
            keys = ext[g, 0, :, near].reshape(keys_n, LANES)
            values = ext[g, 1, :, near].reshape(keys_n, LANES)
            queries, grads = qm[g, y], gm[g, y]
            nt = (((1,), (1,)), ((), ()))
            tn = (((0,), (0,)), ((), ()))
            scores = lax.dot_general(keys, queries, nt, preferred_element_type=F32)
            weights = jnp.exp2(scores * (scaling * LOG2E)) * mask[:, near].reshape(keys_n, LANES)
            totals = jnp.sum(weights, axis=0, keepdims=True) + (1.0 - lane_keep)
            probs = weights * (lane_keep / totals)
            probs_low = probs.astype(BF16)
            dprobs = lax.dot_general(values, grads, nt, preferred_element_type=F32)
            deltas = jnp.sum(probs_low.astype(F32) * dprobs, axis=0, keepdims=True)
            dscores = (scaling * probs * (dprobs - deltas)).astype(BF16)
            shape = (depth + 4, 5, cols, LANES)
            acc[g, 1, :, near] += jnp.dot(
                probs_low, grads, preferred_element_type=F32
            ).reshape(shape)
            acc[g, 0, :, near] += jnp.dot(
                dscores, queries, preferred_element_type=F32
            ).reshape(shape)
            dq = lax.dot_general(dscores, keys, tn, preferred_element_type=F32)
            dq = jnp.where(own_head, dq, 0.0).reshape(depth, GROUP_HEADS, cols, LANES)
            gq_ref[:, pl.ds(y, 1), :, part] = jnp.sum(dq, axis=1)[:, None].astype(BF16)
            return carry

        return row

    def part_copy(g, stage, slot):
        if stage == "y":
            src, dst, sends, recvs = part_y, got_y, py_send, py_recv
        else:
            src, dst, sends, recvs = part_z, got_z, pz_send, pz_recv
        to = stage + ("p" if slot == 0 else "m")
        return to, stage + ("m" if slot == 0 else "p"), pltpu.make_async_remote_copy(
            src_ref=src.at[g, slot],
            dst_ref=dst.at[g, slot],
            send_sem=sends.at[g, slot],
            recv_sem=recvs.at[g, slot],
            device_id=device[to],
            device_id_type=MESH,
        )

    def part_start(g, stage):
        for slot in range(2):
            to, _, copy = part_copy(g, stage, slot)

            @pl.when(has[to])
            def _(copy=copy):
                copy.start()

    def part_got(g, stage):
        for slot in range(2):
            _, source, copy = part_copy(g, stage, slot)

            @pl.when(has[source])
            def _(copy=copy):
                copy.wait_recv()

    def part_sent(g, stage):
        for slot in range(2):
            to, _, copy = part_copy(g, stage, slot)

            @pl.when(has[to])
            def _(copy=copy):
                copy.wait_send()

    def send_rows(g):
        part_y[g, 0] = acc[g, :, :, 2 + rows : 4 + rows].astype(BF16)
        part_y[g, 1] = acc[g, :, :, 0:2].astype(BF16)
        part_start(g, "y")

    def send_sections(g):
        part_got(g, "y")
        acc[g, :, :, 2:4] += got_y[g, 0].astype(F32)
        acc[g, :, :, rows : rows + 2] += got_y[g, 1].astype(F32)
        part_z[g, 0] = acc[g, :, 2 + depth : 4 + depth, 2 : 2 + rows].astype(BF16)
        part_z[g, 1] = acc[g, :, 0:2, 2 : 2 + rows].astype(BF16)
        part_start(g, "z")

    def finish(g):
        part = slice(g * LANES, (g + 1) * LANES)
        part_got(g, "z")
        for kind, out in ((0, gk_ref), (1, gv_ref)):
            total = acc[g, kind, 2 : 2 + depth, 2 : 2 + rows]
            total = total + got_z[g, 0, kind].astype(F32) + got_z[g, 1, kind].astype(F32)
            out[:, :, :, part] = total.astype(BF16)

    def filter_terms(g):
        part = slice(g * LANES, (g + 1) * LANES)

        def one(i, carry):
            oz, oy = i // 3, i % 3
            near = ext[g, 1, pl.ds(1 + oz, depth), pl.ds(1 + oy, rows)].astype(F32)
            for ox in range(3):
                product = (near * shifted[g, ox]).reshape(octets)
                eights[3 * i + ox, :, part] = jnp.sum(product, axis=0)
            return carry

        lax.fori_loop(0, 9, one, 0)

    def sum_copy(r, m, step):
        n = size_of(sum_rounds[r])
        return pltpu.make_async_remote_copy(
            src_ref=terms.at[r, m],
            dst_ref=terms.at[r, m],
            send_sem=sum_send.at[r, step],
            recv_sem=sum_recv.at[r, m],
            device_id=peer(sum_rounds[r], (member_of(sum_rounds[r]) + step) % n),
            device_id_type=MESH,
        )

    def sum_begin():
        me = member_of(sum_rounds[0])
        terms[0, me] = jnp.sum(eights[...], axis=1)
        sum_start(0)

    def sum_start(r):
        me = member_of(sum_rounds[r])
        for step in range(1, size_of(sum_rounds[r])):
            sum_copy(r, me, step).start()

    def sum_got(r):
        n = size_of(sum_rounds[r])
        me = member_of(sum_rounds[r])
        for step in range(1, n):
            sum_copy(r, (me + step) % n, step).wait_recv()
        total = terms[r, 0]
        for m in range(1, n):
            total = total + terms[r, m]
        if r + 1 < len(sum_rounds):
            terms[r + 1, member_of(sum_rounds[r + 1])] = total
            sum_start(r + 1)
        else:
            cg_ref[...] = total[0:27] * ((tokens * sections * rows_n) ** -0.5)

    def relay(g):
        halo_got(g, 0)
        halo_start(g, 4)
        halo_start(g, 5)
        halo_got(g, 1)
        halo_start(g, 6)
        halo_start(g, 7)

    def arrived(g):
        for slot in (2, 3, 4, 5, 6, 7):
            halo_got(g, slot)

    relay(0)
    arrived(0)
    make_mask()
    lax.fori_loop(0, rows // 2, attend(0), 0)
    relay(1)
    lax.fori_loop(rows // 2, rows, attend(0), 0)
    send_rows(0)
    filter_terms(0)
    arrived(1)
    filter_terms(1)
    sum_begin()
    lax.fori_loop(0, rows // 2, attend(1), 0)
    send_sections(0)
    sum_got(0)
    lax.fori_loop(rows // 2, rows, attend(1), 0)
    send_rows(1)
    sum_got(1)
    finish(0)
    send_sections(1)
    for r in range(2, len(sum_rounds)):
        sum_got(r)
    finish(1)
    for g in range(groups):
        for slot in range(8):
            halo_sent(g, slot)
        part_sent(g, "y")
        part_sent(g, "z")
    for r in range(len(sum_rounds)):
        for step in range(1, size_of(sum_rounds[r])):
            sum_copy(r, member_of(sum_rounds[r]), step).wait_send()


def shards(sections, rows_n, queries, keys, values, cotangent, conv_weight, block_keep):
    depth, rows, cols, channels = queries.shape
    groups = channels // LANES
    heads_rows = depth * GROUP_HEADS * cols
    sum_rounds = len(rounds_of(sections, rows_n))
    big = jax.ShapeDtypeStruct(queries.shape, BF16)
    vmem = pl.BlockSpec(memory_space=pltpu.VMEM)
    dma = pltpu.SemaphoreType.DMA
    return pl.pallas_call(
        partial(kernel, sections, rows_n, depth, rows, cols),
        out_shape=(big, big, big, jax.ShapeDtypeStruct(conv_weight.shape, F32)),
        in_specs=[vmem] * 5 + [pl.BlockSpec(memory_space=pltpu.SMEM)],
        out_specs=(vmem,) * 4,
        scratch_shapes=[
            pltpu.VMEM((groups, 2, depth + 4, rows + 4, cols, LANES), BF16),
            pltpu.VMEM((groups, 2, depth + 4, rows + 4, cols, LANES), F32),
            pltpu.VMEM((groups, rows, heads_rows, LANES), BF16),
            pltpu.VMEM((groups, rows, heads_rows, LANES), BF16),
            pltpu.VMEM((groups, 3, depth, rows, cols, LANES), F32),
            pltpu.VMEM((27, 8, channels), F32),
            pltpu.VMEM((32, 8, channels), F32),
            pltpu.VMEM((depth + 4, rows + 4, cols, LANES), F32),
            pltpu.VMEM((groups, 2, 2, depth + 4, 2, cols, LANES), BF16),
            pltpu.VMEM((groups, 2, 2, depth + 4, 2, cols, LANES), BF16),
            pltpu.VMEM((groups, 2, 2, 2, rows, cols, LANES), BF16),
            pltpu.VMEM((groups, 2, 2, 2, rows, cols, LANES), BF16),
            pltpu.VMEM((sum_rounds, 4, 32, channels), F32),
            dma((groups, 8)),
            dma((groups, 8)),
            dma((groups, 2)),
            dma((groups, 2)),
            dma((groups, 2)),
            dma((groups, 2)),
            dma((sum_rounds, 4)),
            dma((sum_rounds, 4)),
        ],
        compiler_params=pltpu.CompilerParams(
            collective_id=0, has_side_effects=True, vmem_limit_bytes=32 * 1024 * 1024
        ),
    )(queries, keys, values, cotangent, conv_weight, block_keep)


def solution(mesh):
    in_specs = (
        P("gz", "gy", None, None),
        P("gz", "gy", None, None),
        P("gz", "gy", None, None),
        P("gz", "gy", None, None),
        P(),
        P("gz", "gy", None),
    )
    out_specs = (
        P("gz", "gy", None, None),
        P("gz", "gy", None, None),
        P("gz", "gy", None, None),
        P(),
    )
    return jax.shard_map(
        partial(shards, mesh.shape["gz"], mesh.shape["gy"]),
        mesh=mesh,
        in_specs=in_specs,
        out_specs=out_specs,
        check_vma=False,
    )
```

```python
from functools import partial

import jax
import jax.numpy as jnp
from jax import lax
from jax.experimental import pallas as pl
from jax.experimental.pallas import tpu as pltpu
from jax.sharding import PartitionSpec as P

HEAD = 32
BX = 8
LANES = 128
GROUP_HEADS = LANES // HEAD
DEAD = 4.0
LOG2E = 1.4426950408889634
MESH = pl.DeviceIdType.MESH
F32 = jnp.float32
BF16 = jnp.bfloat16
SIDES = ("zm", "zp", "ym", "yp")
CORNERS = (("zm", "ym"), ("zm", "yp"), ("zp", "ym"), ("zp", "yp"))


def rounds_of(sections, rows):
    if sections == 16 and rows == 16:
        return [[("gz", 4, 4), ("gy", 8, 2)], [("gz", 1, 4), ("gy", 2, 4)]]
    return [[("gz", 1, sections)], [("gy", 2, rows // 2)]]


def kernel(
    sections,
    rows_n,
    depth,
    rows,
    cols,
    q_hbm,
    k_hbm,
    v_hbm,
    g_hbm,
    w_hbm,
    keep_hbm,
    gq_ref,
    gk_ref,
    gv_ref,
    cg_ref,
    q_ref,
    g_ref,
    w_ref,
    keep_ref,
    ext_k,
    ext_v,
    near_v,
    acc,
    qm,
    gm,
    shifted,
    filt,
    eights,
    mask,
    part_y,
    got_y,
    part_z,
    got_z,
    halves,
    terms,
    load_sem,
    halo_send,
    halo_recv,
    near_send,
    near_recv,
    py_send,
    py_recv,
    pz_send,
    pz_recv,
    half_send,
    half_recv,
    sum_send,
    sum_recv,
):
    groups = acc.shape[0]
    tokens = depth * rows * cols
    place = {"gz": lax.axis_index("gz"), "gy": lax.axis_index("gy")}
    gz, gy = place["gz"], place["gy"]
    has = {
        "zm": gz > 0,
        "zp": gz < sections - 1,
        "ym": gy > 0,
        "yp": gy < rows_n - 1,
    }
    shift = {"zm": -1, "zp": 1, "ym": -1, "yp": 1}
    core = lax.rem(gy, 2)
    partner = (gz, gy + 1 - 2 * core)
    sum_rounds = rounds_of(sections, rows_n)

    def both(names):
        found = has[names[0]]
        for name in names[1:]:
            found = jnp.logical_and(found, has[name])
        return found

    def device(names):
        to = dict(place)
        for name in names:
            axis = "g" + name[0]
            to[axis] = to[axis] + shift[name]
        return (to["gz"], to["gy"])

    def digit(spec):
        axis, stride, count = spec
        return lax.rem(lax.div(place[axis], stride), count)

    def member_of(digits):
        m = 0
        for spec in digits:
            m = m * spec[2] + digit(spec)
        return m

    def peer(digits, m):
        out = dict(place)
        for spec in reversed(digits):
            axis, stride, count = spec
            want = lax.rem(m, count)
            m = lax.div(m, count)
            out[axis] = out[axis] + (want - digit(spec)) * stride
        return (out["gz"], out["gy"])

    def size_of(digits):
        n = 1
        for spec in digits:
            n *= spec[2]
        return n

    def load(source, target, sem):
        return pltpu.make_async_copy(source, target, load_sem.at[sem])

    z_own, z_first, z_last = pl.ds(2, depth), pl.ds(0, 2), pl.ds(2 + depth, 2)
    inner, low, high = pl.ds(2, rows), pl.ds(2, 2), pl.ds(rows, 2)
    y_first, y_last = pl.ds(0, 2), pl.ds(2 + rows, 2)
    parts = [slice(g * LANES, (g + 1) * LANES) for g in range(groups)]
    loads = [load(keep_hbm, keep_ref, 0)]
    loads += [load(v_hbm.at[:, :, :, parts[g]], ext_v.at[g, z_own, inner], 1 + g) for g in range(groups)]
    loads += [load(k_hbm.at[:, :, :, parts[g]], ext_k.at[g, z_own, inner], 3 + g) for g in range(groups)]
    loads += [load(g_hbm, g_ref, 5), load(q_hbm, q_ref, 6), load(w_hbm, w_ref, 7)]
    for copy in loads:
        copy.start()

    barrier = pltpu.get_barrier_semaphore()
    expected = 0
    for names in tuple((side,) for side in SIDES) + CORNERS:

        @pl.when(both(names))
        def _(names=names):
            pl.semaphore_signal(barrier, inc=1, device_id=device(names), device_id_type=MESH)

        expected = expected + both(names).astype(jnp.int32)
    pl.semaphore_signal(barrier, inc=1, device_id=partner, device_id_type=MESH)
    expected = expected + 1
    for digits in sum_rounds:
        n = size_of(digits)
        me = member_of(digits)
        for step in range(1, n):
            pl.semaphore_signal(
                barrier, inc=1, device_id=peer(digits, lax.rem(me + step, n)), device_id_type=MESH
            )
        expected = expected + (n - 1)

    loads[0].wait()
    keep_low = keep_ref[0, 0, 0].astype(F32)
    keep_high = keep_ref[0, 0, 1].astype(F32)
    row_x = lax.broadcasted_iota(jnp.int32, (cols, LANES), 0)
    row_keep = jnp.where(row_x < BX, keep_low, keep_high)
    lane = lax.broadcasted_iota(jnp.int32, (1, LANES), 1)
    lane_x = lane % cols
    lane_keep = jnp.where(lane_x < BX, keep_low, keep_high)
    lane_head = lane // HEAD

    for g in range(groups):
        loads[1 + g].wait()
    for g in range(groups):
        loads[3 + g].wait()
        own = ext_k[g, 2 : 2 + depth, 2 : 2 + rows].astype(F32)
        ext_k[g, 2 : 2 + depth, 2 : 2 + rows] = jnp.where(row_keep > 0.5, own, DEAD).astype(BF16)

    pl.semaphore_wait(barrier, expected)

    kinds = [ext_v] + [ext_k.at[g] for g in range(groups)]
    halo = [
        (("zp",), (z_own, inner), (z_first, inner), ("zm",)),
        (("zm",), (z_own, inner), (z_last, inner), ("zp",)),
        (("yp",), (z_own, high), (z_own, y_first), ("ym",)),
        (("ym",), (z_own, low), (z_own, y_last), ("yp",)),
        (("yp", "zm"), (z_first, high), (z_first, y_first), ("ym", "zm")),
        (("ym", "zm"), (z_first, low), (z_first, y_last), ("yp", "zm")),
        (("yp", "zp"), (z_last, high), (z_last, y_first), ("ym", "zp")),
        (("ym", "zp"), (z_last, low), (z_last, y_last), ("yp", "zp")),
    ]

    def halo_copy(kind, slot):
        to, (sz, sy), (dz, dy), _ = halo[slot]
        ref = kinds[kind]
        src, dst = (ref.at[:, sz, sy], ref.at[:, dz, dy]) if kind == 0 else (ref.at[sz, sy], ref.at[dz, dy])
        return pltpu.make_async_remote_copy(
            src_ref=src,
            dst_ref=dst,
            send_sem=halo_send.at[kind, slot],
            recv_sem=halo_recv.at[kind, slot],
            device_id=device(to[:1]),
            device_id_type=MESH,
        )

    def halo_start(kind, slots):
        for slot in slots:

            @pl.when(both(halo[slot][0]))
            def _(slot=slot):
                halo_copy(kind, slot).start()

    def halo_sent(kind, slots):
        for slot in slots:

            @pl.when(both(halo[slot][0]))
            def _(slot=slot):
                halo_copy(kind, slot).wait_send()

    def halo_got(kind, slots):
        for slot in slots:

            @pl.when(both(halo[slot][3]))
            def _(slot=slot):
                halo_copy(kind, slot).wait_recv()

    def near_copy(corner):
        up_z, up_y = CORNERS[corner][0] == "zm", CORNERS[corner][1] == "ym"
        return pltpu.make_async_remote_copy(
            src_ref=ext_v.at[:, 1 + depth if up_z else 2, 1 + rows if up_y else 2],
            dst_ref=near_v.at[:, 0 if up_z else 1 + depth, 0 if up_y else 1 + rows],
            send_sem=near_send.at[corner],
            recv_sem=near_recv.at[corner],
            device_id=device(("zp" if up_z else "zm", "yp" if up_y else "ym")),
            device_id_type=MESH,
        )

    def opposite(corner):
        return tuple(name[0] + ("p" if name[1] == "m" else "m") for name in CORNERS[corner])

    halo_start(0, (0, 1, 2, 3))
    for corner in range(4):

        @pl.when(both(opposite(corner)))
        def _(corner=corner):
            near_copy(corner).start()

    for g in range(groups):
        halo_start(1 + g, (0, 1, 2, 3))

    for side, where in (
        ("zm", (slice(None), z_first)),
        ("zp", (slice(None), z_last)),
        ("ym", (slice(None), slice(None), y_first)),
        ("yp", (slice(None), slice(None), y_last)),
    ):

        @pl.when(jnp.logical_not(has[side]))
        def _(side=side, where=where):
            shape = ext_k[where].shape
            ext_k[where] = jnp.full(shape, DEAD, BF16)
            ext_v[where] = jnp.zeros(shape, BF16)
            got = got_z if side[0] == "z" else got_y
            slot = 0 if side[1] == "m" else 1
            got[:, slot] = jnp.zeros(got[:, slot].shape, BF16)

    for corner in range(4):

        @pl.when(jnp.logical_not(both(CORNERS[corner])))
        def _(corner=corner):
            z = 0 if CORNERS[corner][0] == "zm" else 1 + depth
            y = 0 if CORNERS[corner][1] == "ym" else 1 + rows
            near_v[:, z, y] = jnp.zeros((groups, cols, LANES), BF16)

    for copy in loads[5:]:
        copy.wait()
    for o in range(27):
        filt[o] = jnp.broadcast_to(w_ref[o : o + 1].astype(F32), filt.shape[1:])

    def own_row(y, carry):
        for g in range(groups):
            part = parts[g]
            for z in range(depth):
                q_row = q_ref[z, y, :, part].astype(F32)
                g_row = g_ref[z, y, :, part].astype(F32)
                for h in range(GROUP_HEADS):
                    at = pl.ds((z * GROUP_HEADS + h) * cols, cols)
                    mine = lane_head == h
                    qm[g, y, at] = jnp.where(mine, q_row, 0.0).astype(BF16)
                    gm[g, y, at] = jnp.where(mine, g_row, 0.0).astype(BF16)
                none = jnp.zeros((1, LANES), F32)
                shifted[g, 0, z, y] = jnp.concatenate([g_row[1:], none], axis=0)
                shifted[g, 1, z, y] = g_row
                shifted[g, 2, z, y] = jnp.concatenate([none, g_row[:-1]], axis=0)
        return carry

    lax.fori_loop(0, rows, own_row, 0)
    acc[...] = jnp.zeros(acc.shape, F32)
    eights[27:] = jnp.zeros((5, 8, eights.shape[2]), F32)
    octets = (depth * rows * cols // 8, 8, LANES)
    whole = (depth, rows, cols, LANES)

    def filter_values(i, carry):
        oz, oy = lax.div(i, 3), lax.rem(i, 3)
        for g in range(groups):
            total = acc[g, 1, pl.ds(1 + oz, depth), pl.ds(1 + oy, rows)].reshape(octets)
            for ox in range(3):
                total = total + filt[3 * i + ox, :, parts[g]] * shifted[g, ox].reshape(octets)
            acc[g, 1, pl.ds(1 + oz, depth), pl.ds(1 + oy, rows)] = total.reshape(whole)
        return carry

    band = jnp.abs(row_x - lane_x) <= 2
    half = lax.broadcasted_iota(jnp.int32, (cols, LANES), 1) // (GROUP_HEADS * cols)

    def make_mask():
        for z in range(depth + 4):
            reach = band
            for own in range(depth):
                if not own <= z <= own + 4:
                    reach = jnp.logical_and(reach, half != own)
            live = jnp.where(reach, 1.0, 0.0)
            mask[z] = jnp.where(ext_k[0, z].astype(F32) < 3.0, live, 0.0)

    scaling = HEAD**-0.5
    keys_n = (depth + 4) * 5 * cols
    head_row = lax.broadcasted_iota(jnp.int32, (depth * GROUP_HEADS * cols, LANES), 0)
    head_row = (head_row // cols) % GROUP_HEADS
    own_head = head_row == lax.broadcasted_iota(jnp.int32, head_row.shape, 1) // HEAD

    def attend(g):
        def row(y, carry):
            near = pl.ds(y, 5)
            keys = ext_k[g, :, near].reshape(keys_n, LANES)
            values = ext_v[g, :, near].reshape(keys_n, LANES)
            queries, grads = qm[g, y], gm[g, y]
            nt = (((1,), (1,)), ((), ()))
            tn = (((0,), (0,)), ((), ()))
            scores = lax.dot_general(keys, queries, nt, preferred_element_type=F32)
            weights = jnp.exp2(scores * (scaling * LOG2E)) * mask[:, near].reshape(keys_n, LANES)
            totals = jnp.sum(weights, axis=0, keepdims=True) + (1.0 - lane_keep)
            probs = weights * (lane_keep / totals)
            probs_low = probs.astype(BF16)
            dprobs = lax.dot_general(values, grads, nt, preferred_element_type=F32)
            deltas = jnp.sum(probs_low.astype(F32) * dprobs, axis=0, keepdims=True)
            dscores = (scaling * probs * (dprobs - deltas)).astype(BF16)
            shape = (depth + 4, 5, cols, LANES)
            acc[g, 1, :, near] += jnp.dot(
                probs_low, grads, preferred_element_type=F32
            ).reshape(shape)
            acc[g, 0, :, near] += jnp.dot(
                dscores, queries, preferred_element_type=F32
            ).reshape(shape)
            dq = lax.dot_general(dscores, keys, tn, preferred_element_type=F32)
            dq = jnp.where(own_head, dq, 0.0).reshape(depth, GROUP_HEADS, cols, LANES)
            gq_ref[:, pl.ds(y, 1), :, parts[g]] = jnp.sum(dq, axis=1)[:, None].astype(BF16)
            return carry

        return row

    def part_copy(g, stage, slot):
        if stage == "y":
            src, dst, sends, recvs = part_y, got_y, py_send, py_recv
        else:
            src, dst, sends, recvs = part_z, got_z, pz_send, pz_recv
        to = stage + ("p" if slot == 0 else "m")
        source = stage + ("m" if slot == 0 else "p")
        copy = pltpu.make_async_remote_copy(
            src_ref=src.at[g, slot],
            dst_ref=dst.at[g, slot],
            send_sem=sends.at[g, slot],
            recv_sem=recvs.at[g, slot],
            device_id=device((to,)),
            device_id_type=MESH,
        )
        return to, source, copy

    def part_start(g, stage, slot):
        to, _, copy = part_copy(g, stage, slot)

        @pl.when(has[to])
        def _():
            copy.start()

    def part_got(g, stage, slot):
        _, source, copy = part_copy(g, stage, slot)

        @pl.when(has[source])
        def _():
            copy.wait_recv()

    def part_sent(g, stage, slot):
        to, _, copy = part_copy(g, stage, slot)

        @pl.when(has[to])
        def _():
            copy.wait_send()

    def send_rows(g, slot):
        at = 2 + rows if slot == 0 else 0
        part_y[g, slot] = acc[g, :, :, at : at + 2].astype(BF16)
        part_start(g, "y", slot)

    def send_sections(g):
        part_got(g, "y", 0)
        part_got(g, "y", 1)
        acc[g, :, :, 2:4] += got_y[g, 0].astype(F32)
        acc[g, :, :, rows : rows + 2] += got_y[g, 1].astype(F32)
        for slot in range(2):
            at = 2 + depth if slot == 0 else 0
            part_z[g, slot] = acc[g, :, at : at + 2, 2 : 2 + rows].astype(BF16)
            part_start(g, "z", slot)

    def finish(g):
        part_got(g, "z", 0)
        part_got(g, "z", 1)
        for kind, out in ((0, gk_ref), (1, gv_ref)):
            total = acc[g, kind, 2 : 2 + depth, 2 : 2 + rows]
            total = total + got_z[g, 0, kind].astype(F32) + got_z[g, 1, kind].astype(F32)
            out[:, :, :, parts[g]] = total.astype(BF16)

    def filter_terms():
        near_v[:, 1 : 1 + depth, 1 : 1 + rows] = ext_v[:, 2 : 2 + depth, 2 : 2 + rows]
        near_v[:, 0, 1 : 1 + rows] = ext_v[:, 1, 2 : 2 + rows]
        near_v[:, 1 + depth, 1 : 1 + rows] = ext_v[:, 2 + depth, 2 : 2 + rows]
        near_v[:, 1 : 1 + depth, 0] = ext_v[:, 2 : 2 + depth, 1]
        near_v[:, 1 : 1 + depth, 1 + rows] = ext_v[:, 2 : 2 + depth, 2 + rows]

        def one(i, carry):
            oz, oy = lax.div(i, 3), lax.rem(i, 3)
            for g in range(groups):
                near = near_v[g, pl.ds(oz, depth), pl.ds(oy, rows)].astype(F32)
                for ox in range(3):
                    product = (near * shifted[g, ox]).reshape(octets)
                    eights[3 * i + ox, :, parts[g]] = jnp.sum(product, axis=0)
            return carry

        lax.fori_loop(0, 9, one, 0)

    def half_copy(stage):
        slot = (1 - core, 2) if stage == 0 else (core, 3)
        return pltpu.make_async_remote_copy(
            src_ref=halves.at[slot[0]],
            dst_ref=halves.at[slot[1]],
            send_sem=half_send.at[stage],
            recv_sem=half_recv.at[stage],
            device_id=partner,
            device_id_type=MESH,
        )

    def sum_begin():
        total = jnp.sum(eights[...], axis=1)
        for g in range(groups):
            halves[g] = total[:, parts[g]]
        half_copy(0).start()

    def sum_copy(r, step):
        digits = sum_rounds[r]
        me = member_of(digits)
        return pltpu.make_async_remote_copy(
            src_ref=terms.at[r, me],
            dst_ref=terms.at[r, me],
            send_sem=sum_send.at[r],
            recv_sem=sum_recv.at[r],
            device_id=peer(digits, lax.rem(me + step, size_of(digits))),
            device_id_type=MESH,
        )

    def sum_all(r):
        n = size_of(sum_rounds[r])
        return pltpu.make_async_remote_copy(
            src_ref=terms.at[r, pl.ds(0, n - 1)],
            dst_ref=terms.at[r, pl.ds(0, n - 1)],
            send_sem=sum_send.at[r],
            recv_sem=sum_recv.at[r],
            device_id=partner,
            device_id_type=MESH,
        )

    def sum_start(r, total):
        terms[r, member_of(sum_rounds[r])] = total.astype(BF16)
        for step in range(1, size_of(sum_rounds[r])):
            sum_copy(r, step).start()

    def sum_first():
        half_copy(0).wait_recv()
        sum_start(0, halves[core] + halves[2])

    def sum_got(r):
        sum_all(r).wait_recv()
        total = terms[r, 0].astype(F32)
        for m in range(1, size_of(sum_rounds[r])):
            total = total + terms[r, m].astype(F32)
        return total

    def sum_second():
        sum_start(1, sum_got(0))

    def sum_third():
        total = sum_got(1) * ((tokens * sections * rows_n) ** -0.5)
        half_copy(0).wait_send()
        halves[core] = total
        half_copy(1).start()

    def sum_last():
        half_copy(1).wait_recv()
        mine, other = halves[core, 0:27], halves[3, 0:27]
        cg_ref[:, parts[0]] = jnp.where(core == 0, mine, other)
        cg_ref[:, parts[1]] = jnp.where(core == 0, other, mine)

    z_slots, y_slots, m_relays, p_relays = (0, 1), (2, 3), (4, 5), (6, 7)

    def relay(kind):
        halo_got(kind, z_slots[:1])
        halo_start(kind, m_relays)
        halo_got(kind, z_slots[1:])
        halo_start(kind, p_relays)

    lax.fori_loop(0, 9, filter_values, 0)
    relay(0)
    halo_got(0, y_slots)
    for corner in range(4):

        @pl.when(both(CORNERS[corner]))
        def _(corner=corner):
            near_copy(corner).wait_recv()

    filter_terms()
    sum_begin()
    relay(1)
    sum_first()
    relay(2)
    halo_got(0, m_relays + p_relays)
    halo_got(1, y_slots + m_relays + p_relays)
    make_mask()
    lax.fori_loop(0, 2, attend(0), 0)
    send_rows(0, 1)
    lax.fori_loop(2, rows, attend(0), 0)
    send_rows(0, 0)
    halo_got(2, y_slots + m_relays + p_relays)
    lax.fori_loop(0, 2, attend(1), 0)
    send_rows(1, 1)
    lax.fori_loop(2, rows, attend(1), 0)
    send_rows(1, 0)
    sum_second()
    send_sections(0)
    send_sections(1)
    for kind in range(3):
        halo_sent(kind, range(8))
    for corner in range(4):

        @pl.when(both(opposite(corner)))
        def _(corner=corner):
            near_copy(corner).wait_send()

    sum_all(0).wait_send()
    sum_third()
    for g in range(groups):
        for slot in range(2):
            part_sent(g, "y", slot)
    finish(0)
    sum_last()
    finish(1)
    for g in range(groups):
        for slot in range(2):
            part_sent(g, "z", slot)
    sum_all(1).wait_send()
    half_copy(1).wait_send()


def write_out(*refs):
    n = len(refs) // 2
    sems = refs[-1]
    copies = [pltpu.make_async_copy(refs[i], refs[n + i], sems.at[i]) for i in range(n)]
    for copy in copies:
        copy.start()
    for copy in copies:
        copy.wait()


def shards(sections, rows_n, queries, keys, values, cotangent, conv_weight, block_keep):
    depth, rows, cols, channels = queries.shape
    groups = channels // LANES
    heads_rows = depth * GROUP_HEADS * cols
    most = max(sections * rows_n // 32, 16)
    big = jax.ShapeDtypeStruct(queries.shape, BF16)
    small = jax.ShapeDtypeStruct(conv_weight.shape, F32)
    vmem = pl.BlockSpec(memory_space=pltpu.VMEM)
    hbm = pl.BlockSpec(memory_space=pltpu.HBM)
    dma = pltpu.SemaphoreType.DMA
    ext = (groups, depth + 4, rows + 4, cols, LANES)
    results = pl.pallas_call(
        partial(kernel, sections, rows_n, depth, rows, cols),
        out_shape=(big, big, big, small),
        in_specs=[hbm] * 6,
        out_specs=(vmem,) * 4,
        scratch_shapes=[
            pltpu.VMEM(queries.shape, BF16),
            pltpu.VMEM(queries.shape, BF16),
            pltpu.VMEM(conv_weight.shape, BF16),
            pltpu.SMEM(block_keep.shape, jnp.int32),
            pltpu.VMEM(ext, BF16),
            pltpu.VMEM(ext, BF16),
            pltpu.VMEM((groups, depth + 2, rows + 2, cols, LANES), BF16),
            pltpu.VMEM((groups, 2, depth + 4, rows + 4, cols, LANES), F32),
            pltpu.VMEM((groups, rows, heads_rows, LANES), BF16),
            pltpu.VMEM((groups, rows, heads_rows, LANES), BF16),
            pltpu.VMEM((groups, 3, depth, rows, cols, LANES), F32),
            pltpu.VMEM((27, 8, channels), F32),
            pltpu.VMEM((32, 8, channels), F32),
            pltpu.VMEM((depth + 4, rows + 4, cols, LANES), F32),
            pltpu.VMEM((groups, 2, 2, depth + 4, 2, cols, LANES), BF16),
            pltpu.VMEM((groups, 2, 2, depth + 4, 2, cols, LANES), BF16),
            pltpu.VMEM((groups, 2, 2, 2, rows, cols, LANES), BF16),
            pltpu.VMEM((groups, 2, 2, 2, rows, cols, LANES), BF16),
            pltpu.VMEM((4, 32, LANES), F32),
            pltpu.VMEM((2, most, 32, LANES), BF16),
            dma((8,)),
            dma((3, 8)),
            dma((3, 8)),
            dma((4,)),
            dma((4,)),
            dma((groups, 2)),
            dma((groups, 2)),
            dma((groups, 2)),
            dma((groups, 2)),
            dma((2,)),
            dma((2,)),
            dma((2,)),
            dma((2,)),
        ],
        compiler_params=pltpu.CompilerParams(
            collective_id=0, has_side_effects=True, vmem_limit_bytes=60 * 1024 * 1024
        ),
    )(queries, keys, values, cotangent, conv_weight, block_keep)
    return pl.pallas_call(
        write_out,
        out_shape=(big, big, big, small),
        in_specs=[vmem] * 4,
        out_specs=(hbm,) * 4,
        scratch_shapes=[dma((4,))],
    )(*results)


def solution(mesh):
    in_specs = (
        P("gz", "gy", None, None),
        P("gz", "gy", None, None),
        P("gz", "gy", None, None),
        P("gz", "gy", None, None),
        P(),
        P("gz", "gy", None),
    )
    out_specs = (
        P("gz", "gy", None, None),
        P("gz", "gy", None, None),
        P("gz", "gy", None, None),
        P(),
    )
    return jax.shard_map(
        partial(shards, mesh.shape["gz"], mesh.shape["gy"]),
        mesh=mesh,
        in_specs=in_specs,
        out_specs=out_specs,
        check_vma=False,
    )
```

```python
from functools import partial

import jax
import jax.numpy as jnp
from jax import lax
from jax.experimental import pallas as pl
from jax.experimental.pallas import tpu as pltpu
from jax.sharding import PartitionSpec as P

HEAD = 32
BX = 8
LANES = 128
GROUP_HEADS = LANES // HEAD
DEAD = 4.0
LOG2E = 1.4426950408889634
HALO_COPIES = 24
MESH = pl.DeviceIdType.MESH
F32 = jnp.float32
BF16 = jnp.bfloat16
SIDES = ("zm", "zp", "ym", "yp")
CORNERS = (("zm", "ym"), ("zm", "yp"), ("zp", "ym"), ("zp", "yp"))


def rounds_of(sections, rows):
    if sections == 16 and rows == 16:
        return [[("gz", 4, 4), ("gy", 8, 2)], [("gz", 1, 4), ("gy", 2, 4)]]
    return [[("gz", 1, sections)], [("gy", 2, rows // 2)]]


def kernel(
    sections,
    rows_n,
    depth,
    rows,
    cols,
    q_hbm,
    k_hbm,
    v_hbm,
    g_hbm,
    w_hbm,
    keep_hbm,
    gq_ref,
    gk_ref,
    gv_ref,
    cg_ref,
    q_ref,
    g_ref,
    w_ref,
    keep_ref,
    ext,
    near_v,
    acc,
    qm,
    gm,
    shifted,
    filt,
    eights,
    mask,
    part_y,
    got_y,
    part_z,
    got_z,
    halves,
    terms,
    load_sem,
    halo_send,
    halo_recv,
    near_send,
    near_recv,
    py_send,
    py_recv,
    pz_send,
    pz_recv,
    half_send,
    half_recv,
    sum_send,
    sum_recv,
):
    groups = acc.shape[0]
    tokens = depth * rows * cols
    place = {"gz": lax.axis_index("gz"), "gy": lax.axis_index("gy")}
    gz, gy = place["gz"], place["gy"]
    has = {
        "zm": gz > 0,
        "zp": gz < sections - 1,
        "ym": gy > 0,
        "yp": gy < rows_n - 1,
    }
    shift = {"zm": -1, "zp": 1, "ym": -1, "yp": 1}
    core = lax.rem(gy, 2)
    partner = (gz, gy + 1 - 2 * core)
    sum_rounds = rounds_of(sections, rows_n)

    def both(names):
        found = has[names[0]]
        for name in names[1:]:
            found = jnp.logical_and(found, has[name])
        return found

    def device(names):
        to = dict(place)
        for name in names:
            axis = "g" + name[0]
            to[axis] = to[axis] + shift[name]
        return (to["gz"], to["gy"])

    def digit(spec):
        axis, stride, count = spec
        return lax.rem(lax.div(place[axis], stride), count)

    def member_of(digits):
        m = 0
        for spec in digits:
            m = m * spec[2] + digit(spec)
        return m

    def peer(digits, moves):
        out = dict(place)
        for spec, move in zip(digits, moves):
            axis, stride, count = spec
            own = digit(spec)
            out[axis] = out[axis] + (lax.rem(own + move, count) - own) * stride
        return (out["gz"], out["gy"])

    def moves_of(digits):
        moves = [()]
        for _, _, count in digits:
            moves = [m + (k,) for m in moves for k in range(count)]
        weight = lambda m: sum(min(k, spec[2] - k) * spec[3] for k, spec in zip(m, hops))
        hops = [spec + (2 if spec[:2] == ("gz", 4) else 1,) for spec in digits]
        return sorted((m for m in moves if any(m)), key=lambda m: (-weight(m), m))

    def size_of(digits):
        n = 1
        for spec in digits:
            n *= spec[2]
        return n

    def load(source, target, sem):
        return pltpu.make_async_copy(source, target, load_sem.at[sem])

    z_own, z_first, z_last = pl.ds(2, depth), pl.ds(0, 2), pl.ds(2 + depth, 2)
    inner, low, high = pl.ds(2, rows), pl.ds(2, 2), pl.ds(rows, 2)
    y_first, y_last = pl.ds(0, 2), pl.ds(2 + rows, 2)
    parts = [slice(g * LANES, (g + 1) * LANES) for g in range(groups)]
    loads = [load(keep_hbm, keep_ref, 0)]
    loads += [load(v_hbm.at[:, :, :, parts[g]], ext.at[g, 1, z_own, inner], 1 + g) for g in range(groups)]
    loads += [load(k_hbm.at[:, :, :, parts[g]], ext.at[g, 0, z_own, inner], 3 + g) for g in range(groups)]
    loads += [load(g_hbm, g_ref, 5), load(q_hbm, q_ref, 6), load(w_hbm, w_ref, 7)]
    for copy in loads:
        copy.start()

    barrier = pltpu.get_barrier_semaphore()
    expected = 0
    for names in tuple((side,) for side in SIDES) + CORNERS:

        @pl.when(both(names))
        def _(names=names):
            pl.semaphore_signal(barrier, inc=1, device_id=device(names), device_id_type=MESH)

        expected = expected + both(names).astype(jnp.int32)
    pl.semaphore_signal(barrier, inc=1, device_id=partner, device_id_type=MESH)
    expected = expected + 1
    for digits in sum_rounds:
        for moves in moves_of(digits):
            pl.semaphore_signal(barrier, inc=1, device_id=peer(digits, moves), device_id_type=MESH)
        expected = expected + (size_of(digits) - 1)

    loads[0].wait()
    keep_low = keep_ref[0, 0, 0].astype(F32)
    keep_high = keep_ref[0, 0, 1].astype(F32)
    row_x = lax.broadcasted_iota(jnp.int32, (cols, LANES), 0)
    row_keep = jnp.where(row_x < BX, keep_low, keep_high)
    lane = lax.broadcasted_iota(jnp.int32, (1, LANES), 1)
    lane_x = lane % cols
    lane_keep = jnp.where(lane_x < BX, keep_low, keep_high)
    lane_head = lane // HEAD

    for g in range(groups):
        loads[1 + g].wait()
    pl.semaphore_wait(barrier, expected)

    every = pl.ds(0, groups)
    border = {"zp": 1 + depth, "zm": 2}
    behind = {"zp": 2, "zm": 1 + depth}
    far = {"zp": -depth, "zm": depth}

    def along_z(name, to):
        if name == "near":
            return (every, 1, pl.ds(border[to], 1), inner), (every, 1, pl.ds(border[to] + far[to], 1), inner)
        g = int(name[-1])
        if name[0] == "v":
            return (g, 1, pl.ds(behind[to], 1), inner), (g, 1, pl.ds(behind[to] + far[to], 1), inner)
        return (g, 0, z_own, inner), (g, 0, z_first if to == "zp" else z_last, inner)

    halo = []
    index = {}
    for name in ["near"] + [kind + str(g) for g in range(groups) for kind in ("v", "k")]:
        for to, source in (("zp", "zm"), ("zm", "zp")):
            src, dst = along_z(name, to)
            index[name, source] = len(halo)
            halo.append(((to,), src, dst, (source,)))
    for name, at in [("vy", (every, 1))] + [("ky" + str(g), (g, 0)) for g in range(groups)]:
        index[name, "ym"] = len(halo)
        halo.append((("yp",), at + (z_own, high), at + (z_own, y_first), ("ym",)))
        index[name, "yp"] = len(halo)
        halo.append((("ym",), at + (z_own, low), at + (z_own, y_last), ("yp",)))
    for g in range(groups):
        kv = pl.ds(0, 2)
        for source, z in (("zm", z_first), ("zp", z_last)):
            index["c", g, "ym", source] = len(halo)
            halo.append((("yp", source), (g, kv, z, high), (g, kv, z, y_first), ("ym", source)))
            index["c", g, "yp", source] = len(halo)
            halo.append((("ym", source), (g, kv, z, low), (g, kv, z, y_last), ("yp", source)))
    assert len(halo) == HALO_COPIES

    def halo_copy(slot):
        to, src, dst, _ = halo[slot]
        return pltpu.make_async_remote_copy(
            src_ref=ext.at[src],
            dst_ref=ext.at[dst],
            send_sem=halo_send.at[slot],
            recv_sem=halo_recv.at[slot],
            device_id=device(to[:1]),
            device_id_type=MESH,
        )

    def halo_start(*names):
        for name in names:
            slot = index[name]

            @pl.when(both(halo[slot][0]))
            def _(slot=slot):
                halo_copy(slot).start()

    def halo_got(*names):
        for name in names:
            slot = index[name]

            @pl.when(both(halo[slot][3]))
            def _(slot=slot):
                halo_copy(slot).wait_recv()

    def halo_sent():
        for slot in range(len(halo)):

            @pl.when(both(halo[slot][0]))
            def _(slot=slot):
                halo_copy(slot).wait_send()

    def near_copy(corner):
        up_z, up_y = CORNERS[corner][0] == "zm", CORNERS[corner][1] == "ym"
        return pltpu.make_async_remote_copy(
            src_ref=ext.at[:, 1, 1 + depth if up_z else 2, 1 + rows if up_y else 2],
            dst_ref=near_v.at[:, 0 if up_z else 1 + depth, 0 if up_y else 1 + rows],
            send_sem=near_send.at[corner],
            recv_sem=near_recv.at[corner],
            device_id=device(("zp" if up_z else "zm", "yp" if up_y else "ym")),
            device_id_type=MESH,
        )

    def opposite(corner):
        return tuple(name[0] + ("p" if name[1] == "m" else "m") for name in CORNERS[corner])

    halo_start(("near", "zm"), ("near", "zp"), ("vy", "ym"), ("vy", "yp"))
    for corner in range(4):

        @pl.when(both(opposite(corner)))
        def _(corner=corner):
            near_copy(corner).start()

    for g in range(groups):
        loads[3 + g].wait()
        own = ext[g, 0, 2 : 2 + depth, 2 : 2 + rows].astype(F32)
        ext[g, 0, 2 : 2 + depth, 2 : 2 + rows] = jnp.where(row_keep > 0.5, own, DEAD).astype(BF16)

    for g in range(groups):
        for kind in ("v", "k"):
            halo_start((kind + str(g), "zm"), (kind + str(g), "zp"))
        halo_start(("ky" + str(g), "ym"), ("ky" + str(g), "yp"))

    for side, where in (
        ("zm", (z_first,)),
        ("zp", (z_last,)),
        ("ym", (slice(None), y_first)),
        ("yp", (slice(None), y_last)),
    ):

        @pl.when(jnp.logical_not(has[side]))
        def _(side=side, where=where):
            shape = ext[(slice(None), 0) + where].shape
            ext[(slice(None), 0) + where] = jnp.full(shape, DEAD, BF16)
            ext[(slice(None), 1) + where] = jnp.zeros(shape, BF16)
            got = got_z if side[0] == "z" else got_y
            slot = 0 if side[1] == "m" else 1
            got[:, slot] = jnp.zeros(got[:, slot].shape, BF16)

    for corner in range(4):

        @pl.when(jnp.logical_not(both(CORNERS[corner])))
        def _(corner=corner):
            z = 0 if CORNERS[corner][0] == "zm" else 1 + depth
            y = 0 if CORNERS[corner][1] == "ym" else 1 + rows
            near_v[:, z, y] = jnp.zeros((groups, cols, LANES), BF16)

    for copy in loads[5:]:
        copy.wait()
    for o in range(27):
        filt[o] = jnp.broadcast_to(w_ref[o : o + 1].astype(F32), filt.shape[1:])

    def own_row(y):
        for g in range(groups):
            part = parts[g]
            for z in range(depth):
                q_row = q_ref[z, y, :, part].astype(F32)
                g_row = g_ref[z, y, :, part].astype(F32)
                for h in range(GROUP_HEADS):
                    at = pl.ds(((y % 2) * depth * GROUP_HEADS + z * GROUP_HEADS + h) * cols, cols)
                    mine = lane_head == h
                    qm[g, y // 2, at] = jnp.where(mine, q_row, 0.0).astype(BF16)
                    gm[g, y // 2, at] = jnp.where(mine, g_row, 0.0).astype(BF16)
                none = jnp.zeros((1, LANES), F32)
                shifted[g, 0, z, y] = jnp.concatenate([g_row[1:], none], axis=0)
                shifted[g, 1, z, y] = g_row
                shifted[g, 2, z, y] = jnp.concatenate([none, g_row[:-1]], axis=0)

    for y in range(rows):
        own_row(y)
    acc[...] = jnp.zeros(acc.shape, F32)
    eights[27:] = jnp.zeros((5, 8, eights.shape[2]), F32)
    octets = (depth * rows * cols // 8, 8, LANES)
    whole = (depth, rows, cols, LANES)

    def filter_values(i, carry):
        oz, oy = lax.div(i, 3), lax.rem(i, 3)
        for g in range(groups):
            total = acc[g, 1, pl.ds(1 + oz, depth), pl.ds(1 + oy, rows)].reshape(octets)
            for ox in range(3):
                total = total + filt[3 * i + ox, :, parts[g]] * shifted[g, ox].reshape(octets)
            acc[g, 1, pl.ds(1 + oz, depth), pl.ds(1 + oy, rows)] = total.reshape(whole)
        return carry

    band = jnp.abs(row_x - lane_x) <= 2
    half = lax.broadcasted_iota(jnp.int32, (cols, LANES), 1) // (GROUP_HEADS * cols)

    def make_mask():
        for z in range(depth + 4):
            reach = band
            for own in range(depth):
                if not own <= z <= own + 4:
                    reach = jnp.logical_and(reach, half != own)
            live = jnp.where(reach, 1.0, 0.0)
            mask[z] = jnp.where(ext[0, 0, z].astype(F32) < 3.0, live, 0.0)

    scaling = HEAD**-0.5
    keys_n = (depth + 4) * 6 * cols
    head_row = lax.broadcasted_iota(jnp.int32, (2 * depth * GROUP_HEADS * cols, LANES), 0)
    head_row = (head_row // cols) % GROUP_HEADS
    own_head = head_row == lax.broadcasted_iota(jnp.int32, head_row.shape, 1) // HEAD
    nt = (((1,), (1,)), ((), ()))
    tn = (((0,), (0,)), ((), ()))

    def beside(first, second):
        none = jnp.zeros((depth + 4, 1, cols, LANES), first.dtype)
        first = jnp.concatenate([first, none], axis=1)
        second = jnp.concatenate([none, second], axis=1)
        return jnp.concatenate([first, second], axis=-1).reshape(keys_n, 2 * LANES)

    def attend(g, pair):
        y = 2 * pair
        keys = ext[g, 0, :, y : y + 6].reshape(keys_n, LANES)
        values = ext[g, 1, :, y : y + 6].reshape(keys_n, LANES)
        queries, grads = qm[g, pair], gm[g, pair]
        shape = (depth + 4, 6, cols, 2 * LANES)
        scores = lax.dot_general(keys, queries, nt, preferred_element_type=F32).reshape(shape)
        dprobs = lax.dot_general(values, grads, nt, preferred_element_type=F32).reshape(shape)
        lows, dscores = [], []
        for i in range(2):
            part = slice(i * LANES, (i + 1) * LANES)
            weights = jnp.exp2(scores[:, i : i + 5, :, part] * (scaling * LOG2E)) * mask[:, y + i : y + i + 5]
            totals = jnp.sum(weights, axis=(0, 1, 2), keepdims=True) + (1.0 - lane_keep)
            probs = weights * (lane_keep / totals)
            low = probs.astype(BF16)
            dprob = dprobs[:, i : i + 5, :, part]
            deltas = jnp.sum(low.astype(F32) * dprob, axis=(0, 1, 2), keepdims=True)
            lows.append(low)
            dscores.append((scaling * probs * (dprob - deltas)).astype(BF16))
        low, dscore = beside(*lows), beside(*dscores)
        shape = (depth + 4, 6, cols, LANES)
        acc[g, 1, :, y : y + 6] += jnp.dot(low, grads, preferred_element_type=F32).reshape(shape)
        acc[g, 0, :, y : y + 6] += jnp.dot(dscore, queries, preferred_element_type=F32).reshape(shape)
        dq = lax.dot_general(dscore, keys, tn, preferred_element_type=F32)
        dq = jnp.where(own_head, dq, 0.0).reshape(2, depth, GROUP_HEADS, cols, LANES)
        dq = jnp.sum(dq, axis=2).astype(BF16)
        for i in range(2):
            gq_ref[:, y + i, :, parts[g]] = dq[i]

    def part_copy(g, stage, slot):
        if stage == "y":
            src, dst, sends, recvs = part_y, got_y, py_send, py_recv
        else:
            src, dst, sends, recvs = part_z, got_z, pz_send, pz_recv
        to = stage + ("p" if slot == 0 else "m")
        source = stage + ("m" if slot == 0 else "p")
        copy = pltpu.make_async_remote_copy(
            src_ref=src.at[g, slot],
            dst_ref=dst.at[g, slot],
            send_sem=sends.at[g, slot],
            recv_sem=recvs.at[g, slot],
            device_id=device((to,)),
            device_id_type=MESH,
        )
        return to, source, copy

    def part_start(g, stage, slot):
        to, _, copy = part_copy(g, stage, slot)

        @pl.when(has[to])
        def _():
            copy.start()

    def part_got(g, stage, slot):
        _, source, copy = part_copy(g, stage, slot)

        @pl.when(has[source])
        def _():
            copy.wait_recv()

    def part_sent(g, stage, slot):
        to, _, copy = part_copy(g, stage, slot)

        @pl.when(has[to])
        def _():
            copy.wait_send()

    def send_rows(g, slot):
        at = 2 + rows if slot == 0 else 0
        part_y[g, slot] = acc[g, :, :, at : at + 2].astype(BF16)
        part_start(g, "y", slot)

    def send_sections(g):
        part_got(g, "y", 0)
        part_got(g, "y", 1)
        acc[g, :, :, 2:4] += got_y[g, 0].astype(F32)
        acc[g, :, :, rows : rows + 2] += got_y[g, 1].astype(F32)
        for slot in range(2):
            at = 2 + depth if slot == 0 else 0
            part_z[g, slot] = acc[g, :, at : at + 2, 2 : 2 + rows].astype(BF16)
            part_start(g, "z", slot)

    def finish(g):
        part_got(g, "z", 0)
        part_got(g, "z", 1)
        for kind, out in ((0, gk_ref), (1, gv_ref)):
            total = acc[g, kind, 2 : 2 + depth, 2 : 2 + rows]
            total = total + got_z[g, 0, kind].astype(F32) + got_z[g, 1, kind].astype(F32)
            out[:, :, :, parts[g]] = total.astype(BF16)

    def filter_terms():
        values = ext.at[:, 1]
        near_v[:, 1 : 1 + depth, 1 : 1 + rows] = values[:, 2 : 2 + depth, 2 : 2 + rows]
        near_v[:, 0, 1 : 1 + rows] = values[:, 1, 2 : 2 + rows]
        near_v[:, 1 + depth, 1 : 1 + rows] = values[:, 2 + depth, 2 : 2 + rows]
        near_v[:, 1 : 1 + depth, 0] = values[:, 2 : 2 + depth, 1]
        near_v[:, 1 : 1 + depth, 1 + rows] = values[:, 2 : 2 + depth, 2 + rows]

        def one(i, carry):
            oz, oy = lax.div(i, 3), lax.rem(i, 3)
            for g in range(groups):
                near = near_v[g, pl.ds(oz, depth), pl.ds(oy, rows)].astype(F32)
                for ox in range(3):
                    product = (near * shifted[g, ox]).reshape(octets)
                    eights[3 * i + ox, :, parts[g]] = jnp.sum(product, axis=0)
            return carry

        lax.fori_loop(0, 9, one, 0)

    def half_copy(stage):
        slot = (1 - core, 2) if stage == 0 else (core, 3)
        return pltpu.make_async_remote_copy(
            src_ref=halves.at[slot[0]],
            dst_ref=halves.at[slot[1]],
            send_sem=half_send.at[stage],
            recv_sem=half_recv.at[stage],
            device_id=partner,
            device_id_type=MESH,
        )

    def sum_begin():
        total = jnp.sum(eights[...], axis=1)
        for g in range(groups):
            halves[g] = total[:, parts[g]]
        half_copy(0).start()

    def sum_copy(r, moves):
        digits = sum_rounds[r]
        me = member_of(digits)
        return pltpu.make_async_remote_copy(
            src_ref=terms.at[r, me],
            dst_ref=terms.at[r, me],
            send_sem=sum_send.at[r],
            recv_sem=sum_recv.at[r],
            device_id=peer(digits, moves),
            device_id_type=MESH,
        )

    def sum_all(r):
        n = size_of(sum_rounds[r])
        return pltpu.make_async_remote_copy(
            src_ref=terms.at[r, pl.ds(0, n - 1)],
            dst_ref=terms.at[r, pl.ds(0, n - 1)],
            send_sem=sum_send.at[r],
            recv_sem=sum_recv.at[r],
            device_id=partner,
            device_id_type=MESH,
        )

    def sum_start(r, total):
        terms[r, member_of(sum_rounds[r])] = total.astype(BF16)
        for moves in moves_of(sum_rounds[r]):
            sum_copy(r, moves).start()

    def sum_first():
        half_copy(0).wait_recv()
        sum_start(0, halves[core] + halves[2])

    def sum_got(r):
        sum_all(r).wait_recv()
        total = terms[r, 0].astype(F32)
        for m in range(1, size_of(sum_rounds[r])):
            total = total + terms[r, m].astype(F32)
        return total

    def sum_second():
        sum_start(1, sum_got(0))

    def sum_third():
        total = sum_got(1) * ((tokens * sections * rows_n) ** -0.5)
        half_copy(0).wait_send()
        halves[core] = total
        half_copy(1).start()

    def sum_last():
        half_copy(1).wait_recv()
        mine, other = halves[core, 0:27], halves[3, 0:27]
        cg_ref[:, parts[0]] = jnp.where(core == 0, mine, other)
        cg_ref[:, parts[1]] = jnp.where(core == 0, other, mine)

    def relay(g):
        for source in ("zm", "zp"):
            halo_got(("v" + str(g), source), ("k" + str(g), source))
            halo_start(("c", g, "ym", source), ("c", g, "yp", source))

    def arrived(g):
        halo_got(("ky" + str(g), "ym"), ("ky" + str(g), "yp"))
        for source in ("zm", "zp"):
            halo_got(("c", g, "ym", source), ("c", g, "yp", source))

    lax.fori_loop(0, 9, filter_values, 0)
    halo_got(("near", "zm"), ("near", "zp"), ("vy", "ym"), ("vy", "yp"))
    for corner in range(4):

        @pl.when(both(CORNERS[corner]))
        def _(corner=corner):
            near_copy(corner).wait_recv()

    relay(0)
    filter_terms()
    sum_begin()
    relay(1)
    sum_first()
    arrived(0)
    make_mask()
    attend(0, 0)
    send_rows(0, 1)
    attend(0, 1)
    send_rows(0, 0)
    arrived(1)
    attend(1, 0)
    send_rows(1, 1)
    attend(1, 1)
    send_rows(1, 0)
    send_sections(0)
    sum_second()
    send_sections(1)
    halo_sent()
    for corner in range(4):

        @pl.when(both(opposite(corner)))
        def _(corner=corner):
            near_copy(corner).wait_send()

    sum_all(0).wait_send()
    for g in range(groups):
        for slot in range(2):
            part_sent(g, "y", slot)
    sum_third()
    finish(0)
    sum_last()
    finish(1)
    for g in range(groups):
        for slot in range(2):
            part_sent(g, "z", slot)
    sum_all(1).wait_send()
    half_copy(1).wait_send()


def write_out(*refs):
    n = len(refs) // 2
    sems = refs[-1]
    copies = [pltpu.make_async_copy(refs[i], refs[n + i], sems.at[i]) for i in range(n)]
    for copy in copies:
        copy.start()
    for copy in copies:
        copy.wait()


def shards(sections, rows_n, queries, keys, values, cotangent, conv_weight, block_keep):
    depth, rows, cols, channels = queries.shape
    groups = channels // LANES
    heads_rows = depth * GROUP_HEADS * cols
    most = max(sections * rows_n // 32, 16)
    big = jax.ShapeDtypeStruct(queries.shape, BF16)
    small = jax.ShapeDtypeStruct(conv_weight.shape, F32)
    vmem = pl.BlockSpec(memory_space=pltpu.VMEM)
    hbm = pl.BlockSpec(memory_space=pltpu.HBM)
    dma = pltpu.SemaphoreType.DMA
    results = pl.pallas_call(
        partial(kernel, sections, rows_n, depth, rows, cols),
        out_shape=(big, big, big, small),
        in_specs=[hbm] * 6,
        out_specs=(vmem,) * 4,
        scratch_shapes=[
            pltpu.VMEM(queries.shape, BF16),
            pltpu.VMEM(queries.shape, BF16),
            pltpu.VMEM(conv_weight.shape, BF16),
            pltpu.SMEM(block_keep.shape, jnp.int32),
            pltpu.VMEM((groups, 2, depth + 4, rows + 4, cols, LANES), BF16),
            pltpu.VMEM((groups, depth + 2, rows + 2, cols, LANES), BF16),
            pltpu.VMEM((groups, 2, depth + 4, rows + 4, cols, LANES), F32),
            pltpu.VMEM((groups, rows // 2, 2 * heads_rows, LANES), BF16),
            pltpu.VMEM((groups, rows // 2, 2 * heads_rows, LANES), BF16),
            pltpu.VMEM((groups, 3, depth, rows, cols, LANES), F32),
            pltpu.VMEM((27, 8, channels), F32),
            pltpu.VMEM((32, 8, channels), F32),
            pltpu.VMEM((depth + 4, rows + 4, cols, LANES), F32),
            pltpu.VMEM((groups, 2, 2, depth + 4, 2, cols, LANES), BF16),
            pltpu.VMEM((groups, 2, 2, depth + 4, 2, cols, LANES), BF16),
            pltpu.VMEM((groups, 2, 2, 2, rows, cols, LANES), BF16),
            pltpu.VMEM((groups, 2, 2, 2, rows, cols, LANES), BF16),
            pltpu.VMEM((4, 32, LANES), F32),
            pltpu.VMEM((2, most, 32, LANES), BF16),
            dma((8,)),
            dma((HALO_COPIES,)),
            dma((HALO_COPIES,)),
            dma((4,)),
            dma((4,)),
            dma((groups, 2)),
            dma((groups, 2)),
            dma((groups, 2)),
            dma((groups, 2)),
            dma((2,)),
            dma((2,)),
            dma((2,)),
            dma((2,)),
        ],
        compiler_params=pltpu.CompilerParams(
            collective_id=0, has_side_effects=True, vmem_limit_bytes=60 * 1024 * 1024
        ),
    )(queries, keys, values, cotangent, conv_weight, block_keep)
    return pl.pallas_call(
        write_out,
        out_shape=(big, big, big, small),
        in_specs=[vmem] * 4,
        out_specs=(hbm,) * 4,
        scratch_shapes=[dma((4,))],
    )(*results)


def solution(mesh):
    in_specs = (
        P("gz", "gy", None, None),
        P("gz", "gy", None, None),
        P("gz", "gy", None, None),
        P("gz", "gy", None, None),
        P(),
        P("gz", "gy", None),
    )
    out_specs = (
        P("gz", "gy", None, None),
        P("gz", "gy", None, None),
        P("gz", "gy", None, None),
        P(),
    )
    return jax.shard_map(
        partial(shards, mesh.shape["gz"], mesh.shape["gy"]),
        mesh=mesh,
        in_specs=in_specs,
        out_specs=out_specs,
        check_vma=False,
    )
```

```python
from functools import partial

import jax
import jax.numpy as jnp
from jax import lax
from jax.experimental import pallas as pl
from jax.experimental.pallas import tpu as pltpu
from jax.sharding import PartitionSpec as P

HEAD = 32
BX = 8
LANES = 128
GROUP_HEADS = LANES // HEAD
DEAD = 4.0
LOG2E = 1.4426950408889634
HALO_COPIES = 24
MESH = pl.DeviceIdType.MESH
F32 = jnp.float32
BF16 = jnp.bfloat16
SIDES = ("zm", "zp", "ym", "yp")
CORNERS = (("zm", "ym"), ("zm", "yp"), ("zp", "ym"), ("zp", "yp"))


def rounds_of(sections, rows):
    if sections == 16 and rows == 16:
        return [[("gz", 4, 4), ("gy", 8, 2)], [("gz", 1, 4), ("gy", 2, 4)]]
    return [[("gz", 1, sections)], [("gy", 2, rows // 2)]]


def kernel(
    sections,
    rows_n,
    depth,
    rows,
    cols,
    q_hbm,
    k_hbm,
    v_hbm,
    g_hbm,
    w_hbm,
    keep_hbm,
    gq_ref,
    gk_ref,
    gv_ref,
    cg_ref,
    q_ref,
    g_ref,
    w_ref,
    keep_ref,
    ext,
    near_v,
    acc,
    qm,
    gm,
    shifted,
    filt,
    eights,
    mask,
    part_y,
    got_y,
    part_z,
    got_z,
    halves,
    terms,
    load_sem,
    halo_send,
    halo_recv,
    near_send,
    near_recv,
    py_send,
    py_recv,
    pz_send,
    pz_recv,
    half_send,
    half_recv,
    sum_send,
    sum_recv,
):
    groups = acc.shape[0]
    tokens = depth * rows * cols
    place = {"gz": lax.axis_index("gz"), "gy": lax.axis_index("gy")}
    gz, gy = place["gz"], place["gy"]
    has = {
        "zm": gz > 0,
        "zp": gz < sections - 1,
        "ym": gy > 0,
        "yp": gy < rows_n - 1,
    }
    shift = {"zm": -1, "zp": 1, "ym": -1, "yp": 1}
    core = lax.rem(gy, 2)
    partner = (gz, gy + 1 - 2 * core)
    has["off"] = jnp.logical_or(jnp.logical_and(core == 0, has["ym"]), jnp.logical_and(core == 1, has["yp"]))
    sum_rounds = rounds_of(sections, rows_n)

    def both(names):
        found = True
        for name in names:
            if name != "on":
                found = has[name] if found is True else jnp.logical_and(found, has[name])
        return found

    def when(names):
        found = both(names)
        return (lambda body: body()) if found is True else pl.when(found)

    def device(names):
        if names == ("on",):
            return partner
        if names == ("off",):
            return (gz, gy - 1 + 2 * core)
        to = dict(place)
        for name in names:
            axis = "g" + name[0]
            to[axis] = to[axis] + shift[name]
        return (to["gz"], to["gy"])

    held = {}

    def digit(spec):
        if spec not in held:
            axis, stride, count = spec
            held[spec] = lax.rem(lax.div(place[axis], stride), count)
        return held[spec]

    def member_of(digits):
        m = 0
        for spec in digits:
            m = m * spec[2] + digit(spec)
        return m

    def peer(digits, moves):
        out = dict(place)
        for spec, move in zip(digits, moves):
            axis, stride, count = spec
            own = digit(spec)
            out[axis] = out[axis] + (lax.rem(own + move, count) - own) * stride
        return (out["gz"], out["gy"])

    def moves_of(digits):
        moves = [()]
        for _, _, count in digits:
            moves = [m + (k,) for m in moves for k in range(count)]
        weight = lambda m: sum(min(k, spec[2] - k) * spec[3] for k, spec in zip(m, hops))
        hops = [spec + (2 if spec[:2] == ("gz", 4) else 1,) for spec in digits]
        return sorted((m for m in moves if any(m)), key=lambda m: (-weight(m), m))

    def size_of(digits):
        n = 1
        for spec in digits:
            n *= spec[2]
        return n

    def load(source, target, sem):
        return pltpu.make_async_copy(source, target, load_sem.at[sem])

    z_own, z_first, z_last = pl.ds(2, depth), pl.ds(0, 2), pl.ds(2 + depth, 2)
    inner, low, high = pl.ds(2, rows), pl.ds(2, 2), pl.ds(rows, 2)
    y_first, y_last = pl.ds(0, 2), pl.ds(2 + rows, 2)
    parts = [slice(g * LANES, (g + 1) * LANES) for g in range(groups)]
    loads = [load(keep_hbm, keep_ref, 0)]
    loads += [load(v_hbm.at[:, :, :, parts[g]], ext.at[g, 1, z_own, inner], 1 + g) for g in range(groups)]
    loads += [load(k_hbm.at[:, :, :, parts[g]], ext.at[g, 0, z_own, inner], 3 + g) for g in range(groups)]
    loads += [load(g_hbm, g_ref, 5), load(q_hbm, q_ref, 6), load(w_hbm, w_ref, 7)]
    for copy in loads[:3]:
        copy.start()

    barrier = pltpu.get_barrier_semaphore()
    expected = 0
    for names in tuple((side,) for side in SIDES) + CORNERS:

        @pl.when(both(names))
        def _(names=names):
            pl.semaphore_signal(barrier, inc=1, device_id=device(names), device_id_type=MESH)

        expected = expected + both(names).astype(jnp.int32)
    for digits in sum_rounds:
        for moves in moves_of(digits):
            pl.semaphore_signal(barrier, inc=1, device_id=peer(digits, moves), device_id_type=MESH)
        expected = expected + (size_of(digits) - 1)
    for copy in loads[3:]:
        copy.start()

    loads[0].wait()
    keep_low = keep_ref[0, 0, 0].astype(F32)
    keep_high = keep_ref[0, 0, 1].astype(F32)
    row_x = lax.broadcasted_iota(jnp.int32, (cols, LANES), 0)
    row_keep = jnp.where(row_x < BX, keep_low, keep_high)
    lane = lax.broadcasted_iota(jnp.int32, (1, LANES), 1)
    lane_x = lane % cols
    lane_keep = jnp.where(lane_x < BX, keep_low, keep_high)
    lane_head = lane // HEAD

    for g in range(groups):
        loads[1 + g].wait()
    pl.semaphore_wait(barrier, expected)

    every = pl.ds(0, groups)
    border = {"zp": 1 + depth, "zm": 2}
    behind = {"zp": 2, "zm": 1 + depth}
    far = {"zp": -depth, "zm": depth}

    def along_z(name, to):
        if name == "near":
            return (every, 1, pl.ds(border[to], 1), inner), (every, 1, pl.ds(border[to] + far[to], 1), inner)
        g = int(name[-1])
        if name[0] == "v":
            return (g, 1, pl.ds(behind[to], 1), inner), (g, 1, pl.ds(behind[to] + far[to], 1), inner)
        return (g, 0, z_own, inner), (g, 0, z_first if to == "zp" else z_last, inner)

    sides = {
        "on": (pl.ds(rows - 2 * core, 2), pl.ds((2 + rows) * core, 2), pl.ds((2 + rows) * (1 - core), 2)),
        "off": (pl.ds(2 + 2 * core, 2), pl.ds((2 + rows) * (1 - core), 2), pl.ds((2 + rows) * core, 2)),
    }
    halo = []
    index = {}
    for name in ["near"] + [kind + str(g) for g in range(groups) for kind in ("v", "k")]:
        for to, source in (("zp", "zm"), ("zm", "zp")):
            src, dst = along_z(name, to)
            index[name, source] = len(halo)
            halo.append(((to,), src, dst, (source,), dst))
    for side, (sent, there, here) in sides.items():
        for name, at in [("vy", (every, 1))] + [("ky" + str(g), (g, 0)) for g in range(groups)]:
            index[name, side] = len(halo)
            halo.append(((side,), at + (z_own, sent), at + (z_own, there), (side,), at + (z_own, here)))
        for g in range(groups):
            at = (g, pl.ds(0, 2))
            for source, z in (("zm", z_first), ("zp", z_last)):
                index["c", g, side, source] = len(halo)
                names = (side, source)
                halo.append((names, at + (z, sent), at + (z, there), names, at + (z, here)))
    assert len(halo) == HALO_COPIES

    def halo_copy(slot, here=False):
        to, src, dst, _, dst_here = halo[slot]
        return pltpu.make_async_remote_copy(
            src_ref=ext.at[src],
            dst_ref=ext.at[dst_here if here else dst],
            send_sem=halo_send.at[slot],
            recv_sem=halo_recv.at[slot],
            device_id=device(to[:1]),
            device_id_type=MESH,
        )

    def halo_start(*names):
        for name in names:
            slot = index[name]

            @when(halo[slot][0])
            def _(slot=slot):
                halo_copy(slot).start()

    def halo_got(*names):
        for name in names:
            slot = index[name]

            @when(halo[slot][3])
            def _(slot=slot):
                halo_copy(slot, here=True).wait_recv()

    def halo_sent():
        for slot in range(len(halo)):

            @when(halo[slot][0])
            def _(slot=slot):
                halo_copy(slot).wait_send()

    def near_copy(corner):
        up_z, up_y = CORNERS[corner][0] == "zm", CORNERS[corner][1] == "ym"
        return pltpu.make_async_remote_copy(
            src_ref=ext.at[:, 1, 1 + depth if up_z else 2, 1 + rows if up_y else 2],
            dst_ref=near_v.at[:, 0 if up_z else 1 + depth, 0 if up_y else 1 + rows],
            send_sem=near_send.at[corner],
            recv_sem=near_recv.at[corner],
            device_id=device(("zp" if up_z else "zm", "yp" if up_y else "ym")),
            device_id_type=MESH,
        )

    def opposite(corner):
        return tuple(name[0] + ("p" if name[1] == "m" else "m") for name in CORNERS[corner])

    halo_start(("near", "zm"), ("near", "zp"), ("vy", "off"), ("vy", "on"))
    for corner in range(4):

        @pl.when(both(opposite(corner)))
        def _(corner=corner):
            near_copy(corner).start()

    for g in range(groups):
        loads[3 + g].wait()
        own = ext[g, 0, 2 : 2 + depth, 2 : 2 + rows].astype(F32)
        ext[g, 0, 2 : 2 + depth, 2 : 2 + rows] = jnp.where(row_keep > 0.5, own, DEAD).astype(BF16)

    for g in range(groups):
        for kind in ("v", "k"):
            halo_start((kind + str(g), "zm"), (kind + str(g), "zp"))
        halo_start(("ky" + str(g), "off"), ("ky" + str(g), "on"))

    for side, where in (
        ("zm", (z_first,)),
        ("zp", (z_last,)),
        ("ym", (slice(None), y_first)),
        ("yp", (slice(None), y_last)),
    ):

        @pl.when(jnp.logical_not(has[side]))
        def _(side=side, where=where):
            shape = ext[(slice(None), 0) + where].shape
            ext[(slice(None), 0) + where] = jnp.full(shape, DEAD, BF16)
            ext[(slice(None), 1) + where] = jnp.zeros(shape, BF16)
            got = got_z if side[0] == "z" else got_y
            slot = 0 if side[1] == "m" else 1
            got[:, slot] = jnp.zeros(got[:, slot].shape, BF16)

    for corner in range(4):

        @pl.when(jnp.logical_not(both(CORNERS[corner])))
        def _(corner=corner):
            z = 0 if CORNERS[corner][0] == "zm" else 1 + depth
            y = 0 if CORNERS[corner][1] == "ym" else 1 + rows
            near_v[:, z, y] = jnp.zeros((groups, cols, LANES), BF16)

    for copy in loads[5:]:
        copy.wait()
    for o in range(27):
        filt[o] = jnp.broadcast_to(w_ref[o : o + 1].astype(F32), filt.shape[1:])

    def own_row(y):
        for g in range(groups):
            part = parts[g]
            for z in range(depth):
                q_row = q_ref[z, y, :, part].astype(F32)
                g_row = g_ref[z, y, :, part].astype(F32)
                for h in range(GROUP_HEADS):
                    at = pl.ds(((y % 2) * depth * GROUP_HEADS + z * GROUP_HEADS + h) * cols, cols)
                    mine = lane_head == h
                    qm[g, y // 2, at] = jnp.where(mine, q_row, 0.0).astype(BF16)
                    gm[g, y // 2, at] = jnp.where(mine, g_row, 0.0).astype(BF16)
                none = jnp.zeros((1, LANES), F32)
                shifted[g, 0, z, y] = jnp.concatenate([g_row[1:], none], axis=0)
                shifted[g, 1, z, y] = g_row
                shifted[g, 2, z, y] = jnp.concatenate([none, g_row[:-1]], axis=0)

    for y in range(rows):
        own_row(y)
    acc[...] = jnp.zeros(acc.shape, F32)
    eights[27:] = jnp.zeros((5, 8, eights.shape[2]), F32)
    octets = (depth * rows * cols // 8, 8, LANES)
    whole = (depth, rows, cols, LANES)

    def filter_values(i, carry):
        oz, oy = lax.div(i, 3), lax.rem(i, 3)
        for g in range(groups):
            total = acc[g, 1, pl.ds(1 + oz, depth), pl.ds(1 + oy, rows)].reshape(octets)
            for ox in range(3):
                total = total + filt[3 * i + ox, :, parts[g]] * shifted[g, ox].reshape(octets)
            acc[g, 1, pl.ds(1 + oz, depth), pl.ds(1 + oy, rows)] = total.reshape(whole)
        return carry

    band = jnp.abs(row_x - lane_x) <= 2
    half = lax.broadcasted_iota(jnp.int32, (cols, LANES), 1) // (GROUP_HEADS * cols)

    def make_mask(near):
        for z in range(depth + 4):
            reach = band
            for own in range(depth):
                if not own <= z <= own + 4:
                    reach = jnp.logical_and(reach, half != own)
            live = jnp.where(reach, 1.0, 0.0)
            mask[z, near] = jnp.where(ext[0, 0, z, near].astype(F32) < 3.0, live, 0.0)

    scaling = HEAD**-0.5
    keys_n = (depth + 4) * 6 * cols
    head_row = lax.broadcasted_iota(jnp.int32, (2 * depth * GROUP_HEADS * cols, LANES), 0)
    head_row = (head_row // cols) % GROUP_HEADS
    own_head = head_row == lax.broadcasted_iota(jnp.int32, head_row.shape, 1) // HEAD
    nt = (((1,), (1,)), ((), ()))
    tn = (((0,), (0,)), ((), ()))

    def beside(first, second):
        none = jnp.zeros((depth + 4, 1, cols, LANES), first.dtype)
        first = jnp.concatenate([first, none], axis=1)
        second = jnp.concatenate([none, second], axis=1)
        return jnp.concatenate([first, second], axis=-1).reshape(keys_n, 2 * LANES)

    def attend(g, pair):
        y = 2 * pair
        keys = ext[g, 0, :, pl.ds(y, 6)].reshape(keys_n, LANES)
        values = ext[g, 1, :, pl.ds(y, 6)].reshape(keys_n, LANES)
        queries, grads = qm[g, pair], gm[g, pair]
        shape = (depth + 4, 6, cols, 2 * LANES)
        scores = lax.dot_general(keys, queries, nt, preferred_element_type=F32).reshape(shape)
        dprobs = lax.dot_general(values, grads, nt, preferred_element_type=F32).reshape(shape)
        lows, dscores = [], []
        for i in range(2):
            part = slice(i * LANES, (i + 1) * LANES)
            weights = jnp.exp2(scores[:, i : i + 5, :, part] * (scaling * LOG2E)) * mask[:, pl.ds(y + i, 5)]
            totals = jnp.sum(weights, axis=(0, 1, 2), keepdims=True) + (1.0 - lane_keep)
            probs = weights * (lane_keep / totals)
            low = probs.astype(BF16)
            dprob = dprobs[:, i : i + 5, :, part]
            deltas = jnp.sum(low.astype(F32) * dprob, axis=(0, 1, 2), keepdims=True)
            lows.append(low)
            dscores.append((scaling * probs * (dprob - deltas)).astype(BF16))
        low, dscore = beside(*lows), beside(*dscores)
        shape = (depth + 4, 6, cols, LANES)
        acc[g, 1, :, pl.ds(y, 6)] += jnp.dot(low, grads, preferred_element_type=F32).reshape(shape)
        acc[g, 0, :, pl.ds(y, 6)] += jnp.dot(dscore, queries, preferred_element_type=F32).reshape(shape)

        def own_queries():
            dq = lax.dot_general(dscore, keys, tn, preferred_element_type=F32)
            dq = jnp.where(own_head, dq, 0.0).reshape(2, depth, GROUP_HEADS, cols, LANES)
            dq = jnp.sum(dq, axis=2).astype(BF16)
            for i in range(2):
                gq_ref[:, pl.ds(y + i, 1), :, parts[g]] = dq[i][:, None]

        return own_queries

    first, later = pl.ds(0, 4), pl.ds(4, depth)

    def rows_copy(g, side, stage, here=False):
        slot = core if (side == "on") != here else 1 - core
        z = later if stage else first
        return pltpu.make_async_remote_copy(
            src_ref=part_y.at[g, slot, :, z],
            dst_ref=got_y.at[g, slot, :, z],
            send_sem=py_send.at[g, slot, stage],
            recv_sem=py_recv.at[g, slot, stage],
            device_id=device((side,)),
            device_id_type=MESH,
        )

    def send_rows(g, side):
        slot = core if side == "on" else 1 - core
        at = pl.ds((2 + rows) * (1 - slot), 2)
        part_y[g, slot, :, 0:2] = acc[g, :, 0:2, at].astype(BF16)
        part_y[g, slot, :, 2:4] = acc[g, :, 2 + depth : 4 + depth, at].astype(BF16)
        part_y[g, slot, :, 4 : 4 + depth] = acc[g, :, 2 : 2 + depth, at].astype(BF16)

        @when((side,))
        def _():
            rows_copy(g, side, 0).start()
            rows_copy(g, side, 1).start()

    def got_rows(g, side, stage):
        @when((side,))
        def _():
            rows_copy(g, side, stage, here=True).wait_recv()

    def sections_copy(g, place_, slot):
        return pltpu.make_async_remote_copy(
            src_ref=part_z.at[g, place_, slot],
            dst_ref=got_z.at[g, place_, slot],
            send_sem=pz_send.at[g, place_, slot],
            recv_sem=pz_recv.at[g, place_, slot],
            device_id=device(("zp" if place_ == 0 else "zm",)),
            device_id_type=MESH,
        )

    def send_sections(g, side):
        slot = 1 - core if side == "on" else core
        got_rows(g, side, 0)
        near = pl.ds(2 + 2 * slot, 2)
        for place_, z in ((0, 2 + depth), (1, 0)):
            given = got_y[g, slot, :, 2 * (1 - place_) : 2 * (2 - place_)].astype(F32)
            part_z[g, place_, slot] = (acc[g, :, z : z + 2, near] + given).astype(BF16)

            @pl.when(has["zp" if place_ == 0 else "zm"])
            def _(place_=place_):
                sections_copy(g, place_, slot).start()

    def finish(g):
        got_rows(g, "on", 1)
        got_rows(g, "off", 1)
        for place_, source in ((0, "zm"), (1, "zp")):

            @pl.when(has[source])
            def _(place_=place_):
                for slot in range(2):
                    sections_copy(g, place_, slot).wait_recv()

        for kind, out in ((0, gk_ref), (1, gv_ref)):
            for slot in range(2):
                near = slice(2 + 2 * slot, 4 + 2 * slot)
                total = acc[g, kind, 2 : 2 + depth, near] + got_y[g, slot, kind, 4 : 4 + depth].astype(F32)
                total = total + got_z[g, 0, slot, kind].astype(F32) + got_z[g, 1, slot, kind].astype(F32)
                out[:, 2 * slot : 2 * slot + 2, :, parts[g]] = total.astype(BF16)

    def rows_sent(g):
        for side in ("on", "off"):

            @when((side,))
            def _(side=side):
                rows_copy(g, side, 0).wait_send()
                rows_copy(g, side, 1).wait_send()

    def sections_sent(g):
        for place_, to in ((0, "zp"), (1, "zm")):

            @pl.when(has[to])
            def _(place_=place_):
                for slot in range(2):
                    sections_copy(g, place_, slot).wait_send()

    def filter_terms():
        values = ext.at[:, 1]
        near_v[:, 1 : 1 + depth, 1 : 1 + rows] = values[:, 2 : 2 + depth, 2 : 2 + rows]
        near_v[:, 0, 1 : 1 + rows] = values[:, 1, 2 : 2 + rows]
        near_v[:, 1 + depth, 1 : 1 + rows] = values[:, 2 + depth, 2 : 2 + rows]
        near_v[:, 1 : 1 + depth, 0] = values[:, 2 : 2 + depth, 1]
        near_v[:, 1 : 1 + depth, 1 + rows] = values[:, 2 : 2 + depth, 2 + rows]

        def one(i, carry):
            oz, oy = lax.div(i, 3), lax.rem(i, 3)
            for g in range(groups):
                near = near_v[g, pl.ds(oz, depth), pl.ds(oy, rows)].astype(F32)
                for ox in range(3):
                    product = (near * shifted[g, ox]).reshape(octets)
                    eights[3 * i + ox, :, parts[g]] = jnp.sum(product, axis=0)
            return carry

        lax.fori_loop(0, 9, one, 0)

    def half_copy(stage):
        slot = (1 - core, 2) if stage == 0 else (core, 3)
        return pltpu.make_async_remote_copy(
            src_ref=halves.at[slot[0]],
            dst_ref=halves.at[slot[1]],
            send_sem=half_send.at[stage],
            recv_sem=half_recv.at[stage],
            device_id=partner,
            device_id_type=MESH,
        )

    def sum_begin():
        total = jnp.sum(eights[...], axis=1)
        for g in range(groups):
            halves[g] = total[:, parts[g]]
        half_copy(0).start()

    def sum_copy(r, moves):
        digits = sum_rounds[r]
        me = member_of(digits)
        return pltpu.make_async_remote_copy(
            src_ref=terms.at[r, me],
            dst_ref=terms.at[r, me],
            send_sem=sum_send.at[r],
            recv_sem=sum_recv.at[r],
            device_id=peer(digits, moves),
            device_id_type=MESH,
        )

    def sum_all(r):
        n = size_of(sum_rounds[r])
        return pltpu.make_async_remote_copy(
            src_ref=terms.at[r, pl.ds(0, n - 1)],
            dst_ref=terms.at[r, pl.ds(0, n - 1)],
            send_sem=sum_send.at[r],
            recv_sem=sum_recv.at[r],
            device_id=partner,
            device_id_type=MESH,
        )

    def sum_start(r, total):
        terms[r, member_of(sum_rounds[r])] = total.astype(BF16)
        for moves in moves_of(sum_rounds[r]):
            sum_copy(r, moves).start()

    def sum_first():
        half_copy(0).wait_recv()
        sum_start(0, halves[core] + halves[2])

    def sum_got(r):
        sum_all(r).wait_recv()
        total = terms[r, 0].astype(F32)
        for m in range(1, size_of(sum_rounds[r])):
            total = total + terms[r, m].astype(F32)
        return total

    def sum_second():
        sum_start(1, sum_got(0))

    def sum_third():
        total = sum_got(1) * ((tokens * sections * rows_n) ** -0.5)
        half_copy(0).wait_send()
        halves[core] = total
        half_copy(1).start()

    def sum_last():
        half_copy(1).wait_recv()
        mine, other = halves[core, 0:27], halves[3, 0:27]
        cg_ref[:, parts[0]] = jnp.where(core == 0, mine, other)
        cg_ref[:, parts[1]] = jnp.where(core == 0, other, mine)

    def relay(g):
        for source in ("zm", "zp"):
            halo_got(("v" + str(g), source), ("k" + str(g), source))
            halo_start(("c", g, "off", source), ("c", g, "on", source))

    def arrived(g, side):
        halo_got(("ky" + str(g), side), ("c", g, side, "zm"), ("c", g, side, "zp"))

    lax.fori_loop(0, 9, filter_values, 0)
    halo_got(("near", "zm"), ("near", "zp"), ("vy", "on"), ("vy", "off"))
    for corner in range(4):

        @pl.when(both(CORNERS[corner]))
        def _(corner=corner):
            near_copy(corner).wait_recv()

    filter_terms()
    sum_begin()
    relay(0)
    sum_first()
    relay(1)
    arrived(0, "on")
    make_mask(pl.ds(2 * (1 - core), 6))
    own_queries = attend(0, 1 - core)
    send_rows(0, "on")
    own_queries()
    arrived(0, "off")
    make_mask(pl.ds((2 + rows) * core, 2))
    own_queries = attend(0, core)
    send_rows(0, "off")
    own_queries()
    arrived(1, "on")
    own_queries = attend(1, 1 - core)
    send_rows(1, "on")
    own_queries()
    send_sections(0, "on")
    arrived(1, "off")
    own_queries = attend(1, core)
    send_rows(1, "off")
    own_queries()
    send_sections(0, "off")
    send_sections(1, "on")
    sum_second()
    send_sections(1, "off")
    halo_sent()
    for corner in range(4):

        @pl.when(both(opposite(corner)))
        def _(corner=corner):
            near_copy(corner).wait_send()

    sum_all(0).wait_send()
    for g in range(groups):
        rows_sent(g)
    sum_third()
    sections_sent(0)
    sum_all(1).wait_send()
    finish(0)
    sum_last()
    half_copy(1).wait_send()
    sections_sent(1)
    finish(1)


def write_out(*refs):
    n = len(refs) // 2
    sems = refs[-1]
    copies = [pltpu.make_async_copy(refs[i], refs[n + i], sems.at[i]) for i in range(n)]
    for copy in copies:
        copy.start()
    for copy in copies:
        copy.wait()


def shards(sections, rows_n, queries, keys, values, cotangent, conv_weight, block_keep):
    depth, rows, cols, channels = queries.shape
    groups = channels // LANES
    heads_rows = depth * GROUP_HEADS * cols
    most = max(sections * rows_n // 32, 16)
    big = jax.ShapeDtypeStruct(queries.shape, BF16)
    small = jax.ShapeDtypeStruct(conv_weight.shape, F32)
    vmem = pl.BlockSpec(memory_space=pltpu.VMEM)
    hbm = pl.BlockSpec(memory_space=pltpu.HBM)
    dma = pltpu.SemaphoreType.DMA
    results = pl.pallas_call(
        partial(kernel, sections, rows_n, depth, rows, cols),
        out_shape=(big, big, big, small),
        in_specs=[hbm] * 6,
        out_specs=(vmem,) * 4,
        scratch_shapes=[
            pltpu.VMEM(queries.shape, BF16),
            pltpu.VMEM(queries.shape, BF16),
            pltpu.VMEM(conv_weight.shape, BF16),
            pltpu.SMEM(block_keep.shape, jnp.int32),
            pltpu.VMEM((groups, 2, depth + 4, rows + 4, cols, LANES), BF16),
            pltpu.VMEM((groups, depth + 2, rows + 2, cols, LANES), BF16),
            pltpu.VMEM((groups, 2, depth + 4, rows + 4, cols, LANES), F32),
            pltpu.VMEM((groups, rows // 2, 2 * heads_rows, LANES), BF16),
            pltpu.VMEM((groups, rows // 2, 2 * heads_rows, LANES), BF16),
            pltpu.VMEM((groups, 3, depth, rows, cols, LANES), F32),
            pltpu.VMEM((27, 8, channels), F32),
            pltpu.VMEM((32, 8, channels), F32),
            pltpu.VMEM((depth + 4, rows + 4, cols, LANES), F32),
            pltpu.VMEM((groups, 2, 2, depth + 4, 2, cols, LANES), BF16),
            pltpu.VMEM((groups, 2, 2, depth + 4, 2, cols, LANES), BF16),
            pltpu.VMEM((groups, 2, 2, 2, 2, 2, cols, LANES), BF16),
            pltpu.VMEM((groups, 2, 2, 2, 2, 2, cols, LANES), BF16),
            pltpu.VMEM((4, 32, LANES), F32),
            pltpu.VMEM((2, most, 32, LANES), BF16),
            dma((8,)),
            dma((HALO_COPIES,)),
            dma((HALO_COPIES,)),
            dma((4,)),
            dma((4,)),
            dma((groups, 2, 2)),
            dma((groups, 2, 2)),
            dma((groups, 2, 2)),
            dma((groups, 2, 2)),
            dma((2,)),
            dma((2,)),
            dma((2,)),
            dma((2,)),
        ],
        compiler_params=pltpu.CompilerParams(
            collective_id=0, has_side_effects=True, vmem_limit_bytes=60 * 1024 * 1024
        ),
    )(queries, keys, values, cotangent, conv_weight, block_keep)
    return pl.pallas_call(
        write_out,
        out_shape=(big, big, big, small),
        in_specs=[vmem] * 4,
        out_specs=(hbm,) * 4,
        scratch_shapes=[dma((4,))],
    )(*results)


def solution(mesh):
    in_specs = (
        P("gz", "gy", None, None),
        P("gz", "gy", None, None),
        P("gz", "gy", None, None),
        P("gz", "gy", None, None),
        P(),
        P("gz", "gy", None),
    )
    out_specs = (
        P("gz", "gy", None, None),
        P("gz", "gy", None, None),
        P("gz", "gy", None, None),
        P(),
    )
    return jax.shard_map(
        partial(shards, mesh.shape["gz"], mesh.shape["gy"]),
        mesh=mesh,
        in_specs=in_specs,
        out_specs=out_specs,
        check_vma=False,
    )
```

```python
from functools import partial

import jax
import jax.numpy as jnp
from jax import lax
from jax.experimental import pallas as pl
from jax.experimental.pallas import tpu as pltpu
from jax.sharding import PartitionSpec as P

HEAD = 32
BX = 8
LANES = 128
GROUP_HEADS = LANES // HEAD
DEAD = 4.0
LOG2E = 1.4426950408889634
HALO_COPIES = 24
DIRECT_FIRST = ()
DIRECT_LAST = (1,)
MESH = pl.DeviceIdType.MESH
F32 = jnp.float32
BF16 = jnp.bfloat16
SIDES = ("zm", "zp", "ym", "yp")
CORNERS = (("zm", "ym"), ("zm", "yp"), ("zp", "ym"), ("zp", "yp"))


def rounds_of(sections, rows):
    if sections == 16 and rows == 16:
        return [[("gz", 4, 4), ("gy", 8, 2)], [("gz", 1, 4), ("gy", 2, 4)]]
    return [[("gz", 1, sections)], [("gy", 2, rows // 2)]]


def kernel(
    sections,
    rows_n,
    depth,
    rows,
    cols,
    q_hbm,
    k_hbm,
    v_hbm,
    g_hbm,
    w_hbm,
    keep_hbm,
    gq_ref,
    gk_ref,
    gv_ref,
    cg_ref,
    q_ref,
    g_ref,
    w_ref,
    keep_ref,
    ext,
    near_v,
    acc,
    qm,
    gm,
    shifted,
    filt,
    eights,
    mask,
    part_y,
    got_y,
    part_z,
    got_z,
    got_c,
    halves,
    terms,
    load_sem,
    halo_send,
    halo_recv,
    near_send,
    near_recv,
    py_send,
    py_recv,
    pc_send,
    pc_recv,
    pz_send,
    pz_recv,
    half_send,
    half_recv,
    sum_send,
    sum_recv,
):
    groups = acc.shape[0]
    tokens = depth * rows * cols
    place = {"gz": lax.axis_index("gz"), "gy": lax.axis_index("gy")}
    gz, gy = place["gz"], place["gy"]
    has = {
        "zm": gz > 0,
        "zp": gz < sections - 1,
        "ym": gy > 0,
        "yp": gy < rows_n - 1,
    }
    shift = {"zm": -1, "zp": 1, "ym": -1, "yp": 1}
    core = lax.rem(gy, 2)
    partner = (gz, gy + 1 - 2 * core)
    has["off"] = jnp.logical_or(jnp.logical_and(core == 0, has["ym"]), jnp.logical_and(core == 1, has["yp"]))
    sum_rounds = rounds_of(sections, rows_n)

    def both(names):
        found = True
        for name in names:
            if name != "on":
                found = has[name] if found is True else jnp.logical_and(found, has[name])
        return found

    def when(names):
        found = both(names)
        return (lambda body: body()) if found is True else pl.when(found)

    def device(names):
        to = dict(place)
        for name in names:
            if name in ("on", "off"):
                to["gy"] = to["gy"] + (1 - 2 * core if name == "on" else 2 * core - 1)
            else:
                axis = "g" + name[0]
                to[axis] = to[axis] + shift[name]
        return (to["gz"], to["gy"])

    held = {}

    def digit(spec):
        if spec not in held:
            axis, stride, count = spec
            held[spec] = lax.rem(lax.div(place[axis], stride), count)
        return held[spec]

    def member_of(digits):
        m = 0
        for spec in digits:
            m = m * spec[2] + digit(spec)
        return m

    def peer(digits, moves):
        out = dict(place)
        for spec, move in zip(digits, moves):
            axis, stride, count = spec
            own = digit(spec)
            out[axis] = out[axis] + (lax.rem(own + move, count) - own) * stride
        return (out["gz"], out["gy"])

    def moves_of(digits):
        moves = [()]
        for _, _, count in digits:
            moves = [m + (k,) for m in moves for k in range(count)]
        weight = lambda m: sum(min(k, spec[2] - k) * spec[3] for k, spec in zip(m, hops))
        hops = [spec + (2 if spec[:2] == ("gz", 4) else 1,) for spec in digits]
        return sorted((m for m in moves if any(m)), key=lambda m: (-weight(m), m))

    def size_of(digits):
        n = 1
        for spec in digits:
            n *= spec[2]
        return n

    def load(source, target, sem):
        return pltpu.make_async_copy(source, target, load_sem.at[sem])

    z_own, z_first, z_last = pl.ds(2, depth), pl.ds(0, 2), pl.ds(2 + depth, 2)
    inner, low, high = pl.ds(2, rows), pl.ds(2, 2), pl.ds(rows, 2)
    y_first, y_last = pl.ds(0, 2), pl.ds(2 + rows, 2)
    parts = [slice(g * LANES, (g + 1) * LANES) for g in range(groups)]
    loads = [load(keep_hbm, keep_ref, 0)]
    loads += [load(v_hbm.at[:, :, :, parts[g]], ext.at[g, 1, z_own, inner], 1 + g) for g in range(groups)]
    loads += [load(k_hbm.at[:, :, :, parts[g]], ext.at[g, 0, z_own, inner], 3 + g) for g in range(groups)]
    loads += [load(g_hbm, g_ref, 5), load(q_hbm, q_ref, 6), load(w_hbm, w_ref, 7)]
    for copy in loads[:3]:
        copy.start()

    barrier = pltpu.get_barrier_semaphore()
    expected = 0
    for names in tuple((side,) for side in SIDES) + CORNERS:

        @pl.when(both(names))
        def _(names=names):
            pl.semaphore_signal(barrier, inc=1, device_id=device(names), device_id_type=MESH)

        expected = expected + both(names).astype(jnp.int32)
    for digits in sum_rounds:
        for moves in moves_of(digits):
            pl.semaphore_signal(barrier, inc=1, device_id=peer(digits, moves), device_id_type=MESH)
        expected = expected + (size_of(digits) - 1)
    for copy in loads[3:]:
        copy.start()

    loads[0].wait()
    keep_low = keep_ref[0, 0, 0].astype(F32)
    keep_high = keep_ref[0, 0, 1].astype(F32)
    row_x = lax.broadcasted_iota(jnp.int32, (cols, LANES), 0)
    row_keep = jnp.where(row_x < BX, keep_low, keep_high)
    lane = lax.broadcasted_iota(jnp.int32, (1, LANES), 1)
    lane_x = lane % cols
    lane_keep = jnp.where(lane_x < BX, keep_low, keep_high)
    lane_head = lane // HEAD

    for g in range(groups):
        loads[1 + g].wait()
    pl.semaphore_wait(barrier, expected)

    every = pl.ds(0, groups)
    border = {"zp": 1 + depth, "zm": 2}
    behind = {"zp": 2, "zm": 1 + depth}
    far = {"zp": -depth, "zm": depth}

    def along_z(name, to):
        if name == "near":
            return (every, 1, pl.ds(border[to], 1), inner), (every, 1, pl.ds(border[to] + far[to], 1), inner)
        g = int(name[-1])
        if name[0] == "v":
            return (g, 1, pl.ds(behind[to], 1), inner), (g, 1, pl.ds(behind[to] + far[to], 1), inner)
        return (g, 0, z_own, inner), (g, 0, z_first if to == "zp" else z_last, inner)

    sides = {
        "on": (pl.ds(rows - 2 * core, 2), pl.ds((2 + rows) * core, 2), pl.ds((2 + rows) * (1 - core), 2)),
        "off": (pl.ds(2 + 2 * core, 2), pl.ds((2 + rows) * (1 - core), 2), pl.ds((2 + rows) * core, 2)),
    }
    halo = []
    index = {}
    for name in ["near"] + [kind + str(g) for g in range(groups) for kind in ("v", "k")]:
        for to, source in (("zp", "zm"), ("zm", "zp")):
            src, dst = along_z(name, to)
            index[name, source] = len(halo)
            halo.append(((to,), src, dst, (source,), dst, (to,)))
    for side, (sent, there, here) in sides.items():
        for name, at in [("vy", (every, 1))] + [("ky" + str(g), (g, 0)) for g in range(groups)]:
            index[name, side] = len(halo)
            names = (side,)
            halo.append((names, at + (z_own, sent), at + (z_own, there), names, at + (z_own, here), names))
        for g in range(groups):
            at = (g, pl.ds(0, 2))
            for source, z in (("zm", z_first), ("zp", z_last)):
                index["c", g, side, source] = len(halo)
                names = (side, source)
                if side == "off" and g in DIRECT_FIRST:
                    to = (side, "zp" if source == "zm" else "zm")
                    halo.append((to, at + (z_own, sent), at + (z, there), names, at + (z, here), to))
                else:
                    halo.append((names, at + (z, sent), at + (z, there), names, at + (z, here), (side,)))
    assert len(halo) == HALO_COPIES

    def halo_copy(slot, here=False):
        _, src, dst, _, dst_here, to = halo[slot]
        return pltpu.make_async_remote_copy(
            src_ref=ext.at[src],
            dst_ref=ext.at[dst_here if here else dst],
            send_sem=halo_send.at[slot],
            recv_sem=halo_recv.at[slot],
            device_id=device(to),
            device_id_type=MESH,
        )

    def halo_start(*names):
        for name in names:
            slot = index[name]

            @when(halo[slot][0])
            def _(slot=slot):
                halo_copy(slot).start()

    def halo_got(*names):
        for name in names:
            slot = index[name]

            @when(halo[slot][3])
            def _(slot=slot):
                halo_copy(slot, here=True).wait_recv()

    def halo_sent():
        for slot in range(len(halo)):

            @when(halo[slot][0])
            def _(slot=slot):
                halo_copy(slot).wait_send()

    def near_copy(corner):
        up_z, up_y = CORNERS[corner][0] == "zm", CORNERS[corner][1] == "ym"
        return pltpu.make_async_remote_copy(
            src_ref=ext.at[:, 1, 1 + depth if up_z else 2, 1 + rows if up_y else 2],
            dst_ref=near_v.at[:, 0 if up_z else 1 + depth, 0 if up_y else 1 + rows],
            send_sem=near_send.at[corner],
            recv_sem=near_recv.at[corner],
            device_id=device(("zp" if up_z else "zm", "yp" if up_y else "ym")),
            device_id_type=MESH,
        )

    def opposite(corner):
        return tuple(name[0] + ("p" if name[1] == "m" else "m") for name in CORNERS[corner])

    halo_start(("near", "zm"), ("near", "zp"), ("vy", "off"), ("vy", "on"))
    for corner in range(4):

        @pl.when(both(opposite(corner)))
        def _(corner=corner):
            near_copy(corner).start()

    for g in range(groups):
        loads[3 + g].wait()
        own = ext[g, 0, 2 : 2 + depth, 2 : 2 + rows].astype(F32)
        ext[g, 0, 2 : 2 + depth, 2 : 2 + rows] = jnp.where(row_keep > 0.5, own, DEAD).astype(BF16)

    for g in range(groups):
        for kind in ("v", "k"):
            halo_start((kind + str(g), "zm"), (kind + str(g), "zp"))
        halo_start(("ky" + str(g), "off"), ("ky" + str(g), "on"))
    for g in DIRECT_FIRST:
        halo_start(("c", g, "off", "zm"), ("c", g, "off", "zp"))

    for side, where in (
        ("zm", (z_first,)),
        ("zp", (z_last,)),
        ("ym", (slice(None), y_first)),
        ("yp", (slice(None), y_last)),
    ):

        @pl.when(jnp.logical_not(has[side]))
        def _(side=side, where=where):
            shape = ext[(slice(None), 0) + where].shape
            ext[(slice(None), 0) + where] = jnp.full(shape, DEAD, BF16)
            ext[(slice(None), 1) + where] = jnp.zeros(shape, BF16)
            got = got_z if side[0] == "z" else got_y
            slot = 0 if side[1] == "m" else 1
            got[:, slot] = jnp.zeros(got[:, slot].shape, BF16)

    for corner in range(4):

        @pl.when(jnp.logical_not(both(CORNERS[corner])))
        def _(corner=corner):
            z = 0 if CORNERS[corner][0] == "zm" else 1 + depth
            y = 0 if CORNERS[corner][1] == "ym" else 1 + rows
            near_v[:, z, y] = jnp.zeros((groups, cols, LANES), BF16)

    for copy in loads[5:]:
        copy.wait()
    for o in range(27):
        filt[o] = jnp.broadcast_to(w_ref[o : o + 1].astype(F32), filt.shape[1:])

    def own_row(y):
        for g in range(groups):
            part = parts[g]
            for z in range(depth):
                q_row = q_ref[z, y, :, part].astype(F32)
                g_row = g_ref[z, y, :, part].astype(F32)
                for h in range(GROUP_HEADS):
                    at = pl.ds(((y % 2) * depth * GROUP_HEADS + z * GROUP_HEADS + h) * cols, cols)
                    mine = lane_head == h
                    qm[g, y // 2, at] = jnp.where(mine, q_row, 0.0).astype(BF16)
                    gm[g, y // 2, at] = jnp.where(mine, g_row, 0.0).astype(BF16)
                none = jnp.zeros((1, LANES), F32)
                shifted[g, 0, z, y] = jnp.concatenate([g_row[1:], none], axis=0)
                shifted[g, 1, z, y] = g_row
                shifted[g, 2, z, y] = jnp.concatenate([none, g_row[:-1]], axis=0)

    for y in range(rows):
        own_row(y)
    acc[...] = jnp.zeros(acc.shape, F32)
    eights[27:] = jnp.zeros((5, 8, eights.shape[2]), F32)
    octets = (depth * rows * cols // 8, 8, LANES)
    whole = (depth, rows, cols, LANES)

    def filter_values(i, carry):
        oz, oy = lax.div(i, 3), lax.rem(i, 3)
        for g in range(groups):
            total = acc[g, 1, pl.ds(1 + oz, depth), pl.ds(1 + oy, rows)].reshape(octets)
            for ox in range(3):
                total = total + filt[3 * i + ox, :, parts[g]] * shifted[g, ox].reshape(octets)
            acc[g, 1, pl.ds(1 + oz, depth), pl.ds(1 + oy, rows)] = total.reshape(whole)
        return carry

    band = jnp.abs(row_x - lane_x) <= 2
    half = lax.broadcasted_iota(jnp.int32, (cols, LANES), 1) // (GROUP_HEADS * cols)

    def make_mask(near):
        for z in range(depth + 4):
            reach = band
            for own in range(depth):
                if not own <= z <= own + 4:
                    reach = jnp.logical_and(reach, half != own)
            live = jnp.where(reach, 1.0, 0.0)
            mask[z, near] = jnp.where(ext[0, 0, z, near].astype(F32) < 3.0, live, 0.0)

    scaling = HEAD**-0.5
    keys_n = (depth + 4) * 6 * cols
    head_row = lax.broadcasted_iota(jnp.int32, (2 * depth * GROUP_HEADS * cols, LANES), 0)
    head_row = (head_row // cols) % GROUP_HEADS
    own_head = head_row == lax.broadcasted_iota(jnp.int32, head_row.shape, 1) // HEAD
    nt = (((1,), (1,)), ((), ()))
    tn = (((0,), (0,)), ((), ()))

    def beside(first, second):
        none = jnp.zeros((depth + 4, 1, cols, LANES), first.dtype)
        first = jnp.concatenate([first, none], axis=1)
        second = jnp.concatenate([none, second], axis=1)
        return jnp.concatenate([first, second], axis=-1).reshape(keys_n, 2 * LANES)

    def attend(g, pair):
        y = 2 * pair
        keys = ext[g, 0, :, pl.ds(y, 6)].reshape(keys_n, LANES)
        values = ext[g, 1, :, pl.ds(y, 6)].reshape(keys_n, LANES)
        queries, grads = qm[g, pair], gm[g, pair]
        shape = (depth + 4, 6, cols, 2 * LANES)
        scores = lax.dot_general(keys, queries, nt, preferred_element_type=F32).reshape(shape)
        dprobs = lax.dot_general(values, grads, nt, preferred_element_type=F32).reshape(shape)
        lows, dscores = [], []
        for i in range(2):
            part = slice(i * LANES, (i + 1) * LANES)
            weights = jnp.exp2(scores[:, i : i + 5, :, part] * (scaling * LOG2E)) * mask[:, pl.ds(y + i, 5)]
            totals = jnp.sum(weights, axis=(0, 1, 2), keepdims=True) + (1.0 - lane_keep)
            probs = weights * (lane_keep / totals)
            low = probs.astype(BF16)
            dprob = dprobs[:, i : i + 5, :, part]
            deltas = jnp.sum(low.astype(F32) * dprob, axis=(0, 1, 2), keepdims=True)
            lows.append(low)
            dscores.append((scaling * probs * (dprob - deltas)).astype(BF16))
        low, dscore = beside(*lows), beside(*dscores)
        shape = (depth + 4, 6, cols, LANES)
        acc[g, 1, :, pl.ds(y, 6)] += jnp.dot(low, grads, preferred_element_type=F32).reshape(shape)
        acc[g, 0, :, pl.ds(y, 6)] += jnp.dot(dscore, queries, preferred_element_type=F32).reshape(shape)

        def own_queries():
            dq = lax.dot_general(dscore, keys, tn, preferred_element_type=F32)
            dq = jnp.where(own_head, dq, 0.0).reshape(2, depth, GROUP_HEADS, cols, LANES)
            dq = jnp.sum(dq, axis=2).astype(BF16)
            for i in range(2):
                gq_ref[:, pl.ds(y + i, 1), :, parts[g]] = dq[i][:, None]

        return own_queries

    first, later = pl.ds(0, 4), pl.ds(4, depth)

    def rows_copy(g, side, stage, here=False):
        slot = core if (side == "on") != here else 1 - core
        z = later if stage else first
        return pltpu.make_async_remote_copy(
            src_ref=part_y.at[g, slot, :, z],
            dst_ref=got_y.at[g, slot, :, z],
            send_sem=py_send.at[g, slot, stage],
            recv_sem=py_recv.at[g, slot, stage],
            device_id=device((side,)),
            device_id_type=MESH,
        )

    def send_rows(g, side):
        slot = core if side == "on" else 1 - core
        at = pl.ds((2 + rows) * (1 - slot), 2)
        part_y[g, slot, :, 0:2] = acc[g, :, 0:2, at].astype(BF16)
        part_y[g, slot, :, 2:4] = acc[g, :, 2 + depth : 4 + depth, at].astype(BF16)
        part_y[g, slot, :, 4 : 4 + depth] = acc[g, :, 2 : 2 + depth, at].astype(BF16)

        if side == "off" and g in DIRECT_LAST:
            for place_, to in ((0, "zp"), (1, "zm")):

                @when((side, to))
                def _(place_=place_):
                    corner_copy(g, place_).start()

        @when((side,))
        def _():
            if not (side == "off" and g in DIRECT_LAST):
                rows_copy(g, side, 0).start()
            rows_copy(g, side, 1).start()

    def corner_copy(g, place_, here=False):
        slot = core if here else 1 - core
        return pltpu.make_async_remote_copy(
            src_ref=part_y.at[g, slot, :, pl.ds(2 * (1 - place_), 2)],
            dst_ref=got_c.at[DIRECT_LAST.index(g), place_],
            send_sem=pc_send.at[DIRECT_LAST.index(g), place_],
            recv_sem=pc_recv.at[DIRECT_LAST.index(g), place_],
            device_id=device(("off", "zp" if place_ == 0 else "zm")),
            device_id_type=MESH,
        )

    def got_rows(g, side, stage):
        @when((side,))
        def _():
            rows_copy(g, side, stage, here=True).wait_recv()

    def sections_copy(g, place_, slot):
        return pltpu.make_async_remote_copy(
            src_ref=part_z.at[g, place_, slot],
            dst_ref=got_z.at[g, place_, slot],
            send_sem=pz_send.at[g, place_, slot],
            recv_sem=pz_recv.at[g, place_, slot],
            device_id=device(("zp" if place_ == 0 else "zm",)),
            device_id_type=MESH,
        )

    def send_sections(g, side):
        slot = 1 - core if side == "on" else core
        direct = side == "off" and g in DIRECT_LAST
        if not direct:
            got_rows(g, side, 0)
        near = pl.ds(2 + 2 * slot, 2)
        for place_, z in ((0, 2 + depth), (1, 0)):
            given = acc[g, :, z : z + 2, near]
            if not direct:
                given = given + got_y[g, slot, :, 2 * (1 - place_) : 2 * (2 - place_)].astype(F32)
            part_z[g, place_, slot] = given.astype(BF16)

            @pl.when(has["zp" if place_ == 0 else "zm"])
            def _(place_=place_):
                sections_copy(g, place_, slot).start()

    def finish(g):
        got_rows(g, "on", 1)
        got_rows(g, "off", 1)
        if g in DIRECT_LAST:
            near = pl.ds(2 + 2 * core, 2)
            for place_, source in ((0, "zm"), (1, "zp")):

                @when(("off", source))
                def _(place_=place_):
                    corner_copy(g, place_, here=True).wait_recv()
                    given = got_c[DIRECT_LAST.index(g), place_].astype(F32)
                    acc[g, :, 2 : 2 + depth, near] += given

        for place_, source in ((0, "zm"), (1, "zp")):

            @pl.when(has[source])
            def _(place_=place_):
                for slot in range(2):
                    sections_copy(g, place_, slot).wait_recv()

        for kind, out in ((0, gk_ref), (1, gv_ref)):
            for slot in range(2):
                near = slice(2 + 2 * slot, 4 + 2 * slot)
                total = acc[g, kind, 2 : 2 + depth, near] + got_y[g, slot, kind, 4 : 4 + depth].astype(F32)
                total = total + got_z[g, 0, slot, kind].astype(F32) + got_z[g, 1, slot, kind].astype(F32)
                out[:, 2 * slot : 2 * slot + 2, :, parts[g]] = total.astype(BF16)

    def rows_sent(g):
        for side in ("on", "off"):

            direct = side == "off" and g in DIRECT_LAST
            if direct:
                for place_, to in ((0, "zp"), (1, "zm")):

                    @when((side, to))
                    def _(place_=place_):
                        corner_copy(g, place_).wait_send()

            @when((side,))
            def _(side=side, direct=direct):
                if not direct:
                    rows_copy(g, side, 0).wait_send()
                rows_copy(g, side, 1).wait_send()

    def sections_sent(g):
        for place_, to in ((0, "zp"), (1, "zm")):

            @pl.when(has[to])
            def _(place_=place_):
                for slot in range(2):
                    sections_copy(g, place_, slot).wait_send()

    def filter_terms():
        values = ext.at[:, 1]
        near_v[:, 1 : 1 + depth, 1 : 1 + rows] = values[:, 2 : 2 + depth, 2 : 2 + rows]
        near_v[:, 0, 1 : 1 + rows] = values[:, 1, 2 : 2 + rows]
        near_v[:, 1 + depth, 1 : 1 + rows] = values[:, 2 + depth, 2 : 2 + rows]
        near_v[:, 1 : 1 + depth, 0] = values[:, 2 : 2 + depth, 1]
        near_v[:, 1 : 1 + depth, 1 + rows] = values[:, 2 : 2 + depth, 2 + rows]

        def one(i, carry):
            oz, oy = lax.div(i, 3), lax.rem(i, 3)
            for g in range(groups):
                near = near_v[g, pl.ds(oz, depth), pl.ds(oy, rows)].astype(F32)
                for ox in range(3):
                    product = (near * shifted[g, ox]).reshape(octets)
                    eights[3 * i + ox, :, parts[g]] = jnp.sum(product, axis=0)
            return carry

        lax.fori_loop(0, 9, one, 0)

    def half_copy(stage):
        slot = (1 - core, 2) if stage == 0 else (core, 3)
        return pltpu.make_async_remote_copy(
            src_ref=halves.at[slot[0]],
            dst_ref=halves.at[slot[1]],
            send_sem=half_send.at[stage],
            recv_sem=half_recv.at[stage],
            device_id=partner,
            device_id_type=MESH,
        )

    def sum_begin():
        total = jnp.sum(eights[...], axis=1)
        for g in range(groups):
            halves[g] = total[:, parts[g]]
        half_copy(0).start()

    def sum_copy(r, moves):
        digits = sum_rounds[r]
        me = member_of(digits)
        return pltpu.make_async_remote_copy(
            src_ref=terms.at[r, me],
            dst_ref=terms.at[r, me],
            send_sem=sum_send.at[r],
            recv_sem=sum_recv.at[r],
            device_id=peer(digits, moves),
            device_id_type=MESH,
        )

    def sum_all(r):
        n = size_of(sum_rounds[r])
        return pltpu.make_async_remote_copy(
            src_ref=terms.at[r, pl.ds(0, n - 1)],
            dst_ref=terms.at[r, pl.ds(0, n - 1)],
            send_sem=sum_send.at[r],
            recv_sem=sum_recv.at[r],
            device_id=partner,
            device_id_type=MESH,
        )

    def sum_start(r, total):
        terms[r, member_of(sum_rounds[r])] = total.astype(BF16)
        for moves in moves_of(sum_rounds[r]):
            sum_copy(r, moves).start()

    def sum_first():
        half_copy(0).wait_recv()
        sum_start(0, halves[core] + halves[2])

    def sum_got(r):
        sum_all(r).wait_recv()
        total = terms[r, 0].astype(F32)
        for m in range(1, size_of(sum_rounds[r])):
            total = total + terms[r, m].astype(F32)
        return total

    def sum_second():
        sum_start(1, sum_got(0))

    def sum_third():
        total = sum_got(1) * ((tokens * sections * rows_n) ** -0.5)
        half_copy(0).wait_send()
        halves[core] = total
        half_copy(1).start()

    def sum_last():
        half_copy(1).wait_recv()
        mine, other = halves[core, 0:27], halves[3, 0:27]
        cg_ref[:, parts[0]] = jnp.where(core == 0, mine, other)
        cg_ref[:, parts[1]] = jnp.where(core == 0, other, mine)

    def relay(g):
        for source in ("zm", "zp"):
            halo_got(("v" + str(g), source), ("k" + str(g), source))
            halo_start(*(("c", g, side, source) for side in ("off", "on") if side == "on" or g not in DIRECT_FIRST))

    def arrived(g, side):
        halo_got(("ky" + str(g), side), ("c", g, side, "zm"), ("c", g, side, "zp"))

    lax.fori_loop(0, 9, filter_values, 0)
    halo_got(("near", "zm"), ("near", "zp"), ("vy", "on"), ("vy", "off"))
    for corner in range(4):

        @pl.when(both(CORNERS[corner]))
        def _(corner=corner):
            near_copy(corner).wait_recv()

    filter_terms()
    sum_begin()
    relay(0)
    sum_first()
    relay(1)
    arrived(0, "on")
    make_mask(pl.ds(2 * (1 - core), 6))
    own_queries = attend(0, 1 - core)
    send_rows(0, "on")
    own_queries()
    arrived(0, "off")
    make_mask(pl.ds((2 + rows) * core, 2))
    own_queries = attend(0, core)
    send_rows(0, "off")
    own_queries()
    arrived(1, "on")
    own_queries = attend(1, 1 - core)
    send_rows(1, "on")
    own_queries()
    send_sections(0, "on")
    arrived(1, "off")
    own_queries = attend(1, core)
    send_rows(1, "off")
    send_sections(1, "off")
    own_queries()
    send_sections(1, "on")
    sum_second()
    send_sections(0, "off")
    halo_sent()
    for corner in range(4):

        @pl.when(both(opposite(corner)))
        def _(corner=corner):
            near_copy(corner).wait_send()

    sum_all(0).wait_send()
    for g in range(groups):
        rows_sent(g)
    sum_third()
    sections_sent(0)
    sum_all(1).wait_send()
    finish(0)
    sum_last()
    half_copy(1).wait_send()
    sections_sent(1)
    finish(1)


def write_out(*refs):
    n = len(refs) // 2
    sems = refs[-1]
    copies = [pltpu.make_async_copy(refs[i], refs[n + i], sems.at[i]) for i in range(n)]
    for copy in copies:
        copy.start()
    for copy in copies:
        copy.wait()


def shards(sections, rows_n, queries, keys, values, cotangent, conv_weight, block_keep):
    depth, rows, cols, channels = queries.shape
    groups = channels // LANES
    heads_rows = depth * GROUP_HEADS * cols
    most = max(sections * rows_n // 32, 16)
    big = jax.ShapeDtypeStruct(queries.shape, BF16)
    small = jax.ShapeDtypeStruct(conv_weight.shape, F32)
    vmem = pl.BlockSpec(memory_space=pltpu.VMEM)
    hbm = pl.BlockSpec(memory_space=pltpu.HBM)
    dma = pltpu.SemaphoreType.DMA
    results = pl.pallas_call(
        partial(kernel, sections, rows_n, depth, rows, cols),
        out_shape=(big, big, big, small),
        in_specs=[hbm] * 6,
        out_specs=(vmem,) * 4,
        scratch_shapes=[
            pltpu.VMEM(queries.shape, BF16),
            pltpu.VMEM(queries.shape, BF16),
            pltpu.VMEM(conv_weight.shape, BF16),
            pltpu.SMEM(block_keep.shape, jnp.int32),
            pltpu.VMEM((groups, 2, depth + 4, rows + 4, cols, LANES), BF16),
            pltpu.VMEM((groups, depth + 2, rows + 2, cols, LANES), BF16),
            pltpu.VMEM((groups, 2, depth + 4, rows + 4, cols, LANES), F32),
            pltpu.VMEM((groups, rows // 2, 2 * heads_rows, LANES), BF16),
            pltpu.VMEM((groups, rows // 2, 2 * heads_rows, LANES), BF16),
            pltpu.VMEM((groups, 3, depth, rows, cols, LANES), F32),
            pltpu.VMEM((27, 8, channels), F32),
            pltpu.VMEM((32, 8, channels), F32),
            pltpu.VMEM((depth + 4, rows + 4, cols, LANES), F32),
            pltpu.VMEM((groups, 2, 2, depth + 4, 2, cols, LANES), BF16),
            pltpu.VMEM((groups, 2, 2, depth + 4, 2, cols, LANES), BF16),
            pltpu.VMEM((groups, 2, 2, 2, 2, 2, cols, LANES), BF16),
            pltpu.VMEM((groups, 2, 2, 2, 2, 2, cols, LANES), BF16),
            pltpu.VMEM((groups, 2, 2, depth, 2, cols, LANES), BF16),
            pltpu.VMEM((4, 32, LANES), F32),
            pltpu.VMEM((2, most, 32, LANES), BF16),
            dma((8,)),
            dma((HALO_COPIES,)),
            dma((HALO_COPIES,)),
            dma((4,)),
            dma((4,)),
            dma((groups, 2, 2)),
            dma((groups, 2, 2)),
            dma((groups, 2)),
            dma((groups, 2)),
            dma((groups, 2, 2)),
            dma((groups, 2, 2)),
            dma((2,)),
            dma((2,)),
            dma((2,)),
            dma((2,)),
        ],
        compiler_params=pltpu.CompilerParams(
            collective_id=0, has_side_effects=True, vmem_limit_bytes=60 * 1024 * 1024
        ),
    )(queries, keys, values, cotangent, conv_weight, block_keep)
    return pl.pallas_call(
        write_out,
        out_shape=(big, big, big, small),
        in_specs=[vmem] * 4,
        out_specs=(hbm,) * 4,
        scratch_shapes=[dma((4,))],
    )(*results)


def solution(mesh):
    in_specs = (
        P("gz", "gy", None, None),
        P("gz", "gy", None, None),
        P("gz", "gy", None, None),
        P("gz", "gy", None, None),
        P(),
        P("gz", "gy", None),
    )
    out_specs = (
        P("gz", "gy", None, None),
        P("gz", "gy", None, None),
        P("gz", "gy", None, None),
        P(),
    )
    return jax.shard_map(
        partial(shards, mesh.shape["gz"], mesh.shape["gy"]),
        mesh=mesh,
        in_specs=in_specs,
        out_specs=out_specs,
        check_vma=False,
    )
```

```python
from functools import partial

import jax
import jax.numpy as jnp
from jax import lax
from jax.experimental import pallas as pl
from jax.experimental.pallas import tpu as pltpu
from jax.sharding import PartitionSpec as P

HEAD = 32
BX = 8
LANES = 128
GROUP_HEADS = LANES // HEAD
DEAD = 4.0
LOG2E = 1.4426950408889634
HALO_COPIES = 24
DIRECT_FIRST = ()
DIRECT_LAST = (1,)
MESH = pl.DeviceIdType.MESH
F32 = jnp.float32
BF16 = jnp.bfloat16
SIDES = ("zm", "zp", "ym", "yp")
CORNERS = (("zm", "ym"), ("zm", "yp"), ("zp", "ym"), ("zp", "yp"))


def rounds_of(sections, rows):
    if sections == 16 and rows == 16:
        return [[("gz", 4, 4), ("gy", 8, 2)], [("gz", 1, 4), ("gy", 2, 4)]]
    return [[("gz", 1, sections)], [("gy", 2, rows // 2)]]


def kernel(
    sections,
    rows_n,
    depth,
    rows,
    cols,
    q_hbm,
    k_hbm,
    v_hbm,
    g_hbm,
    w_hbm,
    keep_hbm,
    gq_ref,
    gk_ref,
    gv_ref,
    cg_ref,
    q_ref,
    g_ref,
    w_ref,
    keep_ref,
    ext,
    near_v,
    acc,
    qm,
    gm,
    shifted,
    filt,
    eights,
    mask,
    part_y,
    got_y,
    part_z,
    got_z,
    got_c,
    halves,
    terms,
    load_sem,
    halo_send,
    halo_recv,
    near_send,
    near_recv,
    py_send,
    py_recv,
    pc_send,
    pc_recv,
    pz_send,
    pz_recv,
    half_send,
    half_recv,
    sum_send,
    sum_recv,
):
    groups = acc.shape[0]
    tokens = depth * rows * cols
    place = {"gz": lax.axis_index("gz"), "gy": lax.axis_index("gy")}
    gz, gy = place["gz"], place["gy"]
    has = {
        "zm": gz > 0,
        "zp": gz < sections - 1,
        "ym": gy > 0,
        "yp": gy < rows_n - 1,
    }
    shift = {"zm": -1, "zp": 1, "ym": -1, "yp": 1}
    core = lax.rem(gy, 2)
    partner = (gz, gy + 1 - 2 * core)
    has["off"] = jnp.logical_or(jnp.logical_and(core == 0, has["ym"]), jnp.logical_and(core == 1, has["yp"]))
    sum_rounds = rounds_of(sections, rows_n)

    def both(names):
        found = True
        for name in names:
            if name != "on":
                found = has[name] if found is True else jnp.logical_and(found, has[name])
        return found

    def when(names):
        found = both(names)
        return (lambda body: body()) if found is True else pl.when(found)

    def device(names):
        to = dict(place)
        for name in names:
            if name in ("on", "off"):
                to["gy"] = to["gy"] + (1 - 2 * core if name == "on" else 2 * core - 1)
            else:
                axis = "g" + name[0]
                to[axis] = to[axis] + shift[name]
        return (to["gz"], to["gy"])

    held = {}

    def digit(spec):
        if spec not in held:
            axis, stride, count = spec
            held[spec] = lax.rem(lax.div(place[axis], stride), count)
        return held[spec]

    def member_of(digits):
        m = 0
        for spec in digits:
            m = m * spec[2] + digit(spec)
        return m

    def peer(digits, moves):
        out = dict(place)
        for spec, move in zip(digits, moves):
            axis, stride, count = spec
            own = digit(spec)
            out[axis] = out[axis] + (lax.rem(own + move, count) - own) * stride
        return (out["gz"], out["gy"])

    def moves_of(digits):
        moves = [()]
        for _, _, count in digits:
            moves = [m + (k,) for m in moves for k in range(count)]
        weight = lambda m: sum(min(k, spec[2] - k) * spec[3] for k, spec in zip(m, hops))
        hops = [spec + (2 if spec[:2] == ("gz", 4) else 1,) for spec in digits]
        return sorted((m for m in moves if any(m)), key=lambda m: (-weight(m), m))

    def size_of(digits):
        n = 1
        for spec in digits:
            n *= spec[2]
        return n

    def load(source, target, sem):
        return pltpu.make_async_copy(source, target, load_sem.at[sem])

    z_own, z_first, z_last = pl.ds(2, depth), pl.ds(0, 2), pl.ds(2 + depth, 2)
    inner, low, high = pl.ds(2, rows), pl.ds(2, 2), pl.ds(rows, 2)
    y_first, y_last = pl.ds(0, 2), pl.ds(2 + rows, 2)
    parts = [slice(g * LANES, (g + 1) * LANES) for g in range(groups)]
    loads = [load(keep_hbm, keep_ref, 0)]
    loads += [load(v_hbm.at[:, :, :, parts[g]], ext.at[g, 1, z_own, inner], 1 + g) for g in range(groups)]
    loads += [load(k_hbm.at[:, :, :, parts[g]], ext.at[g, 0, z_own, inner], 3 + g) for g in range(groups)]
    loads += [load(g_hbm, g_ref, 5), load(q_hbm, q_ref, 6), load(w_hbm, w_ref, 7)]
    for copy in loads[:3]:
        copy.start()

    barrier = pltpu.get_barrier_semaphore()
    expected = 0
    for names in tuple((side,) for side in SIDES) + CORNERS:

        @pl.when(both(names))
        def _(names=names):
            pl.semaphore_signal(barrier, inc=1, device_id=device(names), device_id_type=MESH)

        expected = expected + both(names).astype(jnp.int32)
    for digits in sum_rounds:
        for moves in moves_of(digits):
            pl.semaphore_signal(barrier, inc=1, device_id=peer(digits, moves), device_id_type=MESH)
        expected = expected + (size_of(digits) - 1)
    for copy in loads[3:]:
        copy.start()

    loads[0].wait()
    keep_low = keep_ref[0, 0, 0].astype(F32)
    keep_high = keep_ref[0, 0, 1].astype(F32)
    row_x = lax.broadcasted_iota(jnp.int32, (cols, LANES), 0)
    row_keep = jnp.where(row_x < BX, keep_low, keep_high)
    lane = lax.broadcasted_iota(jnp.int32, (1, LANES), 1)
    lane_x = lane % cols
    lane_keep = jnp.where(lane_x < BX, keep_low, keep_high)
    lane_head = lane // HEAD

    for g in range(groups):
        loads[1 + g].wait()
    pl.semaphore_wait(barrier, expected)

    every = pl.ds(0, groups)
    border = {"zp": 1 + depth, "zm": 2}
    behind = {"zp": 2, "zm": 1 + depth}
    far = {"zp": -depth, "zm": depth}

    def along_z(name, to):
        if name == "near":
            return (every, 1, pl.ds(border[to], 1), inner), (every, 1, pl.ds(border[to] + far[to], 1), inner)
        g = int(name[-1])
        if name[0] == "v":
            return (g, 1, pl.ds(behind[to], 1), inner), (g, 1, pl.ds(behind[to] + far[to], 1), inner)
        return (g, 0, z_own, inner), (g, 0, z_first if to == "zp" else z_last, inner)

    sides = {
        "on": (pl.ds(rows - 2 * core, 2), pl.ds((2 + rows) * core, 2), pl.ds((2 + rows) * (1 - core), 2)),
        "off": (pl.ds(2 + 2 * core, 2), pl.ds((2 + rows) * (1 - core), 2), pl.ds((2 + rows) * core, 2)),
    }
    halo = []
    index = {}
    for name in ["near"] + [kind + str(g) for g in range(groups) for kind in ("v", "k")]:
        for to, source in (("zp", "zm"), ("zm", "zp")):
            src, dst = along_z(name, to)
            index[name, source] = len(halo)
            halo.append(((to,), src, dst, (source,), dst, (to,)))
    for side, (sent, there, here) in sides.items():
        for name, at in [("vy", (every, 1))] + [("ky" + str(g), (g, 0)) for g in range(groups)]:
            index[name, side] = len(halo)
            names = (side,)
            halo.append((names, at + (z_own, sent), at + (z_own, there), names, at + (z_own, here), names))
        for g in range(groups):
            at = (g, pl.ds(0, 2))
            for source, z in (("zm", z_first), ("zp", z_last)):
                index["c", g, side, source] = len(halo)
                names = (side, source)
                if side == "off" and g in DIRECT_FIRST:
                    to = (side, "zp" if source == "zm" else "zm")
                    halo.append((to, at + (z_own, sent), at + (z, there), names, at + (z, here), to))
                else:
                    halo.append((names, at + (z, sent), at + (z, there), names, at + (z, here), (side,)))
    assert len(halo) == HALO_COPIES

    def halo_copy(slot, here=False):
        _, src, dst, _, dst_here, to = halo[slot]
        return pltpu.make_async_remote_copy(
            src_ref=ext.at[src],
            dst_ref=ext.at[dst_here if here else dst],
            send_sem=halo_send.at[slot],
            recv_sem=halo_recv.at[slot],
            device_id=device(to),
            device_id_type=MESH,
        )

    def halo_start(*names):
        for name in names:
            slot = index[name]

            @when(halo[slot][0])
            def _(slot=slot):
                halo_copy(slot).start()

    def halo_got(*names):
        for name in names:
            slot = index[name]

            @when(halo[slot][3])
            def _(slot=slot):
                halo_copy(slot, here=True).wait_recv()

    def halo_sent():
        for slot in range(len(halo)):

            @when(halo[slot][0])
            def _(slot=slot):
                halo_copy(slot).wait_send()

    def near_copy(corner):
        up_z, up_y = CORNERS[corner][0] == "zm", CORNERS[corner][1] == "ym"
        return pltpu.make_async_remote_copy(
            src_ref=ext.at[:, 1, 1 + depth if up_z else 2, 1 + rows if up_y else 2],
            dst_ref=near_v.at[:, 0 if up_z else 1 + depth, 0 if up_y else 1 + rows],
            send_sem=near_send.at[corner],
            recv_sem=near_recv.at[corner],
            device_id=device(("zp" if up_z else "zm", "yp" if up_y else "ym")),
            device_id_type=MESH,
        )

    def opposite(corner):
        return tuple(name[0] + ("p" if name[1] == "m" else "m") for name in CORNERS[corner])

    halo_start(("near", "zm"), ("near", "zp"), ("vy", "off"), ("vy", "on"))
    for corner in range(4):

        @pl.when(both(opposite(corner)))
        def _(corner=corner):
            near_copy(corner).start()

    for g in range(groups):
        loads[3 + g].wait()
        own = ext[g, 0, 2 : 2 + depth, 2 : 2 + rows].astype(F32)
        ext[g, 0, 2 : 2 + depth, 2 : 2 + rows] = jnp.where(row_keep > 0.5, own, DEAD).astype(BF16)

    for g in range(groups):
        for kind in ("v", "k"):
            halo_start((kind + str(g), "zm"), (kind + str(g), "zp"))
        halo_start(("ky" + str(g), "off"), ("ky" + str(g), "on"))
    for g in DIRECT_FIRST:
        halo_start(("c", g, "off", "zm"), ("c", g, "off", "zp"))

    for side, where in (
        ("zm", (z_first,)),
        ("zp", (z_last,)),
        ("ym", (slice(None), y_first)),
        ("yp", (slice(None), y_last)),
    ):

        @pl.when(jnp.logical_not(has[side]))
        def _(side=side, where=where):
            shape = ext[(slice(None), 0) + where].shape
            ext[(slice(None), 0) + where] = jnp.full(shape, DEAD, BF16)
            ext[(slice(None), 1) + where] = jnp.zeros(shape, BF16)
            got = got_z if side[0] == "z" else got_y
            slot = 0 if side[1] == "m" else 1
            got[:, slot] = jnp.zeros(got[:, slot].shape, BF16)

    for corner in range(4):

        @pl.when(jnp.logical_not(both(CORNERS[corner])))
        def _(corner=corner):
            z = 0 if CORNERS[corner][0] == "zm" else 1 + depth
            y = 0 if CORNERS[corner][1] == "ym" else 1 + rows
            near_v[:, z, y] = jnp.zeros((groups, cols, LANES), BF16)

    for copy in loads[5:]:
        copy.wait()
    for o in range(27):
        filt[o] = jnp.broadcast_to(w_ref[o : o + 1].astype(F32), filt.shape[1:])

    def own_row(y):
        for g in range(groups):
            part = parts[g]
            for z in range(depth):
                q_row = q_ref[z, y, :, part].astype(F32)
                g_row = g_ref[z, y, :, part].astype(F32)
                for h in range(GROUP_HEADS):
                    at = pl.ds(((y % 2) * depth * GROUP_HEADS + z * GROUP_HEADS + h) * cols, cols)
                    mine = lane_head == h
                    qm[g, y // 2, at] = jnp.where(mine, q_row, 0.0).astype(BF16)
                    gm[g, y // 2, at] = jnp.where(mine, g_row, 0.0).astype(BF16)
                none = jnp.zeros((1, LANES), F32)
                shifted[g, 0, z, y] = jnp.concatenate([g_row[1:], none], axis=0)
                shifted[g, 1, z, y] = g_row
                shifted[g, 2, z, y] = jnp.concatenate([none, g_row[:-1]], axis=0)

    for y in range(rows):
        own_row(y)
    acc[...] = jnp.zeros(acc.shape, F32)
    eights[27:] = jnp.zeros((5, 8, eights.shape[2]), F32)
    octets = (depth * rows * cols // 8, 8, LANES)
    whole = (depth, rows, cols, LANES)

    def filter_values(i, carry):
        oz, oy = lax.div(i, 3), lax.rem(i, 3)
        for g in range(groups):
            total = acc[g, 1, pl.ds(1 + oz, depth), pl.ds(1 + oy, rows)].reshape(octets)
            for ox in range(3):
                total = total + filt[3 * i + ox, :, parts[g]] * shifted[g, ox].reshape(octets)
            acc[g, 1, pl.ds(1 + oz, depth), pl.ds(1 + oy, rows)] = total.reshape(whole)
        return carry

    band = jnp.abs(row_x - lane_x) <= 2
    half = lax.broadcasted_iota(jnp.int32, (cols, LANES), 1) // (GROUP_HEADS * cols)

    def make_mask(near):
        for z in range(depth + 4):
            reach = band
            for own in range(depth):
                if not own <= z <= own + 4:
                    reach = jnp.logical_and(reach, half != own)
            live = jnp.where(reach, 1.0, 0.0)
            mask[z, near] = jnp.where(ext[0, 0, z, near].astype(F32) < 3.0, live, 0.0)

    scaling = HEAD**-0.5
    keys_n = (depth + 4) * 6 * cols
    head_row = lax.broadcasted_iota(jnp.int32, (2 * depth * GROUP_HEADS * cols, LANES), 0)
    head_row = (head_row // cols) % GROUP_HEADS
    own_head = head_row == lax.broadcasted_iota(jnp.int32, head_row.shape, 1) // HEAD
    nt = (((1,), (1,)), ((), ()))
    tn = (((0,), (0,)), ((), ()))

    def beside(first, second):
        none = jnp.zeros((depth + 4, 1, cols, LANES), first.dtype)
        first = jnp.concatenate([first, none], axis=1)
        second = jnp.concatenate([none, second], axis=1)
        return jnp.concatenate([first, second], axis=-1).reshape(keys_n, 2 * LANES)

    def attend(g, pair):
        y = 2 * pair
        keys = ext[g, 0, :, pl.ds(y, 6)].reshape(keys_n, LANES)
        values = ext[g, 1, :, pl.ds(y, 6)].reshape(keys_n, LANES)
        queries, grads = qm[g, pair], gm[g, pair]
        shape = (depth + 4, 6, cols, 2 * LANES)
        scores = lax.dot_general(keys, queries, nt, preferred_element_type=F32).reshape(shape)
        dprobs = lax.dot_general(values, grads, nt, preferred_element_type=F32).reshape(shape)
        lows, dscores = [], []
        for i in range(2):
            part = slice(i * LANES, (i + 1) * LANES)
            weights = jnp.exp2(scores[:, i : i + 5, :, part] * (scaling * LOG2E)) * mask[:, pl.ds(y + i, 5)]
            totals = jnp.sum(weights, axis=(0, 1, 2), keepdims=True) + (1.0 - lane_keep)
            probs = weights * (lane_keep / totals)
            low = probs.astype(BF16)
            dprob = dprobs[:, i : i + 5, :, part]
            deltas = jnp.sum(low.astype(F32) * dprob, axis=(0, 1, 2), keepdims=True)
            lows.append(low)
            dscores.append((scaling * probs * (dprob - deltas)).astype(BF16))
        low, dscore = beside(*lows), beside(*dscores)
        shape = (depth + 4, 6, cols, LANES)
        acc[g, 1, :, pl.ds(y, 6)] += jnp.dot(low, grads, preferred_element_type=F32).reshape(shape)
        acc[g, 0, :, pl.ds(y, 6)] += jnp.dot(dscore, queries, preferred_element_type=F32).reshape(shape)

        def own_queries():
            dq = lax.dot_general(dscore, keys, tn, preferred_element_type=F32)
            dq = jnp.where(own_head, dq, 0.0).reshape(2, depth, GROUP_HEADS, cols, LANES)
            dq = jnp.sum(dq, axis=2).astype(BF16)
            for i in range(2):
                gq_ref[:, pl.ds(y + i, 1), :, parts[g]] = dq[i][:, None]

        return own_queries

    first, later = pl.ds(0, 4), pl.ds(4, depth)

    def rows_copy(g, side, stage, here=False):
        slot = core if (side == "on") != here else 1 - core
        z = later if stage else first
        return pltpu.make_async_remote_copy(
            src_ref=part_y.at[g, slot, :, z],
            dst_ref=got_y.at[g, slot, :, z],
            send_sem=py_send.at[g, slot, stage],
            recv_sem=py_recv.at[g, slot, stage],
            device_id=device((side,)),
            device_id_type=MESH,
        )

    def send_rows(g, side):
        slot = core if side == "on" else 1 - core
        at = pl.ds((2 + rows) * (1 - slot), 2)
        part_y[g, slot, :, 0:2] = acc[g, :, 0:2, at].astype(BF16)
        part_y[g, slot, :, 2:4] = acc[g, :, 2 + depth : 4 + depth, at].astype(BF16)
        part_y[g, slot, :, 4 : 4 + depth] = acc[g, :, 2 : 2 + depth, at].astype(BF16)

        if side == "off" and g in DIRECT_LAST:
            for place_, to in ((0, "zp"), (1, "zm")):

                @when((side, to))
                def _(place_=place_):
                    corner_copy(g, place_).start()

        @when((side,))
        def _():
            if not (side == "off" and g in DIRECT_LAST):
                rows_copy(g, side, 0).start()
            rows_copy(g, side, 1).start()

    def corner_copy(g, place_, here=False):
        slot = core if here else 1 - core
        return pltpu.make_async_remote_copy(
            src_ref=part_y.at[g, slot, :, pl.ds(2 * (1 - place_), 2)],
            dst_ref=got_c.at[DIRECT_LAST.index(g), place_],
            send_sem=pc_send.at[DIRECT_LAST.index(g), place_],
            recv_sem=pc_recv.at[DIRECT_LAST.index(g), place_],
            device_id=device(("off", "zp" if place_ == 0 else "zm")),
            device_id_type=MESH,
        )

    def got_rows(g, side, stage):
        @when((side,))
        def _():
            rows_copy(g, side, stage, here=True).wait_recv()

    def sections_copy(g, place_, slot):
        return pltpu.make_async_remote_copy(
            src_ref=part_z.at[g, place_, slot],
            dst_ref=got_z.at[g, place_, slot],
            send_sem=pz_send.at[g, place_, slot],
            recv_sem=pz_recv.at[g, place_, slot],
            device_id=device(("zp" if place_ == 0 else "zm",)),
            device_id_type=MESH,
        )

    def send_sections(g, side):
        slot = 1 - core if side == "on" else core
        direct = side == "off" and g in DIRECT_LAST
        if not direct:
            got_rows(g, side, 0)
        near = pl.ds(2 + 2 * slot, 2)
        for place_, z in ((0, 2 + depth), (1, 0)):
            given = acc[g, :, z : z + 2, near]
            if not direct:
                given = given + got_y[g, slot, :, 2 * (1 - place_) : 2 * (2 - place_)].astype(F32)
            part_z[g, place_, slot] = given.astype(BF16)

            @pl.when(has["zp" if place_ == 0 else "zm"])
            def _(place_=place_):
                sections_copy(g, place_, slot).start()

    def finish(g):
        got_rows(g, "on", 1)
        got_rows(g, "off", 1)
        if g in DIRECT_LAST:
            near = pl.ds(2 + 2 * core, 2)
            for place_, source in ((0, "zm"), (1, "zp")):

                @when(("off", source))
                def _(place_=place_):
                    corner_copy(g, place_, here=True).wait_recv()
                    given = got_c[DIRECT_LAST.index(g), place_].astype(F32)
                    acc[g, :, 2 : 2 + depth, near] += given

        for place_, source in ((0, "zm"), (1, "zp")):

            @pl.when(has[source])
            def _(place_=place_):
                for slot in range(2):
                    sections_copy(g, place_, slot).wait_recv()

        for kind, out in ((0, gk_ref), (1, gv_ref)):
            for slot in range(2):
                near = slice(2 + 2 * slot, 4 + 2 * slot)
                total = acc[g, kind, 2 : 2 + depth, near] + got_y[g, slot, kind, 4 : 4 + depth].astype(F32)
                total = total + got_z[g, 0, slot, kind].astype(F32) + got_z[g, 1, slot, kind].astype(F32)
                out[:, 2 * slot : 2 * slot + 2, :, parts[g]] = total.astype(BF16)

    def rows_sent(g):
        for side in ("on", "off"):

            direct = side == "off" and g in DIRECT_LAST
            if direct:
                for place_, to in ((0, "zp"), (1, "zm")):

                    @when((side, to))
                    def _(place_=place_):
                        corner_copy(g, place_).wait_send()

            @when((side,))
            def _(side=side, direct=direct):
                if not direct:
                    rows_copy(g, side, 0).wait_send()
                rows_copy(g, side, 1).wait_send()

    def sections_sent(g):
        for place_, to in ((0, "zp"), (1, "zm")):

            @pl.when(has[to])
            def _(place_=place_):
                for slot in range(2):
                    sections_copy(g, place_, slot).wait_send()

    def filter_terms():
        values = ext.at[:, 1]
        near_v[:, 1 : 1 + depth, 1 : 1 + rows] = values[:, 2 : 2 + depth, 2 : 2 + rows]
        near_v[:, 0, 1 : 1 + rows] = values[:, 1, 2 : 2 + rows]
        near_v[:, 1 + depth, 1 : 1 + rows] = values[:, 2 + depth, 2 : 2 + rows]
        near_v[:, 1 : 1 + depth, 0] = values[:, 2 : 2 + depth, 1]
        near_v[:, 1 : 1 + depth, 1 + rows] = values[:, 2 : 2 + depth, 2 + rows]

        def one(i, carry):
            oz, oy = lax.div(i, 3), lax.rem(i, 3)
            for g in range(groups):
                near = near_v[g, pl.ds(oz, depth), pl.ds(oy, rows)].astype(F32)
                for ox in range(3):
                    product = (near * shifted[g, ox]).reshape(octets)
                    eights[3 * i + ox, :, parts[g]] = jnp.sum(product, axis=0)
            return carry

        lax.fori_loop(0, 9, one, 0)

    def half_copy(stage):
        slot = (1 - core, 2) if stage == 0 else (core, 3)
        return pltpu.make_async_remote_copy(
            src_ref=halves.at[slot[0]],
            dst_ref=halves.at[slot[1]],
            send_sem=half_send.at[stage],
            recv_sem=half_recv.at[stage],
            device_id=partner,
            device_id_type=MESH,
        )

    def sum_begin():
        total = jnp.sum(eights[...], axis=1)
        for g in range(groups):
            halves[g] = total[:, parts[g]]
        half_copy(0).start()

    def sum_copy(r, moves):
        digits = sum_rounds[r]
        me = member_of(digits)
        return pltpu.make_async_remote_copy(
            src_ref=terms.at[r, me],
            dst_ref=terms.at[r, me],
            send_sem=sum_send.at[r],
            recv_sem=sum_recv.at[r],
            device_id=peer(digits, moves),
            device_id_type=MESH,
        )

    def sum_all(r):
        n = size_of(sum_rounds[r])
        return pltpu.make_async_remote_copy(
            src_ref=terms.at[r, pl.ds(0, n - 1)],
            dst_ref=terms.at[r, pl.ds(0, n - 1)],
            send_sem=sum_send.at[r],
            recv_sem=sum_recv.at[r],
            device_id=partner,
            device_id_type=MESH,
        )

    def sum_start(r, total):
        terms[r, member_of(sum_rounds[r])] = total.astype(BF16)
        for moves in moves_of(sum_rounds[r]):
            sum_copy(r, moves).start()

    def sum_first():
        half_copy(0).wait_recv()
        sum_start(0, halves[core] + halves[2])

    def sum_got(r):
        sum_all(r).wait_recv()
        total = terms[r, 0].astype(F32)
        for m in range(1, size_of(sum_rounds[r])):
            total = total + terms[r, m].astype(F32)
        return total

    def sum_second():
        sum_start(1, sum_got(0))

    def sum_third():
        total = sum_got(1) * ((tokens * sections * rows_n) ** -0.5)
        half_copy(0).wait_send()
        halves[core] = total
        half_copy(1).start()

    def sum_last():
        half_copy(1).wait_recv()
        mine, other = halves[core, 0:27], halves[3, 0:27]
        cg_ref[:, parts[0]] = jnp.where(core == 0, mine, other)
        cg_ref[:, parts[1]] = jnp.where(core == 0, other, mine)

    def relay(g):
        for source in ("zm", "zp"):
            halo_got(("v" + str(g), source), ("k" + str(g), source))
            halo_start(*(("c", g, side, source) for side in ("off", "on") if side == "on" or g not in DIRECT_FIRST))

    def arrived(g, side):
        halo_got(("ky" + str(g), side), ("c", g, side, "zm"), ("c", g, side, "zp"))

    lax.fori_loop(0, 9, filter_values, 0)
    halo_got(("near", "zm"), ("near", "zp"), ("vy", "on"), ("vy", "off"))
    for corner in range(4):

        @pl.when(both(CORNERS[corner]))
        def _(corner=corner):
            near_copy(corner).wait_recv()

    filter_terms()
    sum_begin()
    relay(0)
    sum_first()
    relay(1)
    arrived(0, "on")
    make_mask(pl.ds(2 * (1 - core), 6))
    own_queries = attend(0, 1 - core)
    send_rows(0, "on")
    own_queries()
    arrived(0, "off")
    make_mask(pl.ds((2 + rows) * core, 2))
    own_queries = attend(0, core)
    send_rows(0, "off")
    own_queries()
    arrived(1, "on")
    own_queries = attend(1, 1 - core)
    send_rows(1, "on")
    own_queries()
    send_sections(0, "on")
    arrived(1, "off")
    own_queries = attend(1, core)
    send_sections(1, "off")
    send_rows(1, "off")
    send_sections(1, "on")
    sum_second()
    own_queries()
    send_sections(0, "off")
    halo_sent()
    for corner in range(4):

        @pl.when(both(opposite(corner)))
        def _(corner=corner):
            near_copy(corner).wait_send()

    sum_all(0).wait_send()
    for g in range(groups):
        rows_sent(g)
    sum_third()
    sections_sent(0)
    sum_all(1).wait_send()
    finish(0)
    sum_last()
    half_copy(1).wait_send()
    sections_sent(1)
    finish(1)


def write_out(*refs):
    n = len(refs) // 2
    sems = refs[-1]
    copies = [pltpu.make_async_copy(refs[i], refs[n + i], sems.at[i]) for i in range(n)]
    for copy in copies:
        copy.start()
    for copy in copies:
        copy.wait()


def shards(sections, rows_n, queries, keys, values, cotangent, conv_weight, block_keep):
    depth, rows, cols, channels = queries.shape
    groups = channels // LANES
    heads_rows = depth * GROUP_HEADS * cols
    most = max(sections * rows_n // 32, 16)
    big = jax.ShapeDtypeStruct(queries.shape, BF16)
    small = jax.ShapeDtypeStruct(conv_weight.shape, F32)
    vmem = pl.BlockSpec(memory_space=pltpu.VMEM)
    hbm = pl.BlockSpec(memory_space=pltpu.HBM)
    dma = pltpu.SemaphoreType.DMA
    arguments = (queries, keys, values, cotangent, conv_weight, block_keep)
    results = pl.pallas_call(
        partial(kernel, sections, rows_n, depth, rows, cols),
        out_shape=(big, big, big, small),
        in_specs=[hbm] * 6,
        out_specs=(vmem,) * 4,
        scratch_shapes=[
            pltpu.VMEM(queries.shape, BF16),
            pltpu.VMEM(queries.shape, BF16),
            pltpu.VMEM(conv_weight.shape, BF16),
            pltpu.SMEM(block_keep.shape, jnp.int32),
            pltpu.VMEM((groups, 2, depth + 4, rows + 4, cols, LANES), BF16),
            pltpu.VMEM((groups, depth + 2, rows + 2, cols, LANES), BF16),
            pltpu.VMEM((groups, 2, depth + 4, rows + 4, cols, LANES), F32),
            pltpu.VMEM((groups, rows // 2, 2 * heads_rows, LANES), BF16),
            pltpu.VMEM((groups, rows // 2, 2 * heads_rows, LANES), BF16),
            pltpu.VMEM((groups, 3, depth, rows, cols, LANES), F32),
            pltpu.VMEM((27, 8, channels), F32),
            pltpu.VMEM((32, 8, channels), F32),
            pltpu.VMEM((depth + 4, rows + 4, cols, LANES), F32),
            pltpu.VMEM((groups, 2, 2, depth + 4, 2, cols, LANES), BF16),
            pltpu.VMEM((groups, 2, 2, depth + 4, 2, cols, LANES), BF16),
            pltpu.VMEM((groups, 2, 2, 2, 2, 2, cols, LANES), BF16),
            pltpu.VMEM((groups, 2, 2, 2, 2, 2, cols, LANES), BF16),
            pltpu.VMEM((groups, 2, 2, depth, 2, cols, LANES), BF16),
            pltpu.VMEM((4, 32, LANES), F32),
            pltpu.VMEM((2, most, 32, LANES), BF16),
            dma((8,)),
            dma((HALO_COPIES,)),
            dma((HALO_COPIES,)),
            dma((4,)),
            dma((4,)),
            dma((groups, 2, 2)),
            dma((groups, 2, 2)),
            dma((groups, 2)),
            dma((groups, 2)),
            dma((groups, 2, 2)),
            dma((groups, 2, 2)),
            dma((2,)),
            dma((2,)),
            dma((2,)),
            dma((2,)),
        ],
        compiler_params=pltpu.CompilerParams(
            collective_id=0, has_side_effects=True, vmem_limit_bytes=16 * 1024 * 1024
        ),
    )(*(pltpu.with_memory_space_constraint(x, pltpu.HBM) for x in arguments))
    return pl.pallas_call(
        write_out,
        out_shape=(big, big, big, small),
        in_specs=[vmem] * 4,
        out_specs=(hbm,) * 4,
        scratch_shapes=[dma((4,))],
        compiler_params=pltpu.CompilerParams(vmem_limit_bytes=1024 * 1024),
    )(*results)


def solution(mesh):
    in_specs = (
        P("gz", "gy", None, None),
        P("gz", "gy", None, None),
        P("gz", "gy", None, None),
        P("gz", "gy", None, None),
        P(),
        P("gz", "gy", None),
    )
    out_specs = (
        P("gz", "gy", None, None),
        P("gz", "gy", None, None),
        P("gz", "gy", None, None),
        P(),
    )
    return jax.shard_map(
        partial(shards, mesh.shape["gz"], mesh.shape["gy"]),
        mesh=mesh,
        in_specs=in_specs,
        out_specs=out_specs,
        check_vma=False,
    )
```

```python
from functools import partial

import jax
import jax.numpy as jnp
from jax import lax
from jax.experimental import pallas as pl
from jax.experimental.pallas import tpu as pltpu
from jax.sharding import PartitionSpec as P

HEAD = 32
BX = 8
LANES = 128
GROUP_HEADS = LANES // HEAD
DEAD = 4.0
LOG2E = 1.4426950408889634
HALO_COPIES = 24
DIRECT_FIRST = ()
DIRECT_LAST = (1,)
MESH = pl.DeviceIdType.MESH
F32 = jnp.float32
BF16 = jnp.bfloat16
SIDES = ("zm", "zp", "ym", "yp")
CORNERS = (("zm", "ym"), ("zm", "yp"), ("zp", "ym"), ("zp", "yp"))


def rounds_of(sections, rows):
    if sections == 16 and rows == 16:
        return [[("gz", 4, 4), ("gy", 8, 2)], [("gz", 1, 4), ("gy", 2, 4)]]
    return [[("gz", 1, sections)], [("gy", 2, rows // 2)]]


def kernel(
    sections,
    rows_n,
    depth,
    rows,
    cols,
    q_hbm,
    k_hbm,
    v_hbm,
    g_hbm,
    w_hbm,
    keep_hbm,
    gq_ref,
    gk_ref,
    gv_ref,
    cg_ref,
    q_ref,
    g_ref,
    w_ref,
    keep_ref,
    ext,
    near_v,
    acc,
    qm,
    gm,
    shifted,
    filt,
    eights,
    mask,
    part_y,
    got_y,
    part_z,
    got_z,
    got_c,
    halves,
    terms,
    load_sem,
    halo_send,
    halo_recv,
    near_send,
    near_recv,
    py_send,
    py_recv,
    pc_send,
    pc_recv,
    pz_send,
    pz_recv,
    half_send,
    half_recv,
    sum_send,
    sum_recv,
):
    groups = acc.shape[0]
    tokens = depth * rows * cols
    place = {"gz": lax.axis_index("gz"), "gy": lax.axis_index("gy")}
    gz, gy = place["gz"], place["gy"]
    has = {
        "zm": gz > 0,
        "zp": gz < sections - 1,
        "ym": gy > 0,
        "yp": gy < rows_n - 1,
    }
    shift = {"zm": -1, "zp": 1, "ym": -1, "yp": 1}
    core = lax.rem(gy, 2)
    partner = (gz, gy + 1 - 2 * core)
    has["off"] = jnp.logical_or(jnp.logical_and(core == 0, has["ym"]), jnp.logical_and(core == 1, has["yp"]))
    sum_rounds = rounds_of(sections, rows_n)

    def both(names):
        found = True
        for name in names:
            if name != "on":
                found = has[name] if found is True else jnp.logical_and(found, has[name])
        return found

    def when(names):
        found = both(names)
        return (lambda body: body()) if found is True else pl.when(found)

    def device(names):
        to = dict(place)
        for name in names:
            if name in ("on", "off"):
                to["gy"] = to["gy"] + (1 - 2 * core if name == "on" else 2 * core - 1)
            else:
                axis = "g" + name[0]
                to[axis] = to[axis] + shift[name]
        return (to["gz"], to["gy"])

    held = {}

    def digit(spec):
        if spec not in held:
            axis, stride, count = spec
            held[spec] = lax.rem(lax.div(place[axis], stride), count)
        return held[spec]

    def member_of(digits):
        m = 0
        for spec in digits:
            m = m * spec[2] + digit(spec)
        return m

    def peer(digits, moves):
        out = dict(place)
        for spec, move in zip(digits, moves):
            axis, stride, count = spec
            own = digit(spec)
            out[axis] = out[axis] + (lax.rem(own + move, count) - own) * stride
        return (out["gz"], out["gy"])

    def moves_of(digits):
        moves = [()]
        for _, _, count in digits:
            moves = [m + (k,) for m in moves for k in range(count)]
        weight = lambda m: sum(min(k, spec[2] - k) * spec[3] for k, spec in zip(m, hops))
        hops = [spec + (2 if spec[:2] == ("gz", 4) else 1,) for spec in digits]
        return sorted((m for m in moves if any(m)), key=lambda m: (-weight(m), m))

    def size_of(digits):
        n = 1
        for spec in digits:
            n *= spec[2]
        return n

    def load(source, target, sem):
        return pltpu.make_async_copy(source, target, load_sem.at[sem])

    z_own, z_first, z_last = pl.ds(2, depth), pl.ds(0, 2), pl.ds(2 + depth, 2)
    inner, low, high = pl.ds(2, rows), pl.ds(2, 2), pl.ds(rows, 2)
    y_first, y_last = pl.ds(0, 2), pl.ds(2 + rows, 2)
    parts = [slice(g * LANES, (g + 1) * LANES) for g in range(groups)]
    loads = [load(keep_hbm, keep_ref, 0)]
    loads += [load(v_hbm.at[:, :, :, parts[g]], ext.at[g, 1, z_own, inner], 1 + g) for g in range(groups)]
    loads += [load(k_hbm.at[:, :, :, parts[g]], ext.at[g, 0, z_own, inner], 3 + g) for g in range(groups)]
    loads += [load(g_hbm, g_ref, 5), load(q_hbm, q_ref, 6), load(w_hbm, w_ref, 7)]
    for copy in loads[:5]:
        copy.start()

    barrier = pltpu.get_barrier_semaphore()
    expected = 0
    for names in tuple((side,) for side in SIDES) + CORNERS:

        @pl.when(both(names))
        def _(names=names):
            pl.semaphore_signal(barrier, inc=1, device_id=device(names), device_id_type=MESH)

        expected = expected + both(names).astype(jnp.int32)
    for digits in sum_rounds:
        for moves in moves_of(digits):
            pl.semaphore_signal(barrier, inc=1, device_id=peer(digits, moves), device_id_type=MESH)
        expected = expected + (size_of(digits) - 1)
    for copy in loads[5:]:
        copy.start()

    loads[0].wait()
    keep_low = keep_ref[0, 0, 0].astype(F32)
    keep_high = keep_ref[0, 0, 1].astype(F32)
    row_x = lax.broadcasted_iota(jnp.int32, (cols, LANES), 0)
    row_keep = jnp.where(row_x < BX, keep_low, keep_high)
    lane = lax.broadcasted_iota(jnp.int32, (1, LANES), 1)
    lane_x = lane % cols
    lane_keep = jnp.where(lane_x < BX, keep_low, keep_high)
    lane_head = lane // HEAD

    for g in range(groups):
        loads[1 + g].wait()
    pl.semaphore_wait(barrier, expected)

    every = pl.ds(0, groups)
    border = {"zp": 1 + depth, "zm": 2}
    behind = {"zp": 2, "zm": 1 + depth}
    far = {"zp": -depth, "zm": depth}

    def along_z(name, to):
        if name == "near":
            return (every, 1, pl.ds(border[to], 1), inner), (every, 1, pl.ds(border[to] + far[to], 1), inner)
        g = int(name[-1])
        if name[0] == "v":
            return (g, 1, pl.ds(behind[to], 1), inner), (g, 1, pl.ds(behind[to] + far[to], 1), inner)
        return (g, 0, z_own, inner), (g, 0, z_first if to == "zp" else z_last, inner)

    sides = {
        "on": (pl.ds(rows - 2 * core, 2), pl.ds((2 + rows) * core, 2), pl.ds((2 + rows) * (1 - core), 2)),
        "off": (pl.ds(2 + 2 * core, 2), pl.ds((2 + rows) * (1 - core), 2), pl.ds((2 + rows) * core, 2)),
    }
    halo = []
    index = {}
    for name in ["near"] + [kind + str(g) for g in range(groups) for kind in ("v", "k")]:
        for to, source in (("zp", "zm"), ("zm", "zp")):
            src, dst = along_z(name, to)
            index[name, source] = len(halo)
            halo.append(((to,), src, dst, (source,), dst, (to,)))
    for side, (sent, there, here) in sides.items():
        for name, at in [("vy", (every, 1))] + [("ky" + str(g), (g, 0)) for g in range(groups)]:
            index[name, side] = len(halo)
            names = (side,)
            halo.append((names, at + (z_own, sent), at + (z_own, there), names, at + (z_own, here), names))
        for g in range(groups):
            at = (g, pl.ds(0, 2))
            for source, z in (("zm", z_first), ("zp", z_last)):
                index["c", g, side, source] = len(halo)
                names = (side, source)
                if side == "off" and g in DIRECT_FIRST:
                    to = (side, "zp" if source == "zm" else "zm")
                    halo.append((to, at + (z_own, sent), at + (z, there), names, at + (z, here), to))
                else:
                    halo.append((names, at + (z, sent), at + (z, there), names, at + (z, here), (side,)))
    assert len(halo) == HALO_COPIES

    def halo_copy(slot, here=False):
        _, src, dst, _, dst_here, to = halo[slot]
        return pltpu.make_async_remote_copy(
            src_ref=ext.at[src],
            dst_ref=ext.at[dst_here if here else dst],
            send_sem=halo_send.at[slot],
            recv_sem=halo_recv.at[slot],
            device_id=device(to),
            device_id_type=MESH,
        )

    def halo_start(*names):
        for name in names:
            slot = index[name]

            @when(halo[slot][0])
            def _(slot=slot):
                halo_copy(slot).start()

    def halo_got(*names):
        for name in names:
            slot = index[name]

            @when(halo[slot][3])
            def _(slot=slot):
                halo_copy(slot, here=True).wait_recv()

    def halo_sent():
        for slot in range(len(halo)):

            @when(halo[slot][0])
            def _(slot=slot):
                halo_copy(slot).wait_send()

    def near_copy(corner):
        up_z, up_y = CORNERS[corner][0] == "zm", CORNERS[corner][1] == "ym"
        return pltpu.make_async_remote_copy(
            src_ref=ext.at[:, 1, 1 + depth if up_z else 2, 1 + rows if up_y else 2],
            dst_ref=near_v.at[:, 0 if up_z else 1 + depth, 0 if up_y else 1 + rows],
            send_sem=near_send.at[corner],
            recv_sem=near_recv.at[corner],
            device_id=device(("zp" if up_z else "zm", "yp" if up_y else "ym")),
            device_id_type=MESH,
        )

    def opposite(corner):
        return tuple(name[0] + ("p" if name[1] == "m" else "m") for name in CORNERS[corner])

    halo_start(("near", "zm"), ("near", "zp"), ("vy", "off"), ("vy", "on"))
    for corner in range(4):

        @pl.when(both(opposite(corner)))
        def _(corner=corner):
            near_copy(corner).start()

    for g in range(groups):
        loads[3 + g].wait()
        own = ext[g, 0, 2 : 2 + depth, 2 : 2 + rows].astype(F32)
        ext[g, 0, 2 : 2 + depth, 2 : 2 + rows] = jnp.where(row_keep > 0.5, own, DEAD).astype(BF16)

    for g in range(groups):
        for kind in ("v", "k"):
            halo_start((kind + str(g), "zm"), (kind + str(g), "zp"))
        halo_start(("ky" + str(g), "off"), ("ky" + str(g), "on"))
    for g in DIRECT_FIRST:
        halo_start(("c", g, "off", "zm"), ("c", g, "off", "zp"))

    for side, where in (
        ("zm", (z_first,)),
        ("zp", (z_last,)),
        ("ym", (slice(None), y_first)),
        ("yp", (slice(None), y_last)),
    ):

        @pl.when(jnp.logical_not(has[side]))
        def _(side=side, where=where):
            shape = ext[(slice(None), 0) + where].shape
            ext[(slice(None), 0) + where] = jnp.full(shape, DEAD, BF16)
            ext[(slice(None), 1) + where] = jnp.zeros(shape, BF16)
            got = got_z if side[0] == "z" else got_y
            slot = 0 if side[1] == "m" else 1
            got[:, slot] = jnp.zeros(got[:, slot].shape, BF16)

    for corner in range(4):

        @pl.when(jnp.logical_not(both(CORNERS[corner])))
        def _(corner=corner):
            z = 0 if CORNERS[corner][0] == "zm" else 1 + depth
            y = 0 if CORNERS[corner][1] == "ym" else 1 + rows
            near_v[:, z, y] = jnp.zeros((groups, cols, LANES), BF16)

    for copy in loads[5:]:
        copy.wait()
    for o in range(27):
        filt[o] = jnp.broadcast_to(w_ref[o : o + 1].astype(F32), filt.shape[1:])

    def own_row(y):
        for g in range(groups):
            part = parts[g]
            for z in range(depth):
                q_row = q_ref[z, y, :, part].astype(F32)
                g_row = g_ref[z, y, :, part].astype(F32)
                for h in range(GROUP_HEADS):
                    at = pl.ds(((y % 2) * depth * GROUP_HEADS + z * GROUP_HEADS + h) * cols, cols)
                    mine = lane_head == h
                    qm[g, y // 2, at] = jnp.where(mine, q_row, 0.0).astype(BF16)
                    gm[g, y // 2, at] = jnp.where(mine, g_row, 0.0).astype(BF16)
                none = jnp.zeros((1, LANES), F32)
                shifted[g, 0, z, y] = jnp.concatenate([g_row[1:], none], axis=0)
                shifted[g, 1, z, y] = g_row
                shifted[g, 2, z, y] = jnp.concatenate([none, g_row[:-1]], axis=0)

    for y in range(rows):
        own_row(y)
    acc[...] = jnp.zeros(acc.shape, F32)
    eights[27:] = jnp.zeros((5, 8, eights.shape[2]), F32)
    octets = (depth * rows * cols // 8, 8, LANES)
    whole = (depth, rows, cols, LANES)

    def filter_values(i, carry):
        oz, oy = lax.div(i, 3), lax.rem(i, 3)
        for g in range(groups):
            total = acc[g, 1, pl.ds(1 + oz, depth), pl.ds(1 + oy, rows)].reshape(octets)
            for ox in range(3):
                total = total + filt[3 * i + ox, :, parts[g]] * shifted[g, ox].reshape(octets)
            acc[g, 1, pl.ds(1 + oz, depth), pl.ds(1 + oy, rows)] = total.reshape(whole)
        return carry

    band = jnp.abs(row_x - lane_x) <= 2
    half = lax.broadcasted_iota(jnp.int32, (cols, LANES), 1) // (GROUP_HEADS * cols)

    def make_mask(near):
        for z in range(depth + 4):
            reach = band
            for own in range(depth):
                if not own <= z <= own + 4:
                    reach = jnp.logical_and(reach, half != own)
            live = jnp.where(reach, 1.0, 0.0)
            mask[z, near] = jnp.where(ext[0, 0, z, near].astype(F32) < 3.0, live, 0.0)

    scaling = HEAD**-0.5
    keys_n = (depth + 4) * 6 * cols
    head_row = lax.broadcasted_iota(jnp.int32, (2 * depth * GROUP_HEADS * cols, LANES), 0)
    head_row = (head_row // cols) % GROUP_HEADS
    own_head = head_row == lax.broadcasted_iota(jnp.int32, head_row.shape, 1) // HEAD
    nt = (((1,), (1,)), ((), ()))
    tn = (((0,), (0,)), ((), ()))

    def beside(first, second):
        none = jnp.zeros((depth + 4, 1, cols, LANES), first.dtype)
        first = jnp.concatenate([first, none], axis=1)
        second = jnp.concatenate([none, second], axis=1)
        return jnp.concatenate([first, second], axis=-1).reshape(keys_n, 2 * LANES)

    def attend(g, pair):
        y = 2 * pair
        keys = ext[g, 0, :, pl.ds(y, 6)].reshape(keys_n, LANES)
        values = ext[g, 1, :, pl.ds(y, 6)].reshape(keys_n, LANES)
        queries, grads = qm[g, pair], gm[g, pair]
        shape = (depth + 4, 6, cols, 2 * LANES)
        scores = lax.dot_general(keys, queries, nt, preferred_element_type=F32).reshape(shape)
        dprobs = lax.dot_general(values, grads, nt, preferred_element_type=F32).reshape(shape)
        lows, dscores = [], []
        for i in range(2):
            part = slice(i * LANES, (i + 1) * LANES)
            weights = jnp.exp2(scores[:, i : i + 5, :, part] * (scaling * LOG2E)) * mask[:, pl.ds(y + i, 5)]
            totals = jnp.sum(weights, axis=(0, 1, 2), keepdims=True) + (1.0 - lane_keep)
            probs = weights * (lane_keep / totals)
            low = probs.astype(BF16)
            dprob = dprobs[:, i : i + 5, :, part]
            deltas = jnp.sum(low.astype(F32) * dprob, axis=(0, 1, 2), keepdims=True)
            lows.append(low)
            dscores.append((scaling * probs * (dprob - deltas)).astype(BF16))
        low, dscore = beside(*lows), beside(*dscores)
        shape = (depth + 4, 6, cols, LANES)
        acc[g, 1, :, pl.ds(y, 6)] += jnp.dot(low, grads, preferred_element_type=F32).reshape(shape)
        acc[g, 0, :, pl.ds(y, 6)] += jnp.dot(dscore, queries, preferred_element_type=F32).reshape(shape)

        def own_queries():
            dq = lax.dot_general(dscore, keys, tn, preferred_element_type=F32)
            dq = jnp.where(own_head, dq, 0.0).reshape(2, depth, GROUP_HEADS, cols, LANES)
            dq = jnp.sum(dq, axis=2).astype(BF16)
            for i in range(2):
                gq_ref[:, pl.ds(y + i, 1), :, parts[g]] = dq[i][:, None]

        return own_queries

    first, later = pl.ds(0, 4), pl.ds(4, depth)

    def rows_copy(g, side, stage, here=False):
        slot = core if (side == "on") != here else 1 - core
        z = later if stage else first
        return pltpu.make_async_remote_copy(
            src_ref=part_y.at[g, slot, :, z],
            dst_ref=got_y.at[g, slot, :, z],
            send_sem=py_send.at[g, slot, stage],
            recv_sem=py_recv.at[g, slot, stage],
            device_id=device((side,)),
            device_id_type=MESH,
        )

    def send_rows(g, side):
        slot = core if side == "on" else 1 - core
        at = pl.ds((2 + rows) * (1 - slot), 2)
        part_y[g, slot, :, 0:2] = acc[g, :, 0:2, at].astype(BF16)
        part_y[g, slot, :, 2:4] = acc[g, :, 2 + depth : 4 + depth, at].astype(BF16)
        part_y[g, slot, :, 4 : 4 + depth] = acc[g, :, 2 : 2 + depth, at].astype(BF16)

        if side == "off" and g in DIRECT_LAST:
            for place_, to in ((0, "zp"), (1, "zm")):

                @when((side, to))
                def _(place_=place_):
                    corner_copy(g, place_).start()

        @when((side,))
        def _():
            if not (side == "off" and g in DIRECT_LAST):
                rows_copy(g, side, 0).start()
            rows_copy(g, side, 1).start()

    def corner_copy(g, place_, here=False):
        slot = core if here else 1 - core
        return pltpu.make_async_remote_copy(
            src_ref=part_y.at[g, slot, :, pl.ds(2 * (1 - place_), 2)],
            dst_ref=got_c.at[DIRECT_LAST.index(g), place_],
            send_sem=pc_send.at[DIRECT_LAST.index(g), place_],
            recv_sem=pc_recv.at[DIRECT_LAST.index(g), place_],
            device_id=device(("off", "zp" if place_ == 0 else "zm")),
            device_id_type=MESH,
        )

    def got_rows(g, side, stage):
        @when((side,))
        def _():
            rows_copy(g, side, stage, here=True).wait_recv()

    def sections_copy(g, place_, slot):
        return pltpu.make_async_remote_copy(
            src_ref=part_z.at[g, place_, slot],
            dst_ref=got_z.at[g, place_, slot],
            send_sem=pz_send.at[g, place_, slot],
            recv_sem=pz_recv.at[g, place_, slot],
            device_id=device(("zp" if place_ == 0 else "zm",)),
            device_id_type=MESH,
        )

    def send_sections(g, side):
        slot = 1 - core if side == "on" else core
        direct = side == "off" and g in DIRECT_LAST
        if not direct:
            got_rows(g, side, 0)
        near = pl.ds(2 + 2 * slot, 2)
        for place_, z in ((0, 2 + depth), (1, 0)):
            given = acc[g, :, z : z + 2, near]
            if not direct:
                given = given + got_y[g, slot, :, 2 * (1 - place_) : 2 * (2 - place_)].astype(F32)
            part_z[g, place_, slot] = given.astype(BF16)

            @pl.when(has["zp" if place_ == 0 else "zm"])
            def _(place_=place_):
                sections_copy(g, place_, slot).start()

    def finish(g):
        got_rows(g, "on", 1)
        got_rows(g, "off", 1)
        if g in DIRECT_LAST:
            near = pl.ds(2 + 2 * core, 2)
            for place_, source in ((0, "zm"), (1, "zp")):

                @when(("off", source))
                def _(place_=place_):
                    corner_copy(g, place_, here=True).wait_recv()
                    given = got_c[DIRECT_LAST.index(g), place_].astype(F32)
                    acc[g, :, 2 : 2 + depth, near] += given

        for place_, source in ((0, "zm"), (1, "zp")):

            @pl.when(has[source])
            def _(place_=place_):
                for slot in range(2):
                    sections_copy(g, place_, slot).wait_recv()

        for kind, out in ((0, gk_ref), (1, gv_ref)):
            for slot in range(2):
                near = slice(2 + 2 * slot, 4 + 2 * slot)
                total = acc[g, kind, 2 : 2 + depth, near] + got_y[g, slot, kind, 4 : 4 + depth].astype(F32)
                total = total + got_z[g, 0, slot, kind].astype(F32) + got_z[g, 1, slot, kind].astype(F32)
                out[:, 2 * slot : 2 * slot + 2, :, parts[g]] = total.astype(BF16)

    def rows_sent(g):
        for side in ("on", "off"):

            direct = side == "off" and g in DIRECT_LAST
            if direct:
                for place_, to in ((0, "zp"), (1, "zm")):

                    @when((side, to))
                    def _(place_=place_):
                        corner_copy(g, place_).wait_send()

            @when((side,))
            def _(side=side, direct=direct):
                if not direct:
                    rows_copy(g, side, 0).wait_send()
                rows_copy(g, side, 1).wait_send()

    def sections_sent(g):
        for place_, to in ((0, "zp"), (1, "zm")):

            @pl.when(has[to])
            def _(place_=place_):
                for slot in range(2):
                    sections_copy(g, place_, slot).wait_send()

    def filter_terms():
        values = ext.at[:, 1]
        near_v[:, 1 : 1 + depth, 1 : 1 + rows] = values[:, 2 : 2 + depth, 2 : 2 + rows]
        near_v[:, 0, 1 : 1 + rows] = values[:, 1, 2 : 2 + rows]
        near_v[:, 1 + depth, 1 : 1 + rows] = values[:, 2 + depth, 2 : 2 + rows]
        near_v[:, 1 : 1 + depth, 0] = values[:, 2 : 2 + depth, 1]
        near_v[:, 1 : 1 + depth, 1 + rows] = values[:, 2 : 2 + depth, 2 + rows]

        def one(i, carry):
            oz, oy = lax.div(i, 3), lax.rem(i, 3)
            for g in range(groups):
                near = near_v[g, pl.ds(oz, depth), pl.ds(oy, rows)].astype(F32)
                for ox in range(3):
                    product = (near * shifted[g, ox]).reshape(octets)
                    eights[3 * i + ox, :, parts[g]] = jnp.sum(product, axis=0)
            return carry

        lax.fori_loop(0, 9, one, 0)

    def half_copy(stage):
        slot = (1 - core, 2) if stage == 0 else (core, 3)
        return pltpu.make_async_remote_copy(
            src_ref=halves.at[slot[0]],
            dst_ref=halves.at[slot[1]],
            send_sem=half_send.at[stage],
            recv_sem=half_recv.at[stage],
            device_id=partner,
            device_id_type=MESH,
        )

    def sum_begin():
        total = jnp.sum(eights[...], axis=1)
        for g in range(groups):
            halves[g] = total[:, parts[g]]
        half_copy(0).start()

    def sum_copy(r, moves):
        digits = sum_rounds[r]
        me = member_of(digits)
        return pltpu.make_async_remote_copy(
            src_ref=terms.at[r, me],
            dst_ref=terms.at[r, me],
            send_sem=sum_send.at[r],
            recv_sem=sum_recv.at[r],
            device_id=peer(digits, moves),
            device_id_type=MESH,
        )

    def sum_all(r):
        n = size_of(sum_rounds[r])
        return pltpu.make_async_remote_copy(
            src_ref=terms.at[r, pl.ds(0, n - 1)],
            dst_ref=terms.at[r, pl.ds(0, n - 1)],
            send_sem=sum_send.at[r],
            recv_sem=sum_recv.at[r],
            device_id=partner,
            device_id_type=MESH,
        )

    def sum_start(r, total):
        terms[r, member_of(sum_rounds[r])] = total.astype(BF16)
        for moves in moves_of(sum_rounds[r]):
            sum_copy(r, moves).start()

    def sum_first():
        half_copy(0).wait_recv()
        sum_start(0, halves[core] + halves[2])

    def sum_got(r):
        sum_all(r).wait_recv()
        total = terms[r, 0].astype(F32)
        for m in range(1, size_of(sum_rounds[r])):
            total = total + terms[r, m].astype(F32)
        return total

    def sum_second():
        sum_start(1, sum_got(0))

    def sum_third():
        total = sum_got(1) * ((tokens * sections * rows_n) ** -0.5)
        half_copy(0).wait_send()
        halves[core] = total
        half_copy(1).start()

    def sum_last():
        half_copy(1).wait_recv()
        mine, other = halves[core, 0:27], halves[3, 0:27]
        cg_ref[:, parts[0]] = jnp.where(core == 0, mine, other)
        cg_ref[:, parts[1]] = jnp.where(core == 0, other, mine)

    def relay(g):
        for source in ("zm", "zp"):
            halo_got(("v" + str(g), source), ("k" + str(g), source))
            halo_start(*(("c", g, side, source) for side in ("off", "on") if side == "on" or g not in DIRECT_FIRST))

    def arrived(g, side):
        halo_got(("ky" + str(g), side), ("c", g, side, "zm"), ("c", g, side, "zp"))

    lax.fori_loop(0, 9, filter_values, 0)
    halo_got(("near", "zm"), ("near", "zp"), ("vy", "on"), ("vy", "off"))
    for corner in range(4):

        @pl.when(both(CORNERS[corner]))
        def _(corner=corner):
            near_copy(corner).wait_recv()

    filter_terms()
    sum_begin()
    relay(0)
    sum_first()
    relay(1)
    arrived(0, "on")
    make_mask(pl.ds(2 * (1 - core), 6))
    own_queries = attend(0, 1 - core)
    send_rows(0, "on")
    own_queries()
    arrived(0, "off")
    make_mask(pl.ds((2 + rows) * core, 2))
    own_queries = attend(0, core)
    send_rows(0, "off")
    own_queries()
    arrived(1, "on")
    own_queries = attend(1, 1 - core)
    send_rows(1, "on")
    own_queries()
    send_sections(0, "on")
    arrived(1, "off")
    own_queries = attend(1, core)
    send_sections(1, "off")
    send_rows(1, "off")
    send_sections(1, "on")
    sum_second()
    own_queries()
    send_sections(0, "off")
    sum_third()
    halo_sent()
    for corner in range(4):

        @pl.when(both(opposite(corner)))
        def _(corner=corner):
            near_copy(corner).wait_send()

    sum_all(0).wait_send()
    for g in range(groups):
        rows_sent(g)
    sections_sent(0)
    sum_all(1).wait_send()
    finish(0)
    sum_last()
    half_copy(1).wait_send()
    sections_sent(1)
    finish(1)


def write_out(*refs):
    n = len(refs) // 2
    sems = refs[-1]
    copies = [pltpu.make_async_copy(refs[i], refs[n + i], sems.at[i]) for i in range(n)]
    for copy in copies:
        copy.start()
    for copy in copies:
        copy.wait()


def shards(sections, rows_n, queries, keys, values, cotangent, conv_weight, block_keep):
    depth, rows, cols, channels = queries.shape
    groups = channels // LANES
    heads_rows = depth * GROUP_HEADS * cols
    most = max(sections * rows_n // 32, 16)
    big = jax.ShapeDtypeStruct(queries.shape, BF16)
    small = jax.ShapeDtypeStruct(conv_weight.shape, F32)
    vmem = pl.BlockSpec(memory_space=pltpu.VMEM)
    hbm = pl.BlockSpec(memory_space=pltpu.HBM)
    dma = pltpu.SemaphoreType.DMA
    arguments = (queries, keys, values, cotangent, conv_weight, block_keep)
    results = pl.pallas_call(
        partial(kernel, sections, rows_n, depth, rows, cols),
        out_shape=(big, big, big, small),
        in_specs=[hbm] * 6,
        out_specs=(vmem,) * 4,
        scratch_shapes=[
            pltpu.VMEM(queries.shape, BF16),
            pltpu.VMEM(queries.shape, BF16),
            pltpu.VMEM(conv_weight.shape, BF16),
            pltpu.SMEM(block_keep.shape, jnp.int32),
            pltpu.VMEM((groups, 2, depth + 4, rows + 4, cols, LANES), BF16),
            pltpu.VMEM((groups, depth + 2, rows + 2, cols, LANES), BF16),
            pltpu.VMEM((groups, 2, depth + 4, rows + 4, cols, LANES), F32),
            pltpu.VMEM((groups, rows // 2, 2 * heads_rows, LANES), BF16),
            pltpu.VMEM((groups, rows // 2, 2 * heads_rows, LANES), BF16),
            pltpu.VMEM((groups, 3, depth, rows, cols, LANES), F32),
            pltpu.VMEM((27, 8, channels), F32),
            pltpu.VMEM((32, 8, channels), F32),
            pltpu.VMEM((depth + 4, rows + 4, cols, LANES), F32),
            pltpu.VMEM((groups, 2, 2, depth + 4, 2, cols, LANES), BF16),
            pltpu.VMEM((groups, 2, 2, depth + 4, 2, cols, LANES), BF16),
            pltpu.VMEM((groups, 2, 2, 2, 2, 2, cols, LANES), BF16),
            pltpu.VMEM((groups, 2, 2, 2, 2, 2, cols, LANES), BF16),
            pltpu.VMEM((groups, 2, 2, depth, 2, cols, LANES), BF16),
            pltpu.VMEM((4, 32, LANES), F32),
            pltpu.VMEM((2, most, 32, LANES), BF16),
            dma((8,)),
            dma((HALO_COPIES,)),
            dma((HALO_COPIES,)),
            dma((4,)),
            dma((4,)),
            dma((groups, 2, 2)),
            dma((groups, 2, 2)),
            dma((groups, 2)),
            dma((groups, 2)),
            dma((groups, 2, 2)),
            dma((groups, 2, 2)),
            dma((2,)),
            dma((2,)),
            dma((2,)),
            dma((2,)),
        ],
        compiler_params=pltpu.CompilerParams(
            collective_id=0, has_side_effects=True, vmem_limit_bytes=16 * 1024 * 1024
        ),
    )(*(pltpu.with_memory_space_constraint(x, pltpu.HBM) for x in arguments))
    return pl.pallas_call(
        write_out,
        out_shape=(big, big, big, small),
        in_specs=[vmem] * 4,
        out_specs=(hbm,) * 4,
        scratch_shapes=[dma((4,))],
        compiler_params=pltpu.CompilerParams(vmem_limit_bytes=1024 * 1024),
    )(*results)


def solution(mesh):
    in_specs = (
        P("gz", "gy", None, None),
        P("gz", "gy", None, None),
        P("gz", "gy", None, None),
        P("gz", "gy", None, None),
        P(),
        P("gz", "gy", None),
    )
    out_specs = (
        P("gz", "gy", None, None),
        P("gz", "gy", None, None),
        P("gz", "gy", None, None),
        P(),
    )
    return jax.shard_map(
        partial(shards, mesh.shape["gz"], mesh.shape["gy"]),
        mesh=mesh,
        in_specs=in_specs,
        out_specs=out_specs,
        check_vma=False,
    )
```
